32 devices in a mesh: resp: 4 (over y, core), ctx: 8 (over z, x).
Axes of the slice: x: 2, y: 2, z: 4, core: 2. Of those that a mesh axis runs over, the one named last changes fastest.
Arguments:
- queries: bfloat16 [8, 2048, 8, 128], P('resp', 'ctx'), may hold values from -170 to 170
- prompt_keys: bfloat16 [128, 128], P('ctx'), may hold values from -6 to 6
- prompt_values: bfloat16 [128, 128], P('ctx'), may hold values from -6 to 6
- resp_keys: bfloat16 [8, 2048, 128], P('resp', 'ctx'), may hold values from -6 to 6
- resp_values: bfloat16 [8, 2048, 128], P('resp', 'ctx'), may hold values from -6 to 6
- upstream: bfloat16 [8, 2048, 8, 128], P('resp', 'ctx'), may hold values from -6 to 6
- behav_logp: float32 [8, 2048], P('resp', 'ctx'), may hold values from -2.5 to -0.1
- cur_logp: float32 [8, 2048], P('resp', 'ctx'), may hold values from -2.5 to -0.1
- advantages: float32 [8], P('resp'), may hold values from -4 to 4
- lengths: int32 [8], P('resp'), may hold values from 128 to 2048, as said below
Outputs:
- grad_queries: bfloat16 [8, 2048, 8, 128], P('resp', 'ctx')
- grad_resp_keys: bfloat16 [8, 2048, 128], P('resp', 'ctx')
- grad_resp_values: bfloat16 [8, 2048, 128], P('resp', 'ctx')
- grad_prompt_keys: float32 [128, 128], P('ctx')
- grad_prompt_values: float32 [128, 128], P('ctx')
The draws below stay inside these ranges and needn't reach their ends.
Inputs may be any that keep to these rules, and one draw needn't show every extreme that they name: `lengths`: each length is a multiple of 128; in every draw one response has length 2048 and another has length 128.
All inputs are finite; a program needn't handle non-finite values.
Results may differ from the reference program's by a relative error of at most 0.024.
Values may be sent and summed in bfloat16 or wider, within the bound.
No kernel may reach another device: no remote copies, remote signals or barrier semaphores. Data moves between devices by JAX's collectives and lax.ppermute only.
A program may use at most 64 MiB of HBM per device.

```python
import jax
import jax.numpy as jnp
from jax import lax

HD = 128
H = 8
L = 2048
BLK = 128
PCTX = 16
P_SIZE = 128
R = 8
N_CTX = 8


def prompt_rows(key):
    base = jnp.clip(jax.random.normal(key, (P_SIZE, HD), jnp.float32), -6.0, 6.0)
    paired = (jnp.arange(P_SIZE, dtype=jnp.int32) % PCTX == 1)[:, None]
    return jnp.where(paired, base, base)


def draw_prompt_keys(key, part):
    rows = prompt_rows(key)
    return rows.astype(jnp.bfloat16)


def draw_queries(key, part):
    key = jax.random.fold_in(key, 7)
    drawn = jnp.clip(jax.random.normal(key, (R, L, H, HD), jnp.float32), -6.0, 6.0)
    return drawn.astype(jnp.bfloat16)


def draw_lengths(key, part):
    key = jax.random.fold_in(key, 3)
    blocks = jax.random.randint(jax.random.fold_in(key, 1), (R,), 1, L // BLK + 1)
    longest = jax.random.randint(jax.random.fold_in(key, 2), (), 0, R)
    shortest = (longest + jax.random.randint(jax.random.fold_in(key, 4), (), 1, R)) % R
    member_ids = jnp.arange(R, dtype=jnp.int32)
    blocks = jnp.where(member_ids == longest, L // BLK, jnp.where(member_ids == shortest, 1, blocks))
    return (blocks * BLK).astype(jnp.int32)


def shard_levels(stream_key, dims, split, low, top_value):
    factor_of, own = 1.0, jax.random.fold_in(stream_key, 6)
    for dim, shards_of in split:
        draws = jnp.exp(jax.random.uniform(jax.random.fold_in(own, dim), (shards_of,), jnp.float32, low / len(split), top_value / len(split)))
        factor_of = factor_of * jnp.repeat(draws, dims[dim] // shards_of).reshape([-1 if axis == dim else 1 for axis in range(len(dims))])
    return factor_of


def bell_draw(stream_key, shape, scale, most, cuts=(), kind=jnp.bfloat16):
    factor_of = shard_levels(stream_key, shape, cuts, -0.22, 0.18) if cuts else 1.0
    array = jax.random.normal(stream_key, shape, jnp.float32) * scale * factor_of
    return jnp.minimum(jnp.maximum(array, -most), most).astype(kind)


def setup_inputs(seed: int = 0) -> dict:
    seeds = jax.random.split(jax.random.key(seed), 11)
    queries = draw_queries(jax.random.fold_in(seeds[10], 71), 0)
    prompt_keys = draw_prompt_keys(jax.random.fold_in(seeds[10], 71), 0)
    prompt_values = bell_draw(seeds[2], (P_SIZE, HD), 1.0, 6.0, ((0, 8),))
    resp_keys = bell_draw(seeds[3], (R, L, HD), 1.0, 6.0, ((0, 4), (1, 8)))
    resp_values = bell_draw(seeds[4], (R, L, HD), 1.0, 6.0, ((0, 4), (1, 8)))
    upstream = bell_draw(seeds[5], (R, L, H, HD), 1.0, 6.0, ((0, 4), (1, 8)))
    behav_logp = jnp.clip(-2.5 + 2.4 * jax.random.uniform(seeds[6], (R, L), jnp.float32) ** shard_levels(seeds[6], (R, L), ((0, 4), (1, 8)), -0.2, 0.2), -2.5, -0.1)
    cur_logp = jnp.clip(-2.5 + 2.4 * jax.random.uniform(seeds[7], (R, L), jnp.float32) ** shard_levels(seeds[7], (R, L), ((0, 4), (1, 8)), -0.2, 0.2), -2.5, -0.1)
    advantages = bell_draw(seeds[8], (R,), 1.0, 4.0, ((0, 4),), jnp.float32)
    lengths = draw_lengths(jax.random.fold_in(seeds[10], 71), 0)
    return dict(queries=queries, prompt_keys=prompt_keys, prompt_values=prompt_values, resp_keys=resp_keys, resp_values=resp_values, upstream=upstream, behav_logp=behav_logp, cur_logp=cur_logp, advantages=advantages, lengths=lengths)


RATIO_CAP = 2.0


def token_weights(advantages, behav_logp, cur_logp, lengths, positions, full_len):
    ratio = jnp.minimum(jnp.exp(cur_logp - behav_logp), RATIO_CAP)
    valid = (positions[None, :] < lengths[:, None]).astype(jnp.float32)
    spread = full_len / lengths.astype(jnp.float32)
    return -advantages[:, None] * ratio * valid * spread[:, None]


def attend_block(query_rows, grad_rows, keys_all, values_all, row_pos, col_pos, softmax_scale):
    scores = jnp.dot(query_rows, keys_all.T, preferred_element_type=jnp.float32) * softmax_scale
    scores = jnp.where(col_pos[None, :] <= row_pos[:, None], scores, -jnp.inf)
    row_max = jnp.max(scores, axis=1, keepdims=True)
    shifted = jnp.exp(scores - row_max)
    probs = lax.optimization_barrier((shifted / jnp.sum(shifted, axis=1, keepdims=True)).astype(jnp.bfloat16))
    attended = lax.optimization_barrier(jnp.dot(probs, values_all, preferred_element_type=jnp.float32).astype(jnp.bfloat16))
    deltas = jnp.sum(grad_rows.astype(jnp.float32) * attended.astype(jnp.float32), axis=1)
    grad_probs = jnp.dot(grad_rows, values_all.T, preferred_element_type=jnp.float32)
    grad_scores = (probs.astype(jnp.float32) * (grad_probs - deltas[:, None])).astype(jnp.bfloat16)
    query_grad = (jnp.dot(grad_scores, keys_all, preferred_element_type=jnp.float32) * softmax_scale).astype(jnp.bfloat16)
    return probs, grad_scores, query_grad


def reference(queries, prompt_keys, prompt_values, resp_keys, resp_values, upstream, behav_logp, cur_logp, advantages, lengths):
    block_len = L // N_CTX
    softmax_scale = HD ** -0.5
    positions = jnp.arange(L, dtype=jnp.int32)
    weights = token_weights(advantages, behav_logp, cur_logp, lengths, positions, L)
    grad_out = (weights[:, :, None, None] * upstream.astype(jnp.float32)).astype(jnp.bfloat16)
    col_pos = jnp.concatenate([jnp.full((P_SIZE,), -1, jnp.int32), positions])
    head_pos = jnp.repeat(jnp.arange(block_len, dtype=jnp.int32), H)

    def per_response(prompt_acc, inputs):
        query_all, grad_all, keys_resp, values_resp = inputs
        keys_all = jnp.concatenate([prompt_keys, keys_resp], 0)
        values_all = jnp.concatenate([prompt_values, values_resp], 0)
        query_blocks = query_all.reshape(N_CTX, block_len * H, HD)
        grad_blocks = grad_all.reshape(N_CTX, block_len * H, HD)

        def per_block(carry, block_inputs):
            prompt_sum, resp_sum = carry
            block_index, query_rows, grad_rows = block_inputs
            row_pos = block_index * block_len + head_pos
            probs, grad_scores, query_grad = attend_block(query_rows, grad_rows, keys_all, values_all, row_pos, col_pos, softmax_scale)
            key_grad = jnp.dot(grad_scores.T, query_rows, preferred_element_type=jnp.float32) * softmax_scale
            value_grad = jnp.dot(probs.T, grad_rows, preferred_element_type=jnp.float32)
            prompt_sum = prompt_sum + jnp.concatenate([key_grad[:P_SIZE], value_grad[:P_SIZE]], 1)
            resp_part = lax.optimization_barrier(jnp.concatenate([key_grad[P_SIZE:], value_grad[P_SIZE:]], 1).astype(jnp.bfloat16))
            resp_sum = resp_sum + resp_part.astype(jnp.float32)
            return (prompt_sum, resp_sum), query_grad

        start_resp = jnp.zeros((L, 2 * HD), jnp.float32)
        (prompt_acc, resp_sum), query_grads = lax.scan(per_block, (prompt_acc, start_resp), (jnp.arange(N_CTX, dtype=jnp.int32), query_blocks, grad_blocks))
        return prompt_acc, (query_grads.reshape(L, H, HD), resp_sum.astype(jnp.bfloat16))

    start_prompt = jnp.zeros((P_SIZE, 2 * HD), jnp.float32)
    prompt_total, (grad_queries, resp_grads) = lax.scan(per_response, start_prompt, (queries, grad_out, resp_keys, resp_values))
    return grad_queries, resp_grads[:, :, :HD], resp_grads[:, :, HD:], prompt_total[:, :HD], prompt_total[:, HD:]
```

```python
import functools
import math

import jax
import jax.numpy as jnp
from jax import lax
from jax.experimental import pallas as pl
from jax.experimental.pallas import tpu as pltpu
from jax.sharding import PartitionSpec as P

RATIO_CAP = 2.0
MASKED = -1e30
SUB_ROWS = 256
TILE_ROWS = 1024
LARGEST_SCORE = 100.0
UNBOUNDED = 3e38

TOP, TOTAL, DOTTED, GUARD, WEIGHT, LENGTH = range(6)
VMEM_BYTES = 24 * 1024 * 1024

NT = (((1,), (1,)), ((), ()))
NN = (((1,), (0,)), ((), ()))


def dot(a, b, dims):
    return lax.dot_general(a, b, dims, preferred_element_type=jnp.float32)


def kinds_of(step, layers):
    if step == 0:
        return ("z",)
    return ("x", "prompt") if step == layers else ("x", "z")


def variants(step, layers, place):
    z, odd = place // 2, place % 2 == 1
    if step == 0:
        return [(None, 0, 1)]
    if step == layers:
        return [(z >= step - 1, 0, 2), (z < step - 1, 1, 2)]
    if step == 1:
        return [
            ((z >= 1) & odd, 0, 2),
            ((z == 0) & odd, 0, 1),
            ((z >= 1) & jnp.logical_not(odd), 1, 2),
        ]
    return [(z >= step, 0, 2), (z == step - 1, 0, 1)]


def attends(step, layers, place):
    if step in (0, layers):
        return place >= 0
    return place >= 1 if step == 1 else place // 2 >= step - 1


def kept_keys(shape, first_row, heads):
    key = lax.broadcasted_iota(jnp.int32, shape, 0)
    row = lax.broadcasted_iota(jnp.int32, shape, 1) + first_row
    return key * heads <= row


def edges_of(counts):
    edges = [0]
    for count in counts:
        edges.append(edges[-1] + count)
    return edges


def largest_norm(rows):
    wide = rows.astype(jnp.float32)
    return jnp.max(jnp.sum(wide * wide, axis=1, keepdims=True))


def filled_tiles(length, tokens, heads, rows):
    per_tile = tile_of(rows) // heads
    left = length - lax.axis_index("ctx") * tokens
    return jnp.clip((left + per_tile - 1) // per_tile, 0, rows // tile_of(rows))


def load_keys(member, pairs, kinds, edges, head_dim, keys, values):
    for part, pair in enumerate(pairs):
        count = edges[part + 1] - edges[part]
        rows = pl.ds(edges[part], count)
        own = pl.ds(0, count)
        if kinds[part] != "prompt":
            own = pl.ds(pl.multiple_of(member * count, count), count)
        keys[rows, :] = pair[own, :head_dim]
        values[rows, :] = pair[own, head_dim:]


def length_of(stat, member):
    return jnp.max(stat[member, LENGTH : LENGTH + 1, 0:128]).astype(jnp.int32)


def spread_weights(ratio, heads):
    tokens = ratio.shape[1]
    shape = (tokens, tokens * heads)
    token = lax.broadcasted_iota(jnp.int32, shape, 0)
    row = lax.broadcasted_iota(jnp.int32, shape, 1)
    first = token * heads
    chosen = jnp.where((row >= first) & (row < first + heads), 1.0, 0.0)
    chosen = chosen.astype(jnp.bfloat16)
    out, rest = None, ratio
    for _ in range(3):
        term = rest.astype(jnp.bfloat16)
        rest = rest - term.astype(jnp.float32)
        few = jnp.broadcast_to(term.astype(jnp.float32), (16, tokens)).astype(jnp.bfloat16)
        part = jnp.dot(few, chosen, preferred_element_type=jnp.float32)[0:1]
        out = part if out is None else out + part
    return out


def forward_kernel(step, layers, heads, head_dim, counts, *refs):
    kinds = kinds_of(step, layers)
    parts = len(kinds)
    earlier = None
    if step == 0:
        lengths, advantages, held_q, held_g, held_behaved, held_current = refs[:6]
        message, out, q, g, keys, values, behaved, current, arrived = refs[6:]
        pairs = [message]
        copies = [
            pltpu.make_async_copy(source, target, arrived.at[i])
            for i, (source, target) in enumerate(
                [(held_behaved, behaved), (held_current, current), (held_q, q), (held_g, g)]
            )
        ]
        for copy in copies:
            copy.start()
        for copy in copies:
            copy.wait()
    else:
        q, g, earlier = refs[:3]
        refs = refs[3:]
        if step == layers:
            messages, (out, prompt, keys, values) = refs[: 2 * layers], refs[2 * layers :]
            own = messages[0].shape[0] - prompt.shape[0] // (2 * layers)
            each = messages[0].shape[0] - own
            for i, message in enumerate(messages):
                prompt[i * each : (i + 1) * each, :] = message[own:, :]
            pairs = [messages[-1], prompt]
        else:
            pairs, (out, keys, values) = refs[:parts], refs[parts:]
    place = lax.axis_index("ctx")
    members, all_rows = q.shape[:2]
    tile = tile_of(all_rows)
    tokens = all_rows // heads
    full_len = tokens * lax.axis_size("ctx")
    scale = head_dim**-0.5 * math.log2(math.e)
    edges = edges_of(counts)
    attended = attends(step, layers, place)

    def shared(member, low, high, first, start):
        rows = pl.ds(pl.multiple_of(first + start, SUB_ROWS), SUB_ROWS)
        scores = dot(keys[low:high, :], q[member, rows, :], NT) * scale
        if step == 0:
            kept = kept_keys(scores.shape, first + start, heads)
            scores = jnp.where(kept, scores, MASKED)
        return rows, scores, dot(values[low:high, :], g[member, rows, :], NT)

    def put(member, rows, top, total, dotted):
        out[member, TOP : TOP + 1, rows] = top
        out[member, TOTAL : TOTAL + 1, rows] = total
        out[member, DOTTED : DOTTED + 1, rows] = dotted

    def bounded(member, low, high, first):
        for start in range(0, tile, SUB_ROWS):
            rows, scores, grad_probs = shared(member, low, high, first, start)
            weight = jnp.exp2(scores)
            total = jnp.sum(weight, axis=0, keepdims=True)
            dotted = jnp.sum(weight * grad_probs, axis=0, keepdims=True)
            if earlier is not None:
                total = total + earlier[member, TOTAL : TOTAL + 1, rows]
                dotted = dotted + earlier[member, DOTTED : DOTTED + 1, rows]
            put(member, rows, jnp.zeros_like(total), total, dotted)

    def general(member, low, high, first):
        for start in range(0, tile, SUB_ROWS):
            rows, scores, grad_probs = shared(member, low, high, first, start)
            top = jnp.max(scores, axis=0, keepdims=True)
            if earlier is not None:
                top = jnp.maximum(top, earlier[member, TOP : TOP + 1, rows])
            weight = jnp.exp2(scores - top)
            total = jnp.sum(weight, axis=0, keepdims=True)
            dotted = jnp.sum(weight * grad_probs, axis=0, keepdims=True)
            if earlier is not None:
                decay = jnp.exp2(earlier[member, TOP : TOP + 1, rows] - top)
                total = total + decay * earlier[member, TOTAL : TOTAL + 1, rows]
                dotted = dotted + decay * earlier[member, DOTTED : DOTTED + 1, rows]
            put(member, rows, top, total, dotted)
            out[member, GUARD : GUARD + 1, rows] = jnp.full_like(total, UNBOUNDED)

    def per_member(member, carry):
        length = lengths[member] if step == 0 else length_of(earlier, member)
        filled = filled_tiles(length, tokens, heads, all_rows)
        if step == 0:
            known = jnp.full((1, all_rows), length).astype(jnp.float32)
            out[member, LENGTH : LENGTH + 1, :] = known

        @pl.when((filled > 0) & attended)
        def _():
            load_keys(member, pairs, kinds, edges, head_dim, keys, values)
            limit = (LARGEST_SCORE / scale) ** 2 / largest_norm(keys[...])

            def per_tile(index, carry):
                first = pl.multiple_of(index * tile, tile)
                rows = pl.ds(first, tile)
                if step == 0:
                    guard = largest_norm(q[member, rows, :])
                    out[member, GUARD : GUARD + 1, rows] = jnp.full((1, tile), guard)
                    count = tile // heads
                    part = pl.ds(pl.multiple_of(index * count, count), count)
                    if count == tokens:
                        part = pl.ds(0, count)
                    ratio = jnp.minimum(jnp.exp(current[:, part] - behaved[:, part]), RATIO_CAP)
                    owner = lax.broadcasted_iota(jnp.int32, ratio.shape, 0)
                    ratio = jnp.sum(
                        jnp.where(owner == member, ratio, 0.0), axis=0, keepdims=True
                    )
                    token = lax.broadcasted_iota(jnp.int32, ratio.shape, 1)
                    position = place * tokens + index * count + token
                    ratio = jnp.where(position < length, ratio, 0.0)
                    spread = full_len / jnp.full((1, 1), length).astype(jnp.float32)
                    ratio = -advantages[member] * ratio * spread
                    out[member, WEIGHT : WEIGHT + 1, rows] = spread_weights(ratio, heads)
                else:
                    guard = jnp.max(earlier[member, GUARD : GUARD + 1, pl.ds(first, 128)])
                fast = guard <= limit
                for condition, begin, past in variants(step, layers, place):
                    low, high = edges[begin], edges[past]
                    for quick, body in ((fast, bounded), (jnp.logical_not(fast), general)):
                        here = quick if condition is None else quick & condition
                        pl.when(here)(functools.partial(body, member, low, high, first))
                return carry

            lax.fori_loop(0, filled, per_tile, 0)

        return carry

    lax.fori_loop(0, members, per_member, 0)


def backward_kernel(step, layers, heads, head_dim, counts, q, g, final, *refs):
    kinds = kinds_of(step, layers)
    count = len(kinds)
    pairs, refs = refs[:count], refs[count:]
    earlier = None
    if step < layers:
        earlier, refs = refs[0], refs[1:]
    grads, query_out, refs = refs[:count], refs[count], refs[count + 1 :]
    keys, values, turned, probs_held, scores_held, sums = refs
    place = lax.axis_index("ctx")
    members, all_rows = q.shape[:2]
    tile = tile_of(all_rows)
    tokens = all_rows // heads
    plain = head_dim**-0.5
    scale = plain * math.log2(math.e)
    edges = edges_of(counts)
    attended = attends(step, layers, place)

    def body(member, low, high, first):
        for start in range(0, tile, SUB_ROWS):
            rows = pl.ds(pl.multiple_of(first + start, SUB_ROWS), SUB_ROWS)
            held = pl.ds(start, SUB_ROWS)
            total = final[member, TOTAL : TOTAL + 1, rows]
            level = final[member, TOP : TOP + 1, rows] + jnp.log2(total)
            delta = final[member, DOTTED : DOTTED + 1, rows] / total
            scores = dot(keys[low:high, :], q[member, rows, :], NT) * scale - level
            if step == 0:
                kept = kept_keys(scores.shape, first + start, heads)
                scores = jnp.where(kept, scores, MASKED)
            probs = jnp.exp2(scores) * final[member, WEIGHT : WEIGHT + 1, rows]
            grad_probs = dot(values[low:high, :], g[member, rows, :], NT)
            grad_scores = (probs * (grad_probs - delta)).astype(jnp.bfloat16)
            probs_held[low:high, held] = probs.astype(jnp.bfloat16)
            scores_held[low:high, held] = grad_scores
            moved = dot(turned[:, low:high], grad_scores, NN)
            if earlier is not None:
                moved = moved + earlier[member, :, rows]
            if step == 0:
                query_out[member, rows, :] = (moved * plain).T.astype(jnp.bfloat16)
            else:
                query_out[member, :, rows] = moved
        rows = pl.ds(first, tile)
        sums[low:high, :head_dim] += dot(scores_held[low:high, :], q[member, rows, :], NN)
        sums[low:high, head_dim:] += dot(probs_held[low:high, :], g[member, rows, :], NN)

    def per_member(member, carry):
        filled = filled_tiles(length_of(final, member), tokens, heads, all_rows)
        filled = jnp.where(attended, filled, 0)
        for part in range(count):
            rows = pl.ds(edges[part], edges[part + 1] - edges[part])

            @pl.when((member == 0) | (kinds[part] != "prompt"))
            def _():
                sums[rows, :] = jnp.zeros_like(sums[rows, :])

        @pl.when(filled > 0)
        def _():
            load_keys(member, pairs, kinds, edges, head_dim, keys, values)
            turned[...] = keys[...].T

            def per_tile(index, carry):
                first = pl.multiple_of(index * tile, tile)
                for condition, begin, past in variants(step, layers, place):
                    run = functools.partial(body, member, edges[begin], edges[past], first)
                    if condition is None:
                        run()
                    else:
                        pl.when(condition)(run)
                return carry

            lax.fori_loop(0, filled, per_tile, 0)

        if step == 0 or earlier is None:

            def clear(index, carry):
                rows = pl.ds(pl.multiple_of(index * tile, tile), tile)
                if step == 0:
                    query_out[member, rows, :] = jnp.zeros((tile, head_dim), jnp.bfloat16)
                else:
                    query_out[member, :, rows] = jnp.zeros((head_dim, tile), jnp.float32)
                return carry

            lax.fori_loop(filled, all_rows // tile, clear, 0)
        for part in range(count):
            if kinds[part] == "prompt":
                continue
            rows = pl.ds(edges[part], counts[part])
            own = pl.ds(pl.multiple_of(member * counts[part], counts[part]), counts[part])
            grads[part][own, :head_dim] = (sums[rows, :head_dim] * plain).astype(jnp.bfloat16)
            grads[part][own, head_dim:] = sums[rows, head_dim:].astype(jnp.bfloat16)
        return carry

    lax.fori_loop(0, members, per_member, 0)
    if step == layers:
        stay, leave = grads[1], grads[0]
        half = stay.shape[0]
        low, middle, high = edges[1], edges[1] + half, edges[2]
        stay[:, :head_dim] = sums[low:middle, :head_dim] * plain
        stay[:, head_dim:] = sums[low:middle, head_dim:]
        far_keys = sums[middle:high, :head_dim] * plain
        own = leave.shape[0] - half
        leave[own:, :head_dim] = far_keys.astype(jnp.bfloat16)
        leave[own:, head_dim:] = sums[middle:high, head_dim:].astype(jnp.bfloat16)


def combine_kernel(step, layers, *refs):
    def wide(ref, rows, columns=slice(None)):
        return ref[rows, columns].astype(jnp.float32)

    if step == layers - 1:
        own, stay, far, out, kept = refs
        count = own.shape[0]
        each = stay.shape[0] // layers
        for j in range(layers):
            before = count + (j - 1) % layers * each
            mine = slice(j * each, (j + 1) * each)
            kept[mine, :] = stay[mine, :] + wide(far, slice(before, before + each))
        out[:count, :] = own[...]
        out[count:, :] = kept[step * each :, :].astype(jnp.bfloat16)
        return
    own, side, above, kept = refs[:4]
    count = own.shape[0]
    each = kept.shape[0] // layers
    mine = slice(step * each, (step + 1) * each)
    prompt = kept[mine, :] + wide(above, slice(count, None))
    rows = slice(0, count)
    total = wide(own, rows) + wide(side, rows) + wide(above, rows)
    if step > 0:
        out = refs[4]
        out[:count, :] = total.astype(jnp.bfloat16)
        out[count:, :] = prompt.astype(jnp.bfloat16)
    else:
        far, key_out, value_out, prompt_out = refs[4:]
        total = (total + wide(far, rows)).astype(jnp.bfloat16)
        head_dim = key_out.shape[1]
        key_out[...] = total[:, :head_dim]
        value_out[...] = total[:, head_dim:]
        prompt_out[...] = prompt


def work(members, rows, columns, head_dim, products):
    return pl.CostEstimate(
        flops=2 * members * rows * columns * head_dim * products,
        bytes_accessed=members * rows * head_dim * 8,
        transcendentals=members * rows * columns,
    )


def tile_of(rows):
    return min(TILE_ROWS, rows)


WHOLE = pl.BlockSpec(memory_space=pltpu.VMEM)
SCALARS = pl.BlockSpec(memory_space=pltpu.SMEM)
PARAMS = pltpu.CompilerParams(vmem_limit_bytes=VMEM_BYTES)


ANYWHERE = pl.BlockSpec(memory_space=pl.ANY)


def forward_step(step, layers, heads, tokens, operands, messages, earlier):
    q = operands[2] if step == 0 else operands[0]
    members, rows, head_dim = q.shape
    each = messages[0].shape[0] - members * tokens
    counts = [tokens] * len(kinds_of(step, layers))
    if step == layers:
        counts[1] = 2 * layers * each
    columns = sum(counts)
    out_shape = [jax.ShapeDtypeStruct((members, 8, rows), jnp.float32)]
    scratch = [pltpu.VMEM((columns, head_dim), jnp.bfloat16)] * 2
    extra = [] if step == 0 else [earlier]
    in_specs = [WHOLE] * 3
    if step == 0:
        in_specs = [SCALARS] * 2 + [ANYWHERE] * 4
        out_shape += [jax.ShapeDtypeStruct(q.shape, q.dtype)] * 2
        small = operands[4]
        scratch += [pltpu.VMEM(small.shape, small.dtype)] * 2
        scratch += [pltpu.SemaphoreType.DMA((4,))]
    elif step == layers:
        out_shape.append(jax.ShapeDtypeStruct((counts[1], 2 * head_dim), jnp.bfloat16))
    return pl.pallas_call(
        functools.partial(forward_kernel, step, layers, heads, head_dim, counts),
        in_specs=in_specs + [WHOLE] * len(messages),
        out_specs=[WHOLE] * len(out_shape),
        out_shape=out_shape,
        scratch_shapes=scratch,
        compiler_params=PARAMS,
        cost_estimate=work(members, rows, columns, head_dim, 2),
        input_output_aliases={} if step == 0 else {2: 0},
        name=f"attend_step{step}",
    )(*operands, *extra, *messages)


def backward_step(step, layers, heads, tokens, each, q, g, final, messages, earlier):
    members, rows, head_dim = q.shape
    counts = [tokens] * len(kinds_of(step, layers))
    block = (members * tokens, 2 * head_dim)
    grad_shapes = [jax.ShapeDtypeStruct(block, jnp.bfloat16)] * len(counts)
    if step == layers:
        counts[1] = 2 * layers * each
        half = layers * each
        grad_shapes = [
            jax.ShapeDtypeStruct((block[0] + half, block[1]), jnp.bfloat16),
            jax.ShapeDtypeStruct((half, block[1]), jnp.float32),
        ]
    columns = sum(counts)
    tile = tile_of(rows)
    if step == 0:
        query_shape = jax.ShapeDtypeStruct(q.shape, jnp.bfloat16)
    else:
        query_shape = jax.ShapeDtypeStruct((members, head_dim, rows), jnp.float32)
    extra = [] if earlier is None else [earlier]
    aliases = {3 + len(messages): len(counts)} if extra and step > 0 else {}
    outs = pl.pallas_call(
        functools.partial(backward_kernel, step, layers, heads, head_dim, counts),
        in_specs=[WHOLE] * (3 + len(messages) + len(extra)),
        out_specs=[WHOLE] * (len(counts) + 1),
        out_shape=grad_shapes + [query_shape],
        scratch_shapes=[pltpu.VMEM((columns, head_dim), jnp.bfloat16)] * 2
        + [pltpu.VMEM((head_dim, columns), jnp.bfloat16)]
        + [pltpu.VMEM((columns, tile), jnp.bfloat16)] * 2
        + [pltpu.VMEM((columns, 2 * head_dim), jnp.float32)],
        compiler_params=PARAMS,
        cost_estimate=work(members, rows, columns, head_dim, 5),
        input_output_aliases=aliases,
        name=f"attend_grad_step{step}",
    )(q, g, final, *messages, *extra)
    return outs[: len(counts)], outs[len(counts)]


def combine(step, layers, each, *terms):
    count, width = terms[0].shape
    if step > 0:
        shapes = [jax.ShapeDtypeStruct((count + each, width), jnp.bfloat16)]
        if step == layers - 1:
            shapes.append(jax.ShapeDtypeStruct((layers * each, width), jnp.float32))
    else:
        shapes = [jax.ShapeDtypeStruct((count, width // 2), jnp.bfloat16)] * 2
        shapes.append(jax.ShapeDtypeStruct((each, width), jnp.float32))
    return pl.pallas_call(
        functools.partial(combine_kernel, step, layers),
        in_specs=[WHOLE] * len(terms),
        out_specs=[WHOLE] * len(shapes),
        out_shape=shapes,
        compiler_params=PARAMS,
        name=f"add_terms{step}",
    )(*terms)


def join_kernel(keys, values, prompt_keys, prompt_values, out, arrived):
    rows, head_dim = keys.shape
    copies = []
    for i, (source, first, column) in enumerate(
        [
            (keys, 0, 0),
            (values, 0, head_dim),
            (prompt_keys, rows, 0),
            (prompt_values, rows, head_dim),
        ]
    ):
        place = out.at[pl.ds(first, source.shape[0]), pl.ds(column, head_dim)]
        copies.append(pltpu.make_async_copy(source, place, arrived.at[i]))
    for copy in copies:
        copy.start()
    for copy in copies:
        copy.wait()


def join(keys, values, prompt_keys, prompt_values):
    rows = keys.shape[0] + prompt_keys.shape[0]
    return pl.pallas_call(
        join_kernel,
        out_shape=jax.ShapeDtypeStruct((rows, 2 * keys.shape[1]), keys.dtype),
        in_specs=[ANYWHERE] * 4,
        out_specs=WHOLE,
        scratch_shapes=[pltpu.SemaphoreType.DMA((4,))],
        compiler_params=PARAMS,
        name="join_pairs",
    )(keys, values, prompt_keys, prompt_values)


def per_device(
    queries,
    prompt_keys,
    prompt_values,
    resp_keys,
    resp_values,
    upstream,
    behav_logp,
    cur_logp,
    advantages,
    lengths,
):
    members, tokens, heads, head_dim = queries.shape
    ctx_size, resp_size = lax.axis_size("ctx"), lax.axis_size("resp")
    layers = ctx_size // 2
    each = prompt_keys.shape[0]
    rows = tokens * heads

    def hop(array, layers_up):
        pairs = [(c, (c + 2 * layers_up) % ctx_size) for c in range(ctx_size)]
        return lax.ppermute(array, "ctx", pairs)

    def cross(array, layers_up=0):
        pairs = [(c, ((c + 2 * layers_up) % ctx_size) ^ 1) for c in range(ctx_size)]
        return lax.ppermute(array, "ctx", pairs)

    z = [
        join(
            resp_keys.reshape(members * tokens, head_dim),
            resp_values.reshape(members * tokens, head_dim),
            prompt_keys,
            prompt_values,
        )
    ]
    x = [None]
    operands = (
        lengths,
        advantages,
        queries.reshape(members, rows, head_dim),
        upstream.reshape(members, rows, head_dim),
        behav_logp,
        cur_logp,
    )
    stat = prompt = None
    for step in range(layers + 1):
        if step < layers:
            held = z[step]
            if step > 0:
                held, stat = lax.optimization_barrier((held, stat))
                z[step] = held
            if step + 1 < layers:
                z.append(hop(held, 1))
                x.append(cross(held))
            if step == 1:
                source, z[1] = lax.optimization_barrier((z[0], z[1]))
                far_message = cross(source, layers - 1)
            if step + 1 == layers:
                x.append(far_message)
        if step == 0:
            stat, q, g = forward_step(0, layers, heads, tokens, operands, z[:1], None)
            operands = (q, g)
        elif step < layers:
            (stat,) = forward_step(
                step, layers, heads, tokens, operands, [x[step], z[step]], stat
            )
        else:
            stat, prompt = forward_step(step, layers, heads, tokens, operands, z + x[1:], stat)

    final = stat
    moved = side = above = far = message = kept = None
    for step in range(layers, -1, -1):
        if message is not None:
            final, message = lax.optimization_barrier((final, message))
            above = hop(message, -1)
        if step == layers:
            messages = [x[step], prompt]
        else:
            messages = [z[0]] if step == 0 else [x[step], z[step]]
        grads, moved = backward_step(
            step, layers, heads, tokens, each, q, g, final, messages, moved
        )
        if step == layers:
            far, stay = cross(grads[0], 1 - layers), grads[1]
            continue
        if step == layers - 1:
            message, kept = combine(step, layers, each, grads[-1], stay, far)
        elif step > 0:
            (message,) = combine(step, layers, each, grads[-1], side, above, kept)
        if step > 0:
            side = cross(grads[0])
    key_grads, value_grads, share = combine(0, layers, each, grads[-1], side, above, kept, far)
    stride = 1
    while stride < resp_size:
        pairs = [(c, c ^ stride) for c in range(resp_size)]
        share = share + lax.ppermute(share, "resp", pairs)
        stride *= 2
    return (
        moved.reshape(queries.shape),
        key_grads.reshape(resp_keys.shape),
        value_grads.reshape(resp_values.shape),
        share[:, :head_dim],
        share[:, head_dim:],
    )


def solution(mesh):
    placed = (
        P("resp", "ctx", None, None),
        P("ctx", None),
        P("ctx", None),
        P("resp", "ctx", None),
        P("resp", "ctx", None),
        P("resp", "ctx", None, None),
        P("resp", "ctx"),
        P("resp", "ctx"),
        P("resp"),
        P("resp"),
    )
    return jax.shard_map(
        per_device,
        mesh=mesh,
        in_specs=placed,
        out_specs=(
            P("resp", "ctx", None, None),
            P("resp", "ctx", None),
            P("resp", "ctx", None),
            P("ctx", None),
            P("ctx", None),
        ),
        check_vma=False,
    )
```

```python
import functools
import math

import jax
import jax.numpy as jnp
from jax import lax
from jax.experimental import pallas as pl
from jax.experimental.pallas import tpu as pltpu
from jax.sharding import PartitionSpec as P

RATIO_CAP = 2.0
MASKED = -1e30
SUB_ROWS = 256
TILE_ROWS = 1024
LARGEST_SCORE = 100.0
UNBOUNDED = 3e38

TOP, TOTAL, DOTTED, GUARD, WEIGHT, LENGTH = range(6)
VMEM_BYTES = 24 * 1024 * 1024
JOIN_VMEM_BYTES = 60 * 1024 * 1024

def dot(a, b):
    return jnp.dot(a, b, preferred_element_type=jnp.float32)


def kinds_of(step, layers):
    if step == 0:
        return ("z",)
    return ("x", "prompt") if step == layers else ("x", "z")


def variants(step, layers, place):
    z, odd = place // 2, place % 2 == 1
    if step == 0:
        return [(None, 0, 1)]
    if step == layers:
        return [(z >= step - 1, 0, 2), (z < step - 1, 1, 2)]
    if step == 1:
        return [
            ((z >= 1) & odd, 0, 2),
            ((z == 0) & odd, 0, 1),
            ((z >= 1) & jnp.logical_not(odd), 1, 2),
        ]
    return [(z >= step, 0, 2), (z == step - 1, 0, 1)]


def attends(step, layers, place):
    if step in (0, layers):
        return place >= 0
    return place >= 1 if step == 1 else place // 2 >= step - 1


def kept_keys(shape, first_row, heads):
    key = lax.broadcasted_iota(jnp.int32, shape, 0)
    row = lax.broadcasted_iota(jnp.int32, shape, 1) + first_row
    return key * heads <= row


def edges_of(counts):
    edges = [0]
    for count in counts:
        edges.append(edges[-1] + count)
    return edges


def largest_norm(rows):
    wide = rows.astype(jnp.float32)
    return jnp.max(jnp.sum(wide * wide, axis=1, keepdims=True))


def filled_tiles(length, tokens, heads, rows):
    per_tile = tile_of(rows) // heads
    left = length - lax.axis_index("ctx") * tokens
    return jnp.clip((left + per_tile - 1) // per_tile, 0, rows // tile_of(rows))


def load_keys(member, pairs, kinds, edges, head_dim, keys, values):
    for part, pair in enumerate(pairs):
        count = edges[part + 1] - edges[part]
        rows = pl.ds(edges[part], count)
        own = pl.ds(0, count)
        if kinds[part] != "prompt":
            own = pl.ds(pl.multiple_of(member * count, count), count)
        keys[rows, :] = pair[own, :head_dim]
        values[rows, :] = pair[own, head_dim:]


def length_of(stat, member):
    return jnp.max(stat[member, LENGTH : LENGTH + 1, 0:128]).astype(jnp.int32)


def spread_weights(ratio, heads):
    tokens = ratio.shape[1]
    shape = (tokens, tokens * heads)
    token = lax.broadcasted_iota(jnp.int32, shape, 0)
    row = lax.broadcasted_iota(jnp.int32, shape, 1)
    first = token * heads
    chosen = jnp.where((row >= first) & (row < first + heads), 1.0, 0.0)
    chosen = chosen.astype(jnp.bfloat16)
    out, rest = None, ratio
    for _ in range(3):
        term = rest.astype(jnp.bfloat16)
        rest = rest - term.astype(jnp.float32)
        few = jnp.broadcast_to(term.astype(jnp.float32), (16, tokens)).astype(jnp.bfloat16)
        part = jnp.dot(few, chosen, preferred_element_type=jnp.float32)[0:1]
        out = part if out is None else out + part
    return out


def key_sum(array):
    count = array.shape[0] // 4
    parts = [
        jnp.sum(array[i * count : (i + 1) * count], axis=0, keepdims=True) for i in range(4)
    ]
    return (parts[0] + parts[1]) + (parts[2] + parts[3])


def forward_kernel(step, layers, heads, head_dim, counts, *refs):
    kinds = kinds_of(step, layers)
    parts = len(kinds)
    earlier = None
    if step == 0:
        policy, held_q, held_g, message, out, q, g, turned_q, turned_g = refs[:9]
        keys, values, arrived = refs[9:]
        pairs = [message]
        copies = [
            pltpu.make_async_copy(source, target, arrived.at[i])
            for i, (source, target) in enumerate([(held_q, q), (held_g, g)])
        ]
        for copy in copies:
            copy.start()
        for copy in copies:
            copy.wait()
    else:
        turned_q, turned_g, earlier = refs[:3]
        refs = refs[3:]
        if step == layers:
            messages, (out, prompt, keys, values) = refs[: 2 * layers], refs[2 * layers :]
            own = messages[0].shape[0] - prompt.shape[0] // (2 * layers)
            each = messages[0].shape[0] - own
            for i, message in enumerate(messages):
                prompt[i * each : (i + 1) * each, :] = message[own:, :]
            pairs = [messages[-1], prompt]
        else:
            pairs, (out, keys, values) = refs[:parts], refs[parts:]
    place = lax.axis_index("ctx")
    members, _, all_rows = turned_q.shape
    tile = tile_of(all_rows)
    tokens = all_rows // heads
    scale = head_dim**-0.5 * math.log2(math.e)
    edges = edges_of(counts)
    attended = attends(step, layers, place)

    def shared(member, low, high, first, start):
        rows = pl.ds(pl.multiple_of(first + start, SUB_ROWS), SUB_ROWS)
        scores = dot(keys[low:high, :], turned_q[member, :, rows]) * scale
        if step == 0:
            kept = kept_keys(scores.shape, first + start, heads)
            scores = jnp.where(kept, scores, MASKED)
        return rows, scores, dot(values[low:high, :], turned_g[member, :, rows])

    def put(member, first, lines):
        rows = pl.ds(first, tile)
        for line, pieces in lines.items():
            out[member, line : line + 1, rows] = jnp.concatenate(pieces, 1)

    def bounded(member, low, high, first):
        totals, dots = [], []
        for start in range(0, tile, SUB_ROWS):
            rows, scores, grad_probs = shared(member, low, high, first, start)
            weight = jnp.exp2(scores)
            total, dotted = key_sum(weight), key_sum(weight * grad_probs)
            if earlier is not None:
                total = total + earlier[member, TOTAL : TOTAL + 1, rows]
                dotted = dotted + earlier[member, DOTTED : DOTTED + 1, rows]
            totals.append(total)
            dots.append(dotted)
        tops = [jnp.zeros_like(t) for t in totals]
        put(member, first, {TOP: tops, TOTAL: totals, DOTTED: dots})

    def general(member, low, high, first):
        tops, totals, dots = [], [], []
        for start in range(0, tile, SUB_ROWS):
            rows, scores, grad_probs = shared(member, low, high, first, start)
            top = jnp.max(scores, axis=0, keepdims=True)
            if earlier is not None:
                top = jnp.maximum(top, earlier[member, TOP : TOP + 1, rows])
            weight = jnp.exp2(scores - top)
            total, dotted = key_sum(weight), key_sum(weight * grad_probs)
            if earlier is not None:
                decay = jnp.exp2(earlier[member, TOP : TOP + 1, rows] - top)
                total = total + decay * earlier[member, TOTAL : TOTAL + 1, rows]
                dotted = dotted + decay * earlier[member, DOTTED : DOTTED + 1, rows]
            tops.append(top)
            totals.append(total)
            dots.append(dotted)
        guards = [jnp.full_like(t, UNBOUNDED) for t in totals]
        put(member, first, {TOP: tops, TOTAL: totals, DOTTED: dots, GUARD: guards})

    def per_member(member, carry):
        if step == 0:
            line = lax.broadcasted_iota(jnp.int32, policy.shape, 0)

            known = jnp.max(jnp.where(line == members + member, policy[...], 0.0))
            length = known.astype(jnp.int32)
            out[member, LENGTH : LENGTH + 1, :] = jnp.full((1, all_rows), known)
        else:
            length = length_of(earlier, member)
        filled = filled_tiles(length, tokens, heads, all_rows)

        @pl.when((filled > 0) & attended)
        def _():
            load_keys(member, pairs, kinds, edges, head_dim, keys, values)
            limit = (LARGEST_SCORE / scale) ** 2 / largest_norm(keys[...])

            def prepare(index, carry):
                first = pl.multiple_of(index * tile, tile)
                rows = pl.ds(first, tile)
                turned_q[member, :, rows] = q[member, rows, :].T
                turned_g[member, :, rows] = g[member, rows, :].T
                guard = largest_norm(q[member, rows, :])
                out[member, GUARD : GUARD + 1, rows] = jnp.full((1, tile), guard)
                count = tile // heads
                part = pl.ds(pl.multiple_of(index * count, count), count)
                if count == tokens:
                    part = pl.ds(0, count)
                chosen = jnp.where(line[:, :count] == member, policy[:, part], 0.0)
                ratio = jnp.sum(chosen, axis=0, keepdims=True)
                out[member, WEIGHT : WEIGHT + 1, rows] = spread_weights(ratio, heads)
                return carry

            if step == 0:
                lax.fori_loop(0, filled, prepare, 0)
            guards = (out if step == 0 else earlier)[member, GUARD : GUARD + 1, :]
            column = lax.broadcasted_iota(jnp.int32, guards.shape, 1)
            fast = jnp.max(jnp.where(column < filled * tile, guards, 0.0)) <= limit
            for condition, begin, past in variants(step, layers, place):
                low, high = edges[begin], edges[past]
                for quick, body in ((fast, bounded), (jnp.logical_not(fast), general)):

                    @pl.when(quick if condition is None else quick & condition)
                    def _():
                        def per_tile(index, carry):
                            body(member, low, high, pl.multiple_of(index * tile, tile))
                            return carry

                        lax.fori_loop(0, filled, per_tile, 0)

        return carry

    lax.fori_loop(0, members, per_member, 0)


def backward_kernel(step, layers, heads, head_dim, counts, *refs):
    q, g, turned_q, turned_g, final = refs[:5]
    refs = refs[5:]
    kinds = kinds_of(step, layers)
    count = len(kinds)
    pairs, refs = refs[:count], refs[count:]
    earlier = None
    if step < layers:
        earlier, refs = refs[0], refs[1:]
    if step == layers - 1:
        stay, leave = refs[:2]
        refs = refs[2:]
    made = 3 if step == layers else count
    grads, query_out, refs = refs[:made], refs[made], refs[made + 1 :]
    keys, values, turned, probs_held, scores_held, sums = refs
    place = lax.axis_index("ctx")
    members, all_rows = q.shape[:2]
    tile = tile_of(all_rows)
    tokens = all_rows // heads
    plain = head_dim**-0.5
    scale = plain * math.log2(math.e)
    edges = edges_of(counts)
    attended = attends(step, layers, place)

    def body(member, low, high, first):
        whole = pl.ds(first, tile)
        total = final[member, TOTAL : TOTAL + 1, whole]
        level = final[member, TOP : TOP + 1, whole] + jnp.log2(total)
        delta = final[member, DOTTED : DOTTED + 1, whole] / total
        token_weight = final[member, WEIGHT : WEIGHT + 1, whole]
        for start in range(0, tile, SUB_ROWS):
            rows = pl.ds(pl.multiple_of(first + start, SUB_ROWS), SUB_ROWS)
            held = slice(start, start + SUB_ROWS)
            scores = dot(keys[low:high, :], turned_q[member, :, rows]) * scale
            scores = scores - level[:, held]
            if step == 0:
                kept = kept_keys(scores.shape, first + start, heads)
                scores = jnp.where(kept, scores, MASKED)
            probs = jnp.exp2(scores) * token_weight[:, held]
            grad_probs = dot(values[low:high, :], turned_g[member, :, rows])
            grad_scores = probs * (grad_probs - delta[:, held])
            probs_held[low:high, held] = probs.astype(jnp.bfloat16)
            scores_held[low:high, held] = grad_scores.astype(jnp.bfloat16)
        sums[low:high, head_dim:] += dot(probs_held[low:high, :], g[member, whole, :])
        sums[low:high, :head_dim] += dot(scores_held[low:high, :], q[member, whole, :])
        moved = dot(turned[:, low:high], scores_held[low:high, :])
        if earlier is not None:
            moved = moved + earlier[member, :, whole]
        if step == 0:
            query_out[member, whole, :] = (moved * plain).T.astype(jnp.bfloat16)
        else:
            query_out[member, :, whole] = moved

    def per_member(member, carry):
        filled = filled_tiles(length_of(final, member), tokens, heads, all_rows)
        filled = jnp.where(attended, filled, 0)
        for part in range(count):
            rows = pl.ds(edges[part], edges[part + 1] - edges[part])

            @pl.when((member == 0) | (kinds[part] != "prompt"))
            def _():
                sums[rows, :] = jnp.zeros_like(sums[rows, :])

        @pl.when(filled > 0)
        def _():
            load_keys(member, pairs, kinds, edges, head_dim, keys, values)
            turned[...] = keys[...].T

            def per_tile(index, carry):
                first = pl.multiple_of(index * tile, tile)
                for condition, begin, past in variants(step, layers, place):
                    run = functools.partial(body, member, edges[begin], edges[past], first)
                    if condition is None:
                        run()
                    else:
                        pl.when(condition)(run)
                return carry

            lax.fori_loop(0, filled, per_tile, 0)

        if step == 0 or earlier is None:

            def clear(index, carry):
                rows = pl.ds(pl.multiple_of(index * tile, tile), tile)
                if step == 0:
                    query_out[member, rows, :] = jnp.zeros((tile, head_dim), jnp.bfloat16)
                else:
                    query_out[member, :, rows] = jnp.zeros((head_dim, tile), jnp.float32)
                return carry

            lax.fori_loop(filled, all_rows // tile, clear, 0)
        for part in range(count):
            if kinds[part] == "prompt":
                continue
            rows = pl.ds(edges[part], counts[part])
            own = pl.ds(pl.multiple_of(member * counts[part], counts[part]), counts[part])
            grads[part][own, :head_dim] = (sums[rows, :head_dim] * plain).astype(jnp.bfloat16)
            grads[part][own, head_dim:] = sums[rows, head_dim:].astype(jnp.bfloat16)
        return carry

    lax.fori_loop(0, members, per_member, 0)
    tail = members * tokens
    if step == layers:
        far, stay, leave = grads
        middle = edges[1] + stay.shape[0]
        last = middle + leave.shape[0]
        for target, begin, rows in (
            (stay, 0, slice(edges[1], middle)),
            (leave, 0, slice(middle, last)),
            (far, tail, slice(last, edges[2])),
        ):
            end = target.shape[0]
            target[begin:end, :head_dim] = (sums[rows, :head_dim] * plain).astype(target.dtype)
            target[begin:end, head_dim:] = sums[rows, head_dim:].astype(target.dtype)
    elif step == layers - 1:
        grads[0][tail:, :] = leave[...]
        grads[1][tail:, :] = stay[leave.shape[0] :, :].astype(jnp.bfloat16)


def combine_kernel(step, layers, each, own, side, above, kept, *refs):
    def wide(ref, rows):
        return ref[rows, :].astype(jnp.float32)

    count = own.shape[0]
    rows = slice(0, count)
    mine = slice(step * each, (step + 1) * each)
    prompt = kept[mine, :] + wide(above, slice(count, None))
    if step == layers - 2:
        prompt = prompt + wide(side, slice(count + mine.start, count + mine.stop))
    total = wide(own, rows) + wide(side, rows) + wide(above, rows)
    if step > 0:
        out = refs[0]
        out[rows, :] = total.astype(jnp.bfloat16)
        out[count:, :] = prompt.astype(jnp.bfloat16)
        if step == layers - 2:
            refs[1][...] = kept[: step * each, :] + wide(side, slice(count, count + step * each))
    else:
        far, key_out, value_out, prompt_out = refs
        total = (total + wide(far, rows)).astype(jnp.bfloat16)
        head_dim = key_out.shape[1]
        key_out[...] = total[:, :head_dim]
        value_out[...] = total[:, head_dim:]
        prompt_out[...] = prompt + wide(far, slice(count, None))


def tile_of(rows):
    return min(TILE_ROWS, rows)


WHOLE = pl.BlockSpec(memory_space=pltpu.VMEM)
PARAMS = pltpu.CompilerParams(vmem_limit_bytes=VMEM_BYTES)
LITTLE = pl.CostEstimate(flops=1000, bytes_accessed=1000, transcendentals=0)


OUTSIDE = pl.BlockSpec(memory_space=pltpu.HBM)


def forward_step(step, layers, heads, tokens, operands, messages, earlier):
    q = operands[1] if step == 0 else operands[0]
    members, head_dim, rows = q.shape
    if step == 0:
        rows, head_dim = head_dim, rows
    each = messages[0].shape[0] - members * tokens
    counts = [tokens] * len(kinds_of(step, layers))
    if step == layers:
        counts[1] = 2 * layers * each
    columns = sum(counts)
    out_shape = [jax.ShapeDtypeStruct((members, 8, rows), jnp.float32)]
    scratch = [pltpu.VMEM((columns, head_dim), jnp.bfloat16)] * 2
    extra = [] if step == 0 else [earlier]
    in_specs = [WHOLE] * 3
    if step == 0:
        in_specs = [WHOLE] + [OUTSIDE] * 2
        out_shape += [jax.ShapeDtypeStruct(q.shape, q.dtype)] * 2
        out_shape += [jax.ShapeDtypeStruct((members, head_dim, rows), q.dtype)] * 2
        scratch += [pltpu.SemaphoreType.DMA((2,))]
    elif step == layers:
        out_shape.append(jax.ShapeDtypeStruct((counts[1], 2 * head_dim), jnp.bfloat16))
    return pl.pallas_call(
        functools.partial(forward_kernel, step, layers, heads, head_dim, counts),
        in_specs=in_specs + [WHOLE] * len(messages),
        out_specs=[WHOLE] * len(out_shape),
        out_shape=out_shape,
        scratch_shapes=scratch,
        compiler_params=PARAMS,
        cost_estimate=LITTLE,
        input_output_aliases={} if step == 0 else {2: 0},
        name=f"attend_step{step}",
    )(*operands, *extra, *messages)


def backward_step(
    step, layers, heads, tokens, each, held_rows, final, messages, earlier, prompt_terms
):
    q = held_rows[0]
    members, rows, head_dim = q.shape
    counts = [tokens] * len(kinds_of(step, layers))

    def block(more, dtype=jnp.bfloat16, base=members * tokens):
        return jax.ShapeDtypeStruct((base + more, 2 * head_dim), dtype)

    if step == layers:
        counts[1] = 2 * layers * each
        grad_shapes = [
            block(each),
            block(layers * each, jnp.float32, 0),
            block((layers - 1) * each, jnp.bfloat16, 0),
        ]
    elif step == layers - 1:
        grad_shapes = [block((layers - 1) * each), block(each)]
    else:
        grad_shapes = [block(0)] * len(counts)
    columns = sum(counts)
    tile = tile_of(rows)
    if step == 0:
        query_shape = jax.ShapeDtypeStruct(q.shape, jnp.bfloat16)
    else:
        query_shape = jax.ShapeDtypeStruct((members, head_dim, rows), jnp.float32)
    extra = [] if earlier is None else [earlier]
    aliases = {5 + len(messages): len(grad_shapes)} if extra and step > 0 else {}
    if step == layers - 1:
        extra += prompt_terms
    outs = pl.pallas_call(
        functools.partial(backward_kernel, step, layers, heads, head_dim, counts),
        in_specs=[WHOLE] * (5 + len(messages) + len(extra)),
        out_specs=[WHOLE] * (len(grad_shapes) + 1),
        out_shape=grad_shapes + [query_shape],
        scratch_shapes=[pltpu.VMEM((columns, head_dim), jnp.bfloat16)] * 2
        + [pltpu.VMEM((head_dim, columns), jnp.bfloat16)]
        + [pltpu.VMEM((columns, tile), jnp.bfloat16)] * 2
        + [pltpu.VMEM((columns, 2 * head_dim), jnp.float32)],
        compiler_params=PARAMS,
        cost_estimate=LITTLE,
        input_output_aliases=aliases,
        name=f"attend_grad_step{step}",
    )(*held_rows, final, *messages, *extra)
    return outs[:-1], outs[-1]


def combine(step, layers, each, *terms):
    count, width = terms[0].shape
    if step > 0:
        shapes = [jax.ShapeDtypeStruct((count + each, width), jnp.bfloat16)]
        if step == layers - 2:
            shapes.append(jax.ShapeDtypeStruct((step * each, width), jnp.float32))
    else:
        shapes = [jax.ShapeDtypeStruct((count, width // 2), jnp.bfloat16)] * 2
        shapes.append(jax.ShapeDtypeStruct((each, width), jnp.float32))
    return pl.pallas_call(
        functools.partial(combine_kernel, step, layers, each),
        in_specs=[WHOLE] * len(terms),
        out_specs=[WHOLE] * len(shapes),
        out_shape=shapes,
        compiler_params=PARAMS,
        name=f"add_terms{step}",
    )(*terms)


def join_kernel(
    keys, values, prompt_keys, prompt_values, behaved, current, advantages, lengths, *refs
):
    out, policy, held_behaved, held_current, held_advantages, held_lengths, arrived = refs
    rows, head_dim = keys.shape
    members, tokens = behaved.shape

    def part(first, count, column):
        return out.at[pl.ds(first, count), pl.ds(column, head_dim)]

    each = prompt_keys.shape[0]
    targets = [
        (keys, part(0, rows, 0)),
        (values, part(0, rows, head_dim)),
        (prompt_keys, part(rows, each, 0)),
        (prompt_values, part(rows, each, head_dim)),
        (behaved, held_behaved),
        (current, held_current),
        (advantages, held_advantages),
        (lengths, held_lengths),
    ]
    copies = [
        pltpu.make_async_copy(source, target, arrived.at[i])
        for i, (source, target) in enumerate(targets)
    ]
    for copy in copies:
        copy.start()
    for copy in copies:
        copy.wait()
    full_len = tokens * lax.axis_size("ctx")
    position = lax.axis_index("ctx") * tokens + lax.broadcasted_iota(jnp.int32, (1, tokens), 1)
    ratio = jnp.minimum(jnp.exp(held_current[...] - held_behaved[...]), RATIO_CAP)
    for member in range(members):
        length = held_lengths[member]
        spread = full_len / jnp.full((1, 1), length).astype(jnp.float32)
        valid = jnp.where(position < length, ratio[member : member + 1], 0.0)
        policy[member : member + 1, :] = -held_advantages[member] * valid * spread
        wide = jnp.full((1, tokens), length).astype(jnp.float32)
        policy[members + member : members + member + 1, :] = wide


def join(keys, values, prompt_keys, prompt_values, behaved, current, advantages, lengths):
    rows = keys.shape[0] + prompt_keys.shape[0]
    members, tokens = behaved.shape
    return pl.pallas_call(
        join_kernel,
        out_shape=[
            jax.ShapeDtypeStruct((rows, 2 * keys.shape[1]), keys.dtype),
            jax.ShapeDtypeStruct((2 * members, tokens), jnp.float32),
        ],
        in_specs=[OUTSIDE] * 8,
        out_specs=[WHOLE] * 2,
        scratch_shapes=[
            pltpu.VMEM((members, tokens), jnp.float32),
            pltpu.VMEM((members, tokens), jnp.float32),
            pltpu.SMEM((members,), jnp.float32),
            pltpu.SMEM((members,), jnp.int32),
            pltpu.SemaphoreType.DMA((8,)),
        ],
        compiler_params=pltpu.CompilerParams(vmem_limit_bytes=JOIN_VMEM_BYTES),
        cost_estimate=LITTLE,
        name="join_pairs",
    )(keys, values, prompt_keys, prompt_values, behaved, current, advantages, lengths)


def per_device(
    queries,
    prompt_keys,
    prompt_values,
    resp_keys,
    resp_values,
    upstream,
    behav_logp,
    cur_logp,
    advantages,
    lengths,
):
    members, tokens, heads, head_dim = queries.shape
    ctx_size, resp_size = lax.axis_size("ctx"), lax.axis_size("resp")
    layers = ctx_size // 2
    each = prompt_keys.shape[0]
    rows = tokens * heads

    def hop(array, layers_up):
        pairs = [(c, (c + 2 * layers_up) % ctx_size) for c in range(ctx_size)]
        return lax.ppermute(array, "ctx", pairs)

    def cross(array, layers_up=0):
        pairs = [(c, ((c + 2 * layers_up) % ctx_size) ^ 1) for c in range(ctx_size)]
        return lax.ppermute(array, "ctx", pairs)

    own, policy = join(
        resp_keys.reshape(members * tokens, head_dim),
        resp_values.reshape(members * tokens, head_dim),
        prompt_keys,
        prompt_values,
        behav_logp,
        cur_logp,
        advantages,
        lengths,
    )
    z, x = [own], [None]
    operands = (
        policy,
        queries.reshape(members, rows, head_dim),
        upstream.reshape(members, rows, head_dim),
    )
    stat = prompt = None
    far_message = cross(own, layers - 1)
    for step in range(layers + 1):
        if step < layers:
            held = z[step]
            if step > 0:
                held, stat = lax.optimization_barrier((held, stat))
                if step == 1:
                    held, far_message = lax.optimization_barrier((held, far_message))
                z[step] = held
            if step + 1 < layers:
                z.append(hop(held, 1))
                x.append(cross(held))
            if step + 1 == layers:
                x.append(far_message)
        if step == 0:
            stat, *held_rows = forward_step(0, layers, heads, tokens, operands, z[:1], None)
            operands = held_rows[2:]
        elif step < layers:
            (stat,) = forward_step(
                step, layers, heads, tokens, operands, [x[step], z[step]], stat
            )
        else:
            stat, prompt = forward_step(step, layers, heads, tokens, operands, z + x[1:], stat)

    final = stat
    moved = side = above = far = message = kept = terms = None
    for step in range(layers, -1, -1):
        if message is not None:
            final, message = lax.optimization_barrier((final, message))
            above = hop(message, -1)
        if step == layers:
            messages = [x[step], prompt]
        else:
            messages = [z[0]] if step == 0 else [x[step], z[step]]
        grads, moved = backward_step(
            step, layers, heads, tokens, each, held_rows, final, messages, moved, terms
        )
        if step == layers:
            far, terms = cross(grads[0], 1 - layers), list(grads[1:])
            kept = grads[1]
        elif step == layers - 1:
            message = grads[1]
        elif step > 0:
            message, *more = combine(step, layers, each, grads[-1], side, above, kept)
            kept = more[0] if more else kept
        if 0 < step < layers:
            side = cross(grads[0])
    key_grads, value_grads, share = combine(0, layers, each, grads[-1], side, above, kept, far)
    stride = 1
    while stride < resp_size:
        pairs = [(c, c ^ stride) for c in range(resp_size)]
        share = share + lax.ppermute(share, "resp", pairs)
        stride *= 2
    return (
        moved.reshape(queries.shape),
        key_grads.reshape(resp_keys.shape),
        value_grads.reshape(resp_values.shape),
        share[:, :head_dim],
        share[:, head_dim:],
    )


def solution(mesh):
    placed = (
        P("resp", "ctx", None, None),
        P("ctx", None),
        P("ctx", None),
        P("resp", "ctx", None),
        P("resp", "ctx", None),
        P("resp", "ctx", None, None),
        P("resp", "ctx"),
        P("resp", "ctx"),
        P("resp"),
        P("resp"),
    )
    return jax.shard_map(
        per_device,
        mesh=mesh,
        in_specs=placed,
        out_specs=(
            P("resp", "ctx", None, None),
            P("resp", "ctx", None),
            P("resp", "ctx", None),
            P("ctx", None),
            P("ctx", None),
        ),
        check_vma=False,
    )
```

```python
import functools
import math

import jax
import jax.numpy as jnp
from jax import lax
from jax.experimental import pallas as pl
from jax.experimental.pallas import tpu as pltpu
from jax.sharding import PartitionSpec as P

RATIO_CAP = 2.0
MASKED = -1e30
SUB_ROWS = 256
TILE_ROWS = 1024
LARGEST_SCORE = 100.0
UNBOUNDED = 3e38

TOP, TOTAL, DOTTED, GUARD, WEIGHT, LENGTH = range(6)
VMEM_BYTES = 24 * 1024 * 1024
JOIN_VMEM_BYTES = 60 * 1024 * 1024

def dot(a, b):
    return jnp.dot(a, b, preferred_element_type=jnp.float32)


def kinds_of(step, layers):
    if step == 0:
        return ("z",)
    return ("x", "prompt") if step == layers else ("x", "z")


def variants(step, layers, place):
    z, odd = place // 2, place % 2 == 1
    if step == 0:
        return [(None, 0, 1)]
    if step == layers:
        return [(z >= step - 1, 0, 2), (z < step - 1, 1, 2)]
    if step == 1:
        return [
            ((z >= 1) & odd, 0, 2),
            ((z == 0) & odd, 0, 1),
            ((z >= 1) & jnp.logical_not(odd), 1, 2),
        ]
    return [(z >= step, 0, 2), (z == step - 1, 0, 1)]


def attends(step, layers, place):
    if step in (0, layers):
        return place >= 0
    return place >= 1 if step == 1 else place // 2 >= step - 1


def kept_keys(shape, first_row, heads):
    key = lax.broadcasted_iota(jnp.int32, shape, 0)
    row = lax.broadcasted_iota(jnp.int32, shape, 1) + first_row
    return key * heads <= row


def edges_of(counts):
    edges = [0]
    for count in counts:
        edges.append(edges[-1] + count)
    return edges


def largest_norm(rows):
    wide = rows.astype(jnp.float32)
    return jnp.max(jnp.sum(wide * wide, axis=1, keepdims=True))


def filled_tiles(length, tokens, heads, rows):
    per_tile = tile_of(rows) // heads
    left = length - lax.axis_index("ctx") * tokens
    return jnp.clip((left + per_tile - 1) // per_tile, 0, rows // tile_of(rows))


def load_keys(member, pairs, kinds, edges, head_dim, keys, values):
    for part, pair in enumerate(pairs):
        count = edges[part + 1] - edges[part]
        rows = pl.ds(edges[part], count)
        own = pl.ds(0, count)
        if kinds[part] != "prompt":
            own = pl.ds(pl.multiple_of(member * count, count), count)
        keys[rows, :] = pair[own, :head_dim]
        values[rows, :] = pair[own, head_dim:]


def length_of(stat, member):
    return jnp.max(stat[member, LENGTH : LENGTH + 1, 0:128]).astype(jnp.int32)


def spread_weights(ratio, heads):
    tokens = ratio.shape[1]
    shape = (tokens, tokens * heads)
    token = lax.broadcasted_iota(jnp.int32, shape, 0)
    row = lax.broadcasted_iota(jnp.int32, shape, 1)
    first = token * heads
    chosen = jnp.where((row >= first) & (row < first + heads), 1.0, 0.0)
    chosen = chosen.astype(jnp.bfloat16)
    out, rest = None, ratio
    for _ in range(3):
        term = rest.astype(jnp.bfloat16)
        rest = rest - term.astype(jnp.float32)
        few = jnp.broadcast_to(term.astype(jnp.float32), (16, tokens)).astype(jnp.bfloat16)
        part = jnp.dot(few, chosen, preferred_element_type=jnp.float32)[0:1]
        out = part if out is None else out + part
    return out


def key_sum(array):
    count = array.shape[0] // 4
    parts = [
        jnp.sum(array[i * count : (i + 1) * count], axis=0, keepdims=True) for i in range(4)
    ]
    return (parts[0] + parts[1]) + (parts[2] + parts[3])


def forward_kernel(step, layers, heads, head_dim, counts, *refs):
    kinds = kinds_of(step, layers)
    parts = len(kinds)
    earlier = None
    if step == 0:
        policy, held_q, held_g, message, out, q, g, turned_q, turned_g = refs[:9]
        keys, values, arrived = refs[9:]
        pairs = [message]
        copies = [
            pltpu.make_async_copy(source, target, arrived.at[i])
            for i, (source, target) in enumerate([(held_q, q), (held_g, g)])
        ]
        for copy in copies:
            copy.start()
        for copy in copies:
            copy.wait()
    else:
        turned_q, turned_g, earlier = refs[:3]
        refs = refs[3:]
        if step == layers:
            messages, (out, prompt, keys, values) = refs[: 2 * layers], refs[2 * layers :]
            own = messages[0].shape[0] - prompt.shape[0] // (2 * layers)
            each = messages[0].shape[0] - own
            for i, message in enumerate(messages):
                prompt[i * each : (i + 1) * each, :] = message[own:, :]
            pairs = [messages[-1], prompt]
        else:
            pairs, (out, keys, values) = refs[:parts], refs[parts:]
    place = lax.axis_index("ctx")
    members, _, all_rows = turned_q.shape
    tile = tile_of(all_rows)
    tokens = all_rows // heads
    scale = head_dim**-0.5 * math.log2(math.e)
    edges = edges_of(counts)
    attended = attends(step, layers, place)

    def shared(member, low, high, first, start):
        rows = pl.ds(pl.multiple_of(first + start, SUB_ROWS), SUB_ROWS)
        scores = dot(keys[low:high, :], turned_q[member, :, rows]) * scale
        if step == 0:
            kept = kept_keys(scores.shape, first + start, heads)
            scores = jnp.where(kept, scores, MASKED)
        return rows, scores, dot(values[low:high, :], turned_g[member, :, rows])

    def put(member, first, lines):
        rows = pl.ds(first, tile)
        for line, pieces in lines.items():
            out[member, line : line + 1, rows] = jnp.concatenate(pieces, 1)

    def bounded(member, low, high, first):
        totals, dots = [], []
        for start in range(0, tile, SUB_ROWS):
            rows, scores, grad_probs = shared(member, low, high, first, start)
            weight = jnp.exp2(scores)
            total, dotted = key_sum(weight), key_sum(weight * grad_probs)
            if earlier is not None:
                total = total + earlier[member, TOTAL : TOTAL + 1, rows]
                dotted = dotted + earlier[member, DOTTED : DOTTED + 1, rows]
            totals.append(total)
            dots.append(dotted)
        tops = [jnp.zeros_like(t) for t in totals]
        put(member, first, {TOP: tops, TOTAL: totals, DOTTED: dots})

    def general(member, low, high, first):
        tops, totals, dots = [], [], []
        for start in range(0, tile, SUB_ROWS):
            rows, scores, grad_probs = shared(member, low, high, first, start)
            top = jnp.max(scores, axis=0, keepdims=True)
            if earlier is not None:
                top = jnp.maximum(top, earlier[member, TOP : TOP + 1, rows])
            weight = jnp.exp2(scores - top)
            total, dotted = key_sum(weight), key_sum(weight * grad_probs)
            if earlier is not None:
                decay = jnp.exp2(earlier[member, TOP : TOP + 1, rows] - top)
                total = total + decay * earlier[member, TOTAL : TOTAL + 1, rows]
                dotted = dotted + decay * earlier[member, DOTTED : DOTTED + 1, rows]
            tops.append(top)
            totals.append(total)
            dots.append(dotted)
        guards = [jnp.full_like(t, UNBOUNDED) for t in totals]
        put(member, first, {TOP: tops, TOTAL: totals, DOTTED: dots, GUARD: guards})

    def per_member(member, carry):
        if step == 0:
            line = lax.broadcasted_iota(jnp.int32, policy.shape, 0)

            known = jnp.max(jnp.where(line == members + member, policy[...], 0.0))
            length = known.astype(jnp.int32)
            out[member, LENGTH : LENGTH + 1, :] = jnp.full((1, all_rows), known)
        else:
            length = length_of(earlier, member)
        filled = filled_tiles(length, tokens, heads, all_rows)

        @pl.when((filled > 0) & attended)
        def _():
            load_keys(member, pairs, kinds, edges, head_dim, keys, values)
            limit = (LARGEST_SCORE / scale) ** 2 / largest_norm(keys[...])

            def prepare(index, carry):
                first = pl.multiple_of(index * tile, tile)
                rows = pl.ds(first, tile)
                turned_q[member, :, rows] = q[member, rows, :].T
                turned_g[member, :, rows] = g[member, rows, :].T
                guard = largest_norm(q[member, rows, :])
                out[member, GUARD : GUARD + 1, rows] = jnp.full((1, tile), guard)
                count = tile // heads
                part = pl.ds(pl.multiple_of(index * count, count), count)
                if count == tokens:
                    part = pl.ds(0, count)
                chosen = jnp.where(line[:, :count] == member, policy[:, part], 0.0)
                ratio = jnp.sum(chosen, axis=0, keepdims=True)
                out[member, WEIGHT : WEIGHT + 1, rows] = spread_weights(ratio, heads)
                return carry

            if step == 0:
                lax.fori_loop(0, filled, prepare, 0)
            guards = (out if step == 0 else earlier)[member, GUARD : GUARD + 1, :]
            column = lax.broadcasted_iota(jnp.int32, guards.shape, 1)
            fast = jnp.max(jnp.where(column < filled * tile, guards, 0.0)) <= limit
            for condition, begin, past in variants(step, layers, place):
                low, high = edges[begin], edges[past]
                for quick, body in ((fast, bounded), (jnp.logical_not(fast), general)):

                    @pl.when(quick if condition is None else quick & condition)
                    def _():
                        def per_tile(index, carry):
                            body(member, low, high, pl.multiple_of(index * tile, tile))
                            return carry

                        lax.fori_loop(0, filled, per_tile, 0)

        return carry

    lax.fori_loop(0, members, per_member, 0)


def backward_kernel(step, layers, heads, head_dim, counts, *refs):
    q, g, turned_q, turned_g, final = refs[:5]
    refs = refs[5:]
    kinds = kinds_of(step, layers)
    count = len(kinds)
    pairs, refs = refs[:count], refs[count:]
    earlier = None
    if step < layers:
        earlier, refs = refs[0], refs[1:]
    if step == layers - 1:
        stay, leave = refs[:2]
        refs = refs[2:]
    elif step == 1:
        far, refs = refs[0], refs[1:]
    made = 3 if step == layers else count
    grads, query_out, refs = refs[:made], refs[made], refs[made + 1 :]
    keys, values, turned, probs_held, scores_held, sums = refs
    place = lax.axis_index("ctx")
    members, all_rows = q.shape[:2]
    tile = tile_of(all_rows)
    tokens = all_rows // heads
    plain = head_dim**-0.5
    scale = plain * math.log2(math.e)
    edges = edges_of(counts)
    attended = attends(step, layers, place)

    def body(member, low, high, first):
        whole = pl.ds(first, tile)
        total = final[member, TOTAL : TOTAL + 1, whole]
        level = final[member, TOP : TOP + 1, whole] + jnp.log2(total)
        delta = final[member, DOTTED : DOTTED + 1, whole] / total
        token_weight = final[member, WEIGHT : WEIGHT + 1, whole]
        for start in range(0, tile, SUB_ROWS):
            rows = pl.ds(pl.multiple_of(first + start, SUB_ROWS), SUB_ROWS)
            held = slice(start, start + SUB_ROWS)
            scores = dot(keys[low:high, :], turned_q[member, :, rows]) * scale
            scores = scores - level[:, held]
            if step == 0:
                kept = kept_keys(scores.shape, first + start, heads)
                scores = jnp.where(kept, scores, MASKED)
            probs = jnp.exp2(scores) * token_weight[:, held]
            grad_probs = dot(values[low:high, :], turned_g[member, :, rows])
            grad_scores = probs * (grad_probs - delta[:, held])
            probs_held[low:high, held] = probs.astype(jnp.bfloat16)
            scores_held[low:high, held] = grad_scores.astype(jnp.bfloat16)
        sums[low:high, head_dim:] += dot(probs_held[low:high, :], g[member, whole, :])
        sums[low:high, :head_dim] += dot(scores_held[low:high, :], q[member, whole, :])
        moved = dot(turned[:, low:high], scores_held[low:high, :])
        if earlier is not None:
            moved = moved + earlier[member, :, whole]
        if step == 0:
            query_out[member, whole, :] = (moved * plain).T.astype(jnp.bfloat16)
        else:
            query_out[member, :, whole] = moved

    def per_member(member, carry):
        filled = filled_tiles(length_of(final, member), tokens, heads, all_rows)
        filled = jnp.where(attended, filled, 0)
        for part in range(count):
            rows = pl.ds(edges[part], edges[part + 1] - edges[part])

            @pl.when((member == 0) | (kinds[part] != "prompt"))
            def _():
                sums[rows, :] = jnp.zeros_like(sums[rows, :])

        @pl.when(filled > 0)
        def _():
            load_keys(member, pairs, kinds, edges, head_dim, keys, values)
            turned[...] = keys[...].T

            def per_tile(index, carry):
                first = pl.multiple_of(index * tile, tile)
                for condition, begin, past in variants(step, layers, place):
                    run = functools.partial(body, member, edges[begin], edges[past], first)
                    if condition is None:
                        run()
                    else:
                        pl.when(condition)(run)
                return carry

            lax.fori_loop(0, filled, per_tile, 0)

        if step == 0 or earlier is None:

            def clear(index, carry):
                rows = pl.ds(pl.multiple_of(index * tile, tile), tile)
                if step == 0:
                    query_out[member, rows, :] = jnp.zeros((tile, head_dim), jnp.bfloat16)
                else:
                    query_out[member, :, rows] = jnp.zeros((head_dim, tile), jnp.float32)
                return carry

            lax.fori_loop(filled, all_rows // tile, clear, 0)
        for part in range(count):
            if kinds[part] == "prompt":
                continue
            rows = pl.ds(edges[part], counts[part])
            own = pl.ds(pl.multiple_of(member * counts[part], counts[part]), counts[part])
            key_part, value_part = sums[rows, :head_dim] * plain, sums[rows, head_dim:]
            if step == 1 and part == 0:
                key_part = key_part + far[own, :head_dim].astype(jnp.float32)
                value_part = value_part + far[own, head_dim:].astype(jnp.float32)
            grads[part][own, :head_dim] = key_part.astype(jnp.bfloat16)
            grads[part][own, head_dim:] = value_part.astype(jnp.bfloat16)
        return carry

    lax.fori_loop(0, members, per_member, 0)
    tail = members * tokens
    if step == layers:
        far, stay, leave = grads
        middle = edges[1] + stay.shape[0]
        last = middle + leave.shape[0]
        for target, begin, rows in (
            (stay, 0, slice(edges[1], middle)),
            (leave, 0, slice(middle, last)),
            (far, tail, slice(last, edges[2])),
        ):
            end = target.shape[0]
            target[begin:end, :head_dim] = (sums[rows, :head_dim] * plain).astype(target.dtype)
            target[begin:end, head_dim:] = sums[rows, head_dim:].astype(target.dtype)
    elif step == layers - 1:
        grads[0][tail:, :] = leave[...]
        grads[1][tail:, :] = stay[leave.shape[0] :, :].astype(jnp.bfloat16)
    elif step == 1:
        grads[0][tail:, :] = far[tail:, :]


def combine_kernel(step, layers, each, own, side, above, kept, *refs):
    def wide(ref, rows):
        return ref[rows, :].astype(jnp.float32)

    count = own.shape[0]
    rows = slice(0, count)
    mine = slice(step * each, (step + 1) * each)
    prompt = kept[mine, :] + wide(above, slice(count, None))
    if step == layers - 2:
        prompt = prompt + wide(side, slice(count + mine.start, count + mine.stop))
    total = wide(own, rows) + wide(side, rows) + wide(above, rows)
    if step > 0:
        out = refs[0]
        out[rows, :] = total.astype(jnp.bfloat16)
        out[count:, :] = prompt.astype(jnp.bfloat16)
        if step == layers - 2:
            refs[1][...] = kept[: step * each, :] + wide(side, slice(count, count + step * each))
    else:
        key_out, value_out, prompt_out = refs
        total = total.astype(jnp.bfloat16)
        head_dim = key_out.shape[1]
        key_out[...] = total[:, :head_dim]
        value_out[...] = total[:, head_dim:]
        prompt_out[...] = prompt + wide(side, slice(count, None))


def tile_of(rows):
    return min(TILE_ROWS, rows)


WHOLE = pl.BlockSpec(memory_space=pltpu.VMEM)
PARAMS = pltpu.CompilerParams(vmem_limit_bytes=VMEM_BYTES)
LITTLE = pl.CostEstimate(flops=1000, bytes_accessed=1000, transcendentals=0)


OUTSIDE = pl.BlockSpec(memory_space=pltpu.HBM)


def forward_step(step, layers, heads, tokens, operands, messages, earlier):
    q = operands[1] if step == 0 else operands[0]
    members, head_dim, rows = q.shape
    if step == 0:
        rows, head_dim = head_dim, rows
    each = messages[0].shape[0] - members * tokens
    counts = [tokens] * len(kinds_of(step, layers))
    if step == layers:
        counts[1] = 2 * layers * each
    columns = sum(counts)
    out_shape = [jax.ShapeDtypeStruct((members, 8, rows), jnp.float32)]
    scratch = [pltpu.VMEM((columns, head_dim), jnp.bfloat16)] * 2
    extra = [] if step == 0 else [earlier]
    in_specs = [WHOLE] * 3
    if step == 0:
        in_specs = [WHOLE] + [OUTSIDE] * 2
        out_shape += [jax.ShapeDtypeStruct(q.shape, q.dtype)] * 2
        out_shape += [jax.ShapeDtypeStruct((members, head_dim, rows), q.dtype)] * 2
        scratch += [pltpu.SemaphoreType.DMA((2,))]
    elif step == layers:
        out_shape.append(jax.ShapeDtypeStruct((counts[1], 2 * head_dim), jnp.bfloat16))
    return pl.pallas_call(
        functools.partial(forward_kernel, step, layers, heads, head_dim, counts),
        in_specs=in_specs + [WHOLE] * len(messages),
        out_specs=[WHOLE] * len(out_shape),
        out_shape=out_shape,
        scratch_shapes=scratch,
        compiler_params=PARAMS,
        cost_estimate=LITTLE,
        input_output_aliases={} if step == 0 else {2: 0},
        name=f"attend_step{step}",
    )(*operands, *extra, *messages)


def backward_step(
    step, layers, heads, tokens, each, held_rows, final, messages, earlier, prompt_terms
):
    q = held_rows[0]
    members, rows, head_dim = q.shape
    counts = [tokens] * len(kinds_of(step, layers))

    def block(more, dtype=jnp.bfloat16, base=members * tokens):
        return jax.ShapeDtypeStruct((base + more, 2 * head_dim), dtype)

    if step == layers:
        counts[1] = 2 * layers * each
        grad_shapes = [
            block(each),
            block(layers * each, jnp.float32, 0),
            block((layers - 1) * each, jnp.bfloat16, 0),
        ]
    elif step == layers - 1:
        grad_shapes = [block((layers - 1) * each), block(each)]
    elif step == 1:
        grad_shapes = [block(each), block(0)]
    else:
        grad_shapes = [block(0)] * len(counts)
    columns = sum(counts)
    tile = tile_of(rows)
    if step == 0:
        query_shape = jax.ShapeDtypeStruct(q.shape, jnp.bfloat16)
    else:
        query_shape = jax.ShapeDtypeStruct((members, head_dim, rows), jnp.float32)
    extra = [] if earlier is None else [earlier]
    aliases = {5 + len(messages): len(grad_shapes)} if extra and step > 0 else {}
    extra += prompt_terms
    outs = pl.pallas_call(
        functools.partial(backward_kernel, step, layers, heads, head_dim, counts),
        in_specs=[WHOLE] * (5 + len(messages) + len(extra)),
        out_specs=[WHOLE] * (len(grad_shapes) + 1),
        out_shape=grad_shapes + [query_shape],
        scratch_shapes=[pltpu.VMEM((columns, head_dim), jnp.bfloat16)] * 2
        + [pltpu.VMEM((head_dim, columns), jnp.bfloat16)]
        + [pltpu.VMEM((columns, tile), jnp.bfloat16)] * 2
        + [pltpu.VMEM((columns, 2 * head_dim), jnp.float32)],
        compiler_params=PARAMS,
        cost_estimate=LITTLE,
        input_output_aliases=aliases,
        name=f"attend_grad_step{step}",
    )(*held_rows, final, *messages, *extra)
    return outs[:-1], outs[-1]


def combine(step, layers, each, *terms):
    count, width = terms[0].shape
    if step > 0:
        shapes = [jax.ShapeDtypeStruct((count + each, width), jnp.bfloat16)]
        if step == layers - 2:
            shapes.append(jax.ShapeDtypeStruct((step * each, width), jnp.float32))
    else:
        shapes = [jax.ShapeDtypeStruct((count, width // 2), jnp.bfloat16)] * 2
        shapes.append(jax.ShapeDtypeStruct((each, width), jnp.float32))
    return pl.pallas_call(
        functools.partial(combine_kernel, step, layers, each),
        in_specs=[WHOLE] * len(terms),
        out_specs=[WHOLE] * len(shapes),
        out_shape=shapes,
        compiler_params=PARAMS,
        name=f"add_terms{step}",
    )(*terms)


def join_kernel(
    keys, values, prompt_keys, prompt_values, behaved, current, advantages, lengths, *refs
):
    out, policy, held_behaved, held_current, held_advantages, held_lengths, arrived = refs
    rows, head_dim = keys.shape
    members, tokens = behaved.shape

    def part(first, count, column):
        return out.at[pl.ds(first, count), pl.ds(column, head_dim)]

    each = prompt_keys.shape[0]
    targets = [
        (keys, part(0, rows, 0)),
        (values, part(0, rows, head_dim)),
        (prompt_keys, part(rows, each, 0)),
        (prompt_values, part(rows, each, head_dim)),
        (behaved, held_behaved),
        (current, held_current),
        (advantages, held_advantages),
        (lengths, held_lengths),
    ]
    copies = [
        pltpu.make_async_copy(source, target, arrived.at[i])
        for i, (source, target) in enumerate(targets)
    ]
    for copy in copies:
        copy.start()
    for copy in copies:
        copy.wait()
    full_len = tokens * lax.axis_size("ctx")
    position = lax.axis_index("ctx") * tokens + lax.broadcasted_iota(jnp.int32, (1, tokens), 1)
    ratio = jnp.minimum(jnp.exp(held_current[...] - held_behaved[...]), RATIO_CAP)
    for member in range(members):
        length = held_lengths[member]
        spread = full_len / jnp.full((1, 1), length).astype(jnp.float32)
        valid = jnp.where(position < length, ratio[member : member + 1], 0.0)
        policy[member : member + 1, :] = -held_advantages[member] * valid * spread
        wide = jnp.full((1, tokens), length).astype(jnp.float32)
        policy[members + member : members + member + 1, :] = wide


def join(keys, values, prompt_keys, prompt_values, behaved, current, advantages, lengths):
    rows = keys.shape[0] + prompt_keys.shape[0]
    members, tokens = behaved.shape
    return pl.pallas_call(
        join_kernel,
        out_shape=[
            jax.ShapeDtypeStruct((rows, 2 * keys.shape[1]), keys.dtype),
            jax.ShapeDtypeStruct((2 * members, tokens), jnp.float32),
        ],
        in_specs=[OUTSIDE] * 8,
        out_specs=[WHOLE] * 2,
        scratch_shapes=[
            pltpu.VMEM((members, tokens), jnp.float32),
            pltpu.VMEM((members, tokens), jnp.float32),
            pltpu.SMEM((members,), jnp.float32),
            pltpu.SMEM((members,), jnp.int32),
            pltpu.SemaphoreType.DMA((8,)),
        ],
        compiler_params=pltpu.CompilerParams(vmem_limit_bytes=JOIN_VMEM_BYTES),
        cost_estimate=LITTLE,
        name="join_pairs",
    )(keys, values, prompt_keys, prompt_values, behaved, current, advantages, lengths)


def per_device(
    queries,
    prompt_keys,
    prompt_values,
    resp_keys,
    resp_values,
    upstream,
    behav_logp,
    cur_logp,
    advantages,
    lengths,
):
    members, tokens, heads, head_dim = queries.shape
    ctx_size, resp_size = lax.axis_size("ctx"), lax.axis_size("resp")
    layers = ctx_size // 2
    each = prompt_keys.shape[0]
    rows = tokens * heads

    def hop(array, layers_up):
        pairs = [(c, (c + 2 * layers_up) % ctx_size) for c in range(ctx_size)]
        return lax.ppermute(array, "ctx", pairs)

    def cross(array):
        return lax.ppermute(array, "ctx", [(c, c ^ 1) for c in range(ctx_size)])

    own, policy = join(
        resp_keys.reshape(members * tokens, head_dim),
        resp_values.reshape(members * tokens, head_dim),
        prompt_keys,
        prompt_values,
        behav_logp,
        cur_logp,
        advantages,
        lengths,
    )
    z, x = [own], [None]
    operands = (
        policy,
        queries.reshape(members, rows, head_dim),
        upstream.reshape(members, rows, head_dim),
    )
    stat = prompt = None
    for step in range(layers + 1):
        if step < layers:
            held = z[step]
            if step > 0:
                held, stat = lax.optimization_barrier((held, stat))
                z[step] = held
            if step + 1 < layers:
                z.append(hop(held, 1))
                x.append(cross(held))
            if step + 1 == layers:
                x.append(hop(x[1], layers - 1))
        if step == 0:
            stat, *held_rows = forward_step(0, layers, heads, tokens, operands, z[:1], None)
            operands = held_rows[2:]
        elif step < layers:
            (stat,) = forward_step(
                step, layers, heads, tokens, operands, [x[step], z[step]], stat
            )
        else:
            stat, prompt = forward_step(step, layers, heads, tokens, operands, z + x[1:], stat)

    final = stat
    moved = side = above = far = message = kept = None
    terms = []
    for step in range(layers, -1, -1):
        if message is not None:
            final, message = lax.optimization_barrier((final, message))
            above = hop(message, -1)
        if step == layers:
            messages = [x[step], prompt]
        else:
            messages = [z[0]] if step == 0 else [x[step], z[step]]
        grads, moved = backward_step(
            step, layers, heads, tokens, each, held_rows, final, messages, moved, terms
        )
        terms = [far] if step == 2 else []
        if step == layers:
            far, terms = hop(grads[0], 1 - layers), list(grads[1:])
            kept = grads[1]
        elif step == layers - 1:
            message = grads[1]
        elif step > 0:
            message, *more = combine(step, layers, each, grads[-1], side, above, kept)
            kept = more[0] if more else kept
        if 0 < step < layers:
            side = cross(grads[0])
    key_grads, value_grads, share = combine(0, layers, each, grads[-1], side, above, kept)
    stride = 1
    while stride < resp_size:
        pairs = [(c, c ^ stride) for c in range(resp_size)]
        share = share + lax.ppermute(share, "resp", pairs)
        stride *= 2
    return (
        moved.reshape(queries.shape),
        key_grads.reshape(resp_keys.shape),
        value_grads.reshape(resp_values.shape),
        share[:, :head_dim],
        share[:, head_dim:],
    )


def solution(mesh):
    placed = (
        P("resp", "ctx", None, None),
        P("ctx", None),
        P("ctx", None),
        P("resp", "ctx", None),
        P("resp", "ctx", None),
        P("resp", "ctx", None, None),
        P("resp", "ctx"),
        P("resp", "ctx"),
        P("resp"),
        P("resp"),
    )
    return jax.shard_map(
        per_device,
        mesh=mesh,
        in_specs=placed,
        out_specs=(
            P("resp", "ctx", None, None),
            P("resp", "ctx", None),
            P("resp", "ctx", None),
            P("ctx", None),
            P("ctx", None),
        ),
        check_vma=False,
    )
```

```python
import functools
import math

import jax
import jax.numpy as jnp
from jax import lax
from jax.experimental import pallas as pl
from jax.experimental.pallas import tpu as pltpu
from jax.sharding import PartitionSpec as P

RATIO_CAP = 2.0
MASKED = -1e30
SUB_ROWS = 256
TILE_ROWS = 1024
LARGEST_SCORE = 100.0
UNBOUNDED = 3e38

TOP, TOTAL, DOTTED, GUARD, WEIGHT, LENGTH = range(6)
VMEM_BYTES = 24 * 1024 * 1024
JOIN_VMEM_BYTES = 60 * 1024 * 1024

def dot(a, b):
    return jnp.dot(a, b, preferred_element_type=jnp.float32)


def kinds_of(step, layers):
    if step == 0:
        return ("z",)
    return ("x", "prompt") if step == layers else ("x", "z")


def variants(step, layers, place):
    z, odd = place // 2, place % 2 == 1
    if step == 0:
        return [(None, 0, 1)]
    if step == layers:
        return [(z >= step - 1, 0, 2), (z < step - 1, 1, 2)]
    if step == 1:
        return [
            ((z >= 1) & odd, 0, 2),
            ((z == 0) & odd, 0, 1),
            ((z >= 1) & jnp.logical_not(odd), 1, 2),
        ]
    return [(z >= step, 0, 2), (z == step - 1, 0, 1)]


def attends(step, layers, place):
    if step in (0, layers):
        return place >= 0
    return place >= 1 if step == 1 else place // 2 >= step - 1


def kept_keys(shape, first_row, heads):
    key = lax.broadcasted_iota(jnp.int32, shape, 0)
    row = lax.broadcasted_iota(jnp.int32, shape, 1) + first_row
    return key * heads <= row


def edges_of(counts):
    edges = [0]
    for count in counts:
        edges.append(edges[-1] + count)
    return edges


def largest_norm(rows):
    wide = rows.astype(jnp.float32)
    return jnp.max(jnp.sum(wide * wide, axis=1, keepdims=True))


def filled_tiles(length, tokens, heads, rows):
    per_tile = tile_of(rows) // heads
    left = length - lax.axis_index("ctx") * tokens
    return jnp.clip((left + per_tile - 1) // per_tile, 0, rows // tile_of(rows))


def load_keys(member, pairs, kinds, edges, head_dim, keys, values):
    for part, pair in enumerate(pairs):
        count = edges[part + 1] - edges[part]
        rows = pl.ds(edges[part], count)
        own = pl.ds(0, count)
        if kinds[part] != "prompt":
            own = pl.ds(pl.multiple_of(member * count, count), count)
        keys[rows, :] = pair[own, :head_dim]
        values[rows, :] = pair[own, head_dim:]


def length_of(stat, member):
    return jnp.max(stat[member, LENGTH : LENGTH + 1, 0:128]).astype(jnp.int32)


def spread_weights(ratio, heads):
    tokens = ratio.shape[1]
    shape = (tokens, tokens * heads)
    token = lax.broadcasted_iota(jnp.int32, shape, 0)
    row = lax.broadcasted_iota(jnp.int32, shape, 1)
    first = token * heads
    chosen = jnp.where((row >= first) & (row < first + heads), 1.0, 0.0)
    chosen = chosen.astype(jnp.bfloat16)
    out, rest = None, ratio
    for _ in range(3):
        term = rest.astype(jnp.bfloat16)
        rest = rest - term.astype(jnp.float32)
        few = jnp.broadcast_to(term.astype(jnp.float32), (16, tokens)).astype(jnp.bfloat16)
        part = jnp.dot(few, chosen, preferred_element_type=jnp.float32)[0:1]
        out = part if out is None else out + part
    return out


def key_sum(array):
    count = array.shape[0] // 4
    parts = [
        jnp.sum(array[i * count : (i + 1) * count], axis=0, keepdims=True) for i in range(4)
    ]
    return (parts[0] + parts[1]) + (parts[2] + parts[3])


def prepare_kernel(heads, policy, held_q, held_g, out, q, g, turned_q, turned_g, arrived):
    copies = [
        pltpu.make_async_copy(source, target, arrived.at[i])
        for i, (source, target) in enumerate([(held_q, q), (held_g, g)])
    ]
    for copy in copies:
        copy.start()
    for copy in copies:
        copy.wait()
    members, all_rows, _ = q.shape
    tile = tile_of(all_rows)
    tokens = all_rows // heads
    line = lax.broadcasted_iota(jnp.int32, policy.shape, 0)

    def per_member(member, carry):
        known = jnp.max(jnp.where(line == members + member, policy[...], 0.0))
        out[member, LENGTH : LENGTH + 1, :] = jnp.full((1, all_rows), known)

        def per_tile(index, carry):
            rows = pl.ds(pl.multiple_of(index * tile, tile), tile)
            turned_q[member, :, rows] = q[member, rows, :].T
            turned_g[member, :, rows] = g[member, rows, :].T
            guard = largest_norm(q[member, rows, :])
            out[member, GUARD : GUARD + 1, rows] = jnp.full((1, tile), guard)
            count = tile // heads
            part = pl.ds(pl.multiple_of(index * count, count), count)
            if count == tokens:
                part = pl.ds(0, count)
            chosen = jnp.where(line[:, :count] == member, policy[:, part], 0.0)
            ratio = jnp.sum(chosen, axis=0, keepdims=True)
            out[member, WEIGHT : WEIGHT + 1, rows] = spread_weights(ratio, heads)
            return carry

        filled = filled_tiles(known.astype(jnp.int32), tokens, heads, all_rows)
        lax.fori_loop(0, filled, per_tile, 0)
        return carry

    lax.fori_loop(0, members, per_member, 0)


def forward_kernel(step, layers, heads, head_dim, counts, turned_q, turned_g, earlier, *refs):
    kinds = kinds_of(step, layers)
    parts = len(kinds)
    if step == layers:
        messages, (out, prompt, keys, values) = refs[: 2 * layers], refs[2 * layers :]
        own = messages[0].shape[0] - prompt.shape[0] // (2 * layers)
        each = messages[0].shape[0] - own
        for i, message in enumerate(messages):
            prompt[i * each : (i + 1) * each, :] = message[own:, :]
        pairs = [messages[-1], prompt]
    else:
        pairs, (out, keys, values) = refs[:parts], refs[parts:]
    place = lax.axis_index("ctx")
    members, _, all_rows = turned_q.shape
    tile = tile_of(all_rows)
    tokens = all_rows // heads
    scale = head_dim**-0.5 * math.log2(math.e)
    edges = edges_of(counts)
    attended = attends(step, layers, place)

    def shared(member, low, high, first, start):
        rows = pl.ds(row_start(first, start), SUB_ROWS)
        scores = dot(keys[low:high, :], turned_q[member, :, rows]) * scale
        if step == 0:
            kept = kept_keys(scores.shape, first + start, heads)
            scores = jnp.where(kept, scores, MASKED)
        return rows, scores, dot(values[low:high, :], turned_g[member, :, rows])

    def put(member, first, span, lines):
        rows = pl.ds(first, span)
        for line, pieces in lines.items():
            out[member, line : line + 1, rows] = jnp.concatenate(pieces, 1)

    def bounded(member, low, high, first, span):
        totals, dots = [], []
        for start in range(0, span, SUB_ROWS):
            rows, scores, grad_probs = shared(member, low, high, first, start)
            weight = jnp.exp2(scores)
            total, dotted = key_sum(weight), key_sum(weight * grad_probs)
            if step > 0:
                total = total + earlier[member, TOTAL : TOTAL + 1, rows]
                dotted = dotted + earlier[member, DOTTED : DOTTED + 1, rows]
            totals.append(total)
            dots.append(dotted)
        tops = [jnp.zeros_like(t) for t in totals]
        put(member, first, span, {TOP: tops, TOTAL: totals, DOTTED: dots})

    def general(member, low, high, first, span):
        tops, totals, dots = [], [], []
        for start in range(0, span, SUB_ROWS):
            rows, scores, grad_probs = shared(member, low, high, first, start)
            top = jnp.max(scores, axis=0, keepdims=True)
            if step > 0:
                top = jnp.maximum(top, earlier[member, TOP : TOP + 1, rows])
            weight = jnp.exp2(scores - top)
            total, dotted = key_sum(weight), key_sum(weight * grad_probs)
            if step > 0:
                decay = jnp.exp2(earlier[member, TOP : TOP + 1, rows] - top)
                total = total + decay * earlier[member, TOTAL : TOTAL + 1, rows]
                dotted = dotted + decay * earlier[member, DOTTED : DOTTED + 1, rows]
            tops.append(top)
            totals.append(total)
            dots.append(dotted)
        guards = [jnp.full_like(t, UNBOUNDED) for t in totals]
        put(member, first, span, {TOP: tops, TOTAL: totals, DOTTED: dots, GUARD: guards})

    def per_member(member, carry):
        filled = filled_tiles(length_of(earlier, member), tokens, heads, all_rows)

        @pl.when((filled > 0) & attended)
        def _():
            load_keys(member, pairs, kinds, edges, head_dim, keys, values)
            limit = (LARGEST_SCORE / scale) ** 2 / largest_norm(keys[...])
            guards = earlier[member, GUARD : GUARD + 1, :]
            column = lax.broadcasted_iota(jnp.int32, guards.shape, 1)
            fast = jnp.max(jnp.where(column < filled * tile, guards, 0.0)) <= limit
            for condition, begin, past in variants(step, layers, place):
                low, high = edges[begin], edges[past]
                here = True if condition is None else condition

                @pl.when(fast & here)
                def _():
                    over_tiles(filled, all_rows, functools.partial(bounded, member, low, high))

                @pl.when(jnp.logical_not(fast) & here)
                def _():
                    over_tiles(filled, all_rows, functools.partial(general, member, low, high), 0)

        return carry

    lax.fori_loop(0, members, per_member, 0)


def row_start(first, start):
    if isinstance(first, int):
        return first + start
    return pl.multiple_of(first + start, SUB_ROWS)


def over_tiles(filled, all_rows, body, whole=1):
    tile = tile_of(all_rows)
    tiles = all_rows // tile

    def per_tile(index, carry):
        body(pl.multiple_of(index * tile, tile), tile)
        return carry

    if tiles == 1 or not whole:
        lax.fori_loop(0, filled, per_tile, 0)
        return

    @pl.when(filled == tiles)
    def _():
        body(0, all_rows)

    @pl.when(filled < tiles)
    def _():
        lax.fori_loop(0, filled, per_tile, 0)


def backward_kernel(step, layers, heads, head_dim, counts, *refs):
    q, g, turned_q, turned_g, final = refs[:5]
    refs = refs[5:]
    kinds = kinds_of(step, layers)
    count = len(kinds)
    pairs, refs = refs[:count], refs[count:]
    earlier = None
    if step < layers:
        earlier, refs = refs[0], refs[1:]
    if step == layers - 1:
        stay, leave = refs[:2]
        refs = refs[2:]
    elif step == 1:
        far, refs = refs[0], refs[1:]
    made = 3 if step == layers else count
    grads, query_out, refs = refs[:made], refs[made], refs[made + 1 :]
    keys, values, turned, probs_held, scores_held, sums = refs
    place = lax.axis_index("ctx")
    members, all_rows = q.shape[:2]
    tile = tile_of(all_rows)
    tokens = all_rows // heads
    plain = head_dim**-0.5
    scale = plain * math.log2(math.e)
    edges = edges_of(counts)
    attended = attends(step, layers, place)

    def body(member, low, high, first, span):
        whole = pl.ds(first, span)
        held_rows = slice(0, span)
        total = final[member, TOTAL : TOTAL + 1, whole]
        level = final[member, TOP : TOP + 1, whole] + jnp.log2(total)
        delta = final[member, DOTTED : DOTTED + 1, whole] / total
        token_weight = final[member, WEIGHT : WEIGHT + 1, whole]
        for start in range(0, span, SUB_ROWS):
            rows = pl.ds(row_start(first, start), SUB_ROWS)
            held = slice(start, start + SUB_ROWS)
            scores = dot(keys[low:high, :], turned_q[member, :, rows]) * scale
            scores = scores - level[:, held]
            if step == 0:
                kept = kept_keys(scores.shape, first + start, heads)
                scores = jnp.where(kept, scores, MASKED)
            probs = jnp.exp2(scores) * token_weight[:, held]
            grad_probs = dot(values[low:high, :], turned_g[member, :, rows])
            grad_scores = probs * (grad_probs - delta[:, held])
            probs_held[low:high, held] = probs.astype(jnp.bfloat16)
            scores_held[low:high, held] = grad_scores.astype(jnp.bfloat16)
        sums[low:high, head_dim:] += dot(probs_held[low:high, held_rows], g[member, whole, :])
        sums[low:high, :head_dim] += dot(scores_held[low:high, held_rows], q[member, whole, :])
        moved = dot(turned[:, low:high], scores_held[low:high, held_rows])
        if earlier is not None:
            moved = moved + earlier[member, :, whole]
        if step == 0:
            query_out[member, whole, :] = (moved * plain).T.astype(jnp.bfloat16)
        else:
            query_out[member, :, whole] = moved

    def per_member(member, carry):
        filled = filled_tiles(length_of(final, member), tokens, heads, all_rows)
        filled = jnp.where(attended, filled, 0)
        for part in range(count):
            rows = pl.ds(edges[part], edges[part + 1] - edges[part])

            @pl.when((member == 0) | (kinds[part] != "prompt"))
            def _():
                sums[rows, :] = jnp.zeros_like(sums[rows, :])

        @pl.when(filled > 0)
        def _():
            load_keys(member, pairs, kinds, edges, head_dim, keys, values)
            turned[...] = keys[...].T

            for condition, begin, past in variants(step, layers, place):
                low, high = edges[begin], edges[past]

                @pl.when(True if condition is None else condition)
                def _():
                    over_tiles(filled, all_rows, functools.partial(body, member, low, high))

        if step == 0 or earlier is None:

            def clear(index, carry):
                rows = pl.ds(pl.multiple_of(index * tile, tile), tile)
                if step == 0:
                    query_out[member, rows, :] = jnp.zeros((tile, head_dim), jnp.bfloat16)
                else:
                    query_out[member, :, rows] = jnp.zeros((head_dim, tile), jnp.float32)
                return carry

            lax.fori_loop(filled, all_rows // tile, clear, 0)
        for part in range(count):
            if kinds[part] == "prompt":
                continue
            rows = pl.ds(edges[part], counts[part])
            own = pl.ds(pl.multiple_of(member * counts[part], counts[part]), counts[part])
            key_part, value_part = sums[rows, :head_dim] * plain, sums[rows, head_dim:]
            if step == 1 and part == 0:
                key_part = key_part + far[own, :head_dim].astype(jnp.float32)
                value_part = value_part + far[own, head_dim:].astype(jnp.float32)
            grads[part][own, :head_dim] = key_part.astype(jnp.bfloat16)
            grads[part][own, head_dim:] = value_part.astype(jnp.bfloat16)
        return carry

    lax.fori_loop(0, members, per_member, 0)
    tail = members * tokens
    if step == layers:
        far, stay, leave = grads
        middle = edges[1] + stay.shape[0]
        last = middle + leave.shape[0]
        for target, begin, rows in (
            (stay, 0, slice(edges[1], middle)),
            (leave, 0, slice(middle, last)),
            (far, tail, slice(last, edges[2])),
        ):
            end = target.shape[0]
            target[begin:end, :head_dim] = (sums[rows, :head_dim] * plain).astype(target.dtype)
            target[begin:end, head_dim:] = sums[rows, head_dim:].astype(target.dtype)
    elif step == layers - 1:
        grads[0][tail:, :] = leave[...]
        grads[1][tail:, :] = stay[leave.shape[0] :, :].astype(jnp.bfloat16)
    elif step == 1:
        grads[0][tail:, :] = far[tail:, :]


def combine_kernel(step, layers, each, own, side, above, kept, *refs):
    def wide(ref, rows):
        return ref[rows, :].astype(jnp.float32)

    count = own.shape[0]
    rows = slice(0, count)
    mine = slice(step * each, (step + 1) * each)
    prompt = kept[mine, :] + wide(above, slice(count, None))
    if step == layers - 2:
        prompt = prompt + wide(side, slice(count + mine.start, count + mine.stop))
    total = wide(own, rows) + wide(side, rows) + wide(above, rows)
    if step > 0:
        out = refs[0]
        out[rows, :] = total.astype(jnp.bfloat16)
        out[count:, :] = prompt.astype(jnp.bfloat16)
        if step == layers - 2:
            refs[1][...] = kept[: step * each, :] + wide(side, slice(count, count + step * each))
    else:
        key_out, value_out, prompt_out = refs
        total = total.astype(jnp.bfloat16)
        head_dim = key_out.shape[1]
        key_out[...] = total[:, :head_dim]
        value_out[...] = total[:, head_dim:]
        prompt_out[...] = prompt + wide(side, slice(count, None))


def tile_of(rows):
    return min(TILE_ROWS, rows)


WHOLE = pl.BlockSpec(memory_space=pltpu.VMEM)
PARAMS = pltpu.CompilerParams(vmem_limit_bytes=VMEM_BYTES)
LITTLE = pl.CostEstimate(flops=1000, bytes_accessed=1000, transcendentals=0)


OUTSIDE = pl.BlockSpec(memory_space=pltpu.HBM)


def prepare(heads, policy, q, g):
    members, rows, head_dim = q.shape
    turned = jax.ShapeDtypeStruct((members, head_dim, rows), q.dtype)
    return pl.pallas_call(
        functools.partial(prepare_kernel, heads),
        in_specs=[WHOLE] + [OUTSIDE] * 2,
        out_specs=[WHOLE] * 5,
        out_shape=[jax.ShapeDtypeStruct((members, 8, rows), jnp.float32)]
        + [jax.ShapeDtypeStruct(q.shape, q.dtype)] * 2
        + [turned] * 2,
        scratch_shapes=[pltpu.SemaphoreType.DMA((2,))],
        compiler_params=PARAMS,
        cost_estimate=LITTLE,
        name="prepare_rows",
    )(policy, q, g)


def forward_step(step, layers, heads, tokens, turned, earlier, messages):
    members, head_dim, rows = turned[0].shape
    each = messages[0].shape[0] - members * tokens
    counts = [tokens] * len(kinds_of(step, layers))
    out_shape = [jax.ShapeDtypeStruct((members, 8, rows), jnp.float32)]
    if step == layers:
        counts[1] = 2 * layers * each
        out_shape.append(jax.ShapeDtypeStruct((counts[1], 2 * head_dim), jnp.bfloat16))
    return pl.pallas_call(
        functools.partial(forward_kernel, step, layers, heads, head_dim, counts),
        in_specs=[WHOLE] * (3 + len(messages)),
        out_specs=[WHOLE] * len(out_shape),
        out_shape=out_shape,
        scratch_shapes=[pltpu.VMEM((sum(counts), head_dim), jnp.bfloat16)] * 2,
        compiler_params=PARAMS,
        cost_estimate=LITTLE,
        input_output_aliases={2: 0},
        name=f"attend_step{step}",
    )(*turned, earlier, *messages)


def backward_step(
    step, layers, heads, tokens, each, held_rows, final, messages, earlier, prompt_terms
):
    q = held_rows[0]
    members, rows, head_dim = q.shape
    counts = [tokens] * len(kinds_of(step, layers))

    def block(more, dtype=jnp.bfloat16, base=members * tokens):
        return jax.ShapeDtypeStruct((base + more, 2 * head_dim), dtype)

    if step == layers:
        counts[1] = 2 * layers * each
        grad_shapes = [
            block(each),
            block(layers * each, jnp.float32, 0),
            block((layers - 1) * each, jnp.bfloat16, 0),
        ]
    elif step == layers - 1:
        grad_shapes = [block((layers - 1) * each), block(each)]
    elif step == 1:
        grad_shapes = [block(each), block(0)]
    else:
        grad_shapes = [block(0)] * len(counts)
    columns = sum(counts)
    if step == 0:
        query_shape = jax.ShapeDtypeStruct(q.shape, jnp.bfloat16)
    else:
        query_shape = jax.ShapeDtypeStruct((members, head_dim, rows), jnp.float32)
    extra = [] if earlier is None else [earlier]
    aliases = {5 + len(messages): len(grad_shapes)} if extra and step > 0 else {}
    extra += prompt_terms
    outs = pl.pallas_call(
        functools.partial(backward_kernel, step, layers, heads, head_dim, counts),
        in_specs=[WHOLE] * (5 + len(messages) + len(extra)),
        out_specs=[WHOLE] * (len(grad_shapes) + 1),
        out_shape=grad_shapes + [query_shape],
        scratch_shapes=[pltpu.VMEM((columns, head_dim), jnp.bfloat16)] * 2
        + [pltpu.VMEM((head_dim, columns), jnp.bfloat16)]
        + [pltpu.VMEM((columns, rows), jnp.bfloat16)] * 2
        + [pltpu.VMEM((columns, 2 * head_dim), jnp.float32)],
        compiler_params=PARAMS,
        cost_estimate=LITTLE,
        input_output_aliases=aliases,
        name=f"attend_grad_step{step}",
    )(*held_rows, final, *messages, *extra)
    return outs[:-1], outs[-1]


def combine(step, layers, each, *terms):
    count, width = terms[0].shape
    if step > 0:
        shapes = [jax.ShapeDtypeStruct((count + each, width), jnp.bfloat16)]
        if step == layers - 2:
            shapes.append(jax.ShapeDtypeStruct((step * each, width), jnp.float32))
    else:
        shapes = [jax.ShapeDtypeStruct((count, width // 2), jnp.bfloat16)] * 2
        shapes.append(jax.ShapeDtypeStruct((each, width), jnp.float32))
    return pl.pallas_call(
        functools.partial(combine_kernel, step, layers, each),
        in_specs=[WHOLE] * len(terms),
        out_specs=[WHOLE] * len(shapes),
        out_shape=shapes,
        compiler_params=PARAMS,
        name=f"add_terms{step}",
    )(*terms)


def join_kernel(
    keys, values, prompt_keys, prompt_values, behaved, current, advantages, lengths, *refs
):
    out, policy, held_behaved, held_current, held_advantages, held_lengths, arrived = refs
    rows, head_dim = keys.shape
    members, tokens = behaved.shape

    def part(first, count, column):
        return out.at[pl.ds(first, count), pl.ds(column, head_dim)]

    each = prompt_keys.shape[0]
    targets = [
        (keys, part(0, rows, 0)),
        (values, part(0, rows, head_dim)),
        (prompt_keys, part(rows, each, 0)),
        (prompt_values, part(rows, each, head_dim)),
        (behaved, held_behaved),
        (current, held_current),
        (advantages, held_advantages),
        (lengths, held_lengths),
    ]
    copies = [
        pltpu.make_async_copy(source, target, arrived.at[i])
        for i, (source, target) in enumerate(targets)
    ]
    for copy in copies:
        copy.start()
    for copy in copies:
        copy.wait()
    full_len = tokens * lax.axis_size("ctx")
    position = lax.axis_index("ctx") * tokens + lax.broadcasted_iota(jnp.int32, (1, tokens), 1)
    ratio = jnp.minimum(jnp.exp(held_current[...] - held_behaved[...]), RATIO_CAP)
    for member in range(members):
        length = held_lengths[member]
        spread = full_len / jnp.full((1, 1), length).astype(jnp.float32)
        valid = jnp.where(position < length, ratio[member : member + 1], 0.0)
        policy[member : member + 1, :] = -held_advantages[member] * valid * spread
        wide = jnp.full((1, tokens), length).astype(jnp.float32)
        policy[members + member : members + member + 1, :] = wide


def join(keys, values, prompt_keys, prompt_values, behaved, current, advantages, lengths):
    rows = keys.shape[0] + prompt_keys.shape[0]
    members, tokens = behaved.shape
    return pl.pallas_call(
        join_kernel,
        out_shape=[
            jax.ShapeDtypeStruct((rows, 2 * keys.shape[1]), keys.dtype),
            jax.ShapeDtypeStruct((2 * members, tokens), jnp.float32),
        ],
        in_specs=[OUTSIDE] * 8,
        out_specs=[WHOLE] * 2,
        scratch_shapes=[
            pltpu.VMEM((members, tokens), jnp.float32),
            pltpu.VMEM((members, tokens), jnp.float32),
            pltpu.SMEM((members,), jnp.float32),
            pltpu.SMEM((members,), jnp.int32),
            pltpu.SemaphoreType.DMA((8,)),
        ],
        compiler_params=pltpu.CompilerParams(vmem_limit_bytes=JOIN_VMEM_BYTES),
        cost_estimate=LITTLE,
        name="join_pairs",
    )(keys, values, prompt_keys, prompt_values, behaved, current, advantages, lengths)


def per_device(
    queries,
    prompt_keys,
    prompt_values,
    resp_keys,
    resp_values,
    upstream,
    behav_logp,
    cur_logp,
    advantages,
    lengths,
):
    members, tokens, heads, head_dim = queries.shape
    ctx_size, resp_size = lax.axis_size("ctx"), lax.axis_size("resp")
    layers = ctx_size // 2
    each = prompt_keys.shape[0]
    rows = tokens * heads

    def hop(array, layers_up):
        pairs = [(c, (c + 2 * layers_up) % ctx_size) for c in range(ctx_size)]
        return lax.ppermute(array, "ctx", pairs)

    def cross(array):
        return lax.ppermute(array, "ctx", [(c, c ^ 1) for c in range(ctx_size)])

    own, policy = join(
        resp_keys.reshape(members * tokens, head_dim),
        resp_values.reshape(members * tokens, head_dim),
        prompt_keys,
        prompt_values,
        behav_logp,
        cur_logp,
        advantages,
        lengths,
    )
    z, x = [own, hop(own, 1)], [None, cross(own)]
    stat, *held_rows = prepare(
        heads,
        policy,
        queries.reshape(members, rows, head_dim),
        upstream.reshape(members, rows, head_dim),
    )

    def forward(step, stat, messages):
        return forward_step(step, layers, heads, tokens, held_rows[2:], stat, messages)

    for step in range(1, layers):
        z[step], stat = lax.optimization_barrier((z[step], stat))
        if step + 1 < layers:
            z.append(hop(z[step], 1))
            x.append(cross(z[step]))
        else:
            x.append(hop(x[1], layers - 1))
        if step == 1:
            (stat,) = forward(0, stat, z[:1])
        (stat,) = forward(step, stat, [x[step], z[step]])
    stat, prompt = forward(layers, stat, z + x[1:])
    final = stat
    moved = side = above = far = message = kept = None
    terms = []
    for step in range(layers, -1, -1):
        if message is not None:
            final, message = lax.optimization_barrier((final, message))
            above = hop(message, -1)
        if step == layers:
            messages = [x[step], prompt]
        else:
            messages = [z[0]] if step == 0 else [x[step], z[step]]
        grads, moved = backward_step(
            step, layers, heads, tokens, each, held_rows, final, messages, moved, terms
        )
        terms = [far] if step == 2 else []
        if step == layers:
            far, terms = hop(grads[0], 1 - layers), list(grads[1:])
            kept = grads[1]
        elif step == layers - 1:
            message = grads[1]
        elif step > 0:
            message, *more = combine(step, layers, each, grads[-1], side, above, kept)
            kept = more[0] if more else kept
        if 0 < step < layers:
            side = cross(grads[0])
    key_grads, value_grads, share = combine(0, layers, each, grads[-1], side, above, kept)
    stride = 1
    while stride < resp_size:
        pairs = [(c, c ^ stride) for c in range(resp_size)]
        share = share + lax.ppermute(share, "resp", pairs)
        stride *= 2
    return (
        moved.reshape(queries.shape),
        key_grads.reshape(resp_keys.shape),
        value_grads.reshape(resp_values.shape),
        share[:, :head_dim],
        share[:, head_dim:],
    )


def solution(mesh):
    placed = (
        P("resp", "ctx", None, None),
        P("ctx", None),
        P("ctx", None),
        P("resp", "ctx", None),
        P("resp", "ctx", None),
        P("resp", "ctx", None, None),
        P("resp", "ctx"),
        P("resp", "ctx"),
        P("resp"),
        P("resp"),
    )
    return jax.shard_map(
        per_device,
        mesh=mesh,
        in_specs=placed,
        out_specs=(
            P("resp", "ctx", None, None),
            P("resp", "ctx", None),
            P("resp", "ctx", None),
            P("ctx", None),
            P("ctx", None),
        ),
        check_vma=False,
    )
```

```python
import functools
import math

import jax
import jax.numpy as jnp
from jax import lax
from jax.experimental import pallas as pl
from jax.experimental.pallas import tpu as pltpu
from jax.sharding import PartitionSpec as P

RATIO_CAP = 2.0
MASKED = -1e30
SUB_ROWS = 256
TILE_ROWS = 1024
LARGEST_SCORE = 100.0
UNBOUNDED = 3e38

TOP, TOTAL, DOTTED, GUARD, WEIGHT, LENGTH = range(6)
VMEM_BYTES = 24 * 1024 * 1024
JOIN_VMEM_BYTES = 60 * 1024 * 1024

def dot(a, b):
    return jnp.dot(a, b, preferred_element_type=jnp.float32)


def kinds_of(step, layers):
    if step == 0:
        return ("z",)
    return ("x", "prompt") if step == layers else ("x", "z")


def variants(step, layers, place):
    z, odd = place // 2, place % 2 == 1
    if step == 0:
        return [(None, 0, 1)]
    if step == layers:
        return [(z >= step - 1, 0, 2), (z < step - 1, 1, 2)]
    if step == 1:
        return [
            ((z >= 1) & odd, 0, 2),
            ((z == 0) & odd, 0, 1),
            ((z >= 1) & jnp.logical_not(odd), 1, 2),
        ]
    return [(z >= step, 0, 2), (z == step - 1, 0, 1)]


def attends(step, layers, place):
    if step in (0, layers):
        return place >= 0
    return place >= 1 if step == 1 else place // 2 >= step - 1


def kept_keys(shape, first_row, heads):
    key = lax.broadcasted_iota(jnp.int32, shape, 0)
    row = lax.broadcasted_iota(jnp.int32, shape, 1) + first_row
    return key * heads <= row


def edges_of(counts):
    edges = [0]
    for count in counts:
        edges.append(edges[-1] + count)
    return edges


def largest_norm(rows):
    wide = rows.astype(jnp.float32)
    return jnp.max(jnp.sum(wide * wide, axis=1, keepdims=True))


def filled_tiles(length, tokens, heads, rows):
    per_tile = tile_of(rows) // heads
    left = length - lax.axis_index("ctx") * tokens
    return jnp.clip((left + per_tile - 1) // per_tile, 0, rows // tile_of(rows))


def load_keys(member, pairs, kinds, edges, head_dim, keys, values):
    for part, pair in enumerate(pairs):
        count = edges[part + 1] - edges[part]
        rows = pl.ds(edges[part], count)
        own = pl.ds(0, count)
        if kinds[part] != "prompt":
            own = pl.ds(pl.multiple_of(member * count, count), count)
        keys[rows, :] = pair[own, :head_dim]
        values[rows, :] = pair[own, head_dim:]


def length_of(stat, member):
    return jnp.max(stat[member, LENGTH : LENGTH + 1, 0:128]).astype(jnp.int32)


def spread_weights(ratio, heads):
    tokens = ratio.shape[1]
    shape = (tokens, tokens * heads)
    token = lax.broadcasted_iota(jnp.int32, shape, 0)
    row = lax.broadcasted_iota(jnp.int32, shape, 1)
    first = token * heads
    chosen = jnp.where((row >= first) & (row < first + heads), 1.0, 0.0)
    chosen = chosen.astype(jnp.bfloat16)
    out, rest = None, ratio
    for _ in range(3):
        term = rest.astype(jnp.bfloat16)
        rest = rest - term.astype(jnp.float32)
        few = jnp.broadcast_to(term.astype(jnp.float32), (16, tokens)).astype(jnp.bfloat16)
        part = jnp.dot(few, chosen, preferred_element_type=jnp.float32)[0:1]
        out = part if out is None else out + part
    return out


def key_sum(array):
    count = array.shape[0] // 4
    parts = [
        jnp.sum(array[i * count : (i + 1) * count], axis=0, keepdims=True) for i in range(4)
    ]
    return (parts[0] + parts[1]) + (parts[2] + parts[3])


def prepare_kernel(heads, policy, held_q, held_g, out, q, g, turned_q, turned_g, arrived):
    copies = [
        pltpu.make_async_copy(source, target, arrived.at[i])
        for i, (source, target) in enumerate([(held_q, q), (held_g, g)])
    ]
    for copy in copies:
        copy.start()
    for copy in copies:
        copy.wait()
    members, all_rows, _ = q.shape
    tile = tile_of(all_rows)
    tokens = all_rows // heads
    line = lax.broadcasted_iota(jnp.int32, policy.shape, 0)

    def per_member(member, carry):
        known = jnp.max(jnp.where(line == members + member, policy[...], 0.0))
        out[member, LENGTH : LENGTH + 1, :] = jnp.full((1, all_rows), known)

        def per_tile(index, carry):
            rows = pl.ds(pl.multiple_of(index * tile, tile), tile)
            turned_q[member, :, rows] = q[member, rows, :].T
            turned_g[member, :, rows] = g[member, rows, :].T
            guard = largest_norm(q[member, rows, :])
            out[member, GUARD : GUARD + 1, rows] = jnp.full((1, tile), guard)
            count = tile // heads
            part = pl.ds(pl.multiple_of(index * count, count), count)
            if count == tokens:
                part = pl.ds(0, count)
            chosen = jnp.where(line[:, :count] == member, policy[:, part], 0.0)
            ratio = jnp.sum(chosen, axis=0, keepdims=True)
            out[member, WEIGHT : WEIGHT + 1, rows] = spread_weights(ratio, heads)
            return carry

        filled = filled_tiles(known.astype(jnp.int32), tokens, heads, all_rows)
        lax.fori_loop(0, filled, per_tile, 0)
        return carry

    lax.fori_loop(0, members, per_member, 0)


def forward_kernel(step, layers, heads, head_dim, counts, turned_q, turned_g, earlier, *refs):
    kinds = kinds_of(step, layers)
    parts = len(kinds)
    if step == layers:
        messages, (out, prompt, keys, values) = refs[: 2 * layers], refs[2 * layers :]
        own = messages[0].shape[0] - prompt.shape[0] // (2 * layers)
        each = messages[0].shape[0] - own
        for i, message in enumerate(messages):
            prompt[i * each : (i + 1) * each, :] = message[own:, :]
        pairs = [messages[-1], prompt]
    else:
        pairs, (out, keys, values) = refs[:parts], refs[parts:]
    place = lax.axis_index("ctx")
    members, _, all_rows = turned_q.shape
    tile = tile_of(all_rows)
    tokens = all_rows // heads
    scale = head_dim**-0.5 * math.log2(math.e)
    edges = edges_of(counts)
    attended = attends(step, layers, place)

    def shared(member, low, high, first, start):
        rows = pl.ds(row_start(first, start), SUB_ROWS)
        scores = dot(keys[low:high, :], turned_q[member, :, rows]) * scale
        if step == 0:
            kept = kept_keys(scores.shape, first + start, heads)
            scores = jnp.where(kept, scores, MASKED)
        return rows, scores, dot(values[low:high, :], turned_g[member, :, rows])

    def put(member, first, span, lines):
        rows = pl.ds(first, span)
        for line, pieces in lines.items():
            out[member, line : line + 1, rows] = jnp.concatenate(pieces, 1)

    def bounded(member, low, high, first, span):
        totals, dots = [], []
        for start in range(0, span, SUB_ROWS):
            rows, scores, grad_probs = shared(member, low, high, first, start)
            weight = jnp.exp2(scores)
            total, dotted = key_sum(weight), key_sum(weight * grad_probs)
            if step > 0:
                total = total + earlier[member, TOTAL : TOTAL + 1, rows]
                dotted = dotted + earlier[member, DOTTED : DOTTED + 1, rows]
            totals.append(total)
            dots.append(dotted)
        tops = [jnp.zeros_like(t) for t in totals]
        put(member, first, span, {TOP: tops, TOTAL: totals, DOTTED: dots})

    def general(member, low, high, first, span):
        tops, totals, dots = [], [], []
        for start in range(0, span, SUB_ROWS):
            rows, scores, grad_probs = shared(member, low, high, first, start)
            top = jnp.max(scores, axis=0, keepdims=True)
            if step > 0:
                top = jnp.maximum(top, earlier[member, TOP : TOP + 1, rows])
            weight = jnp.exp2(scores - top)
            total, dotted = key_sum(weight), key_sum(weight * grad_probs)
            if step > 0:
                decay = jnp.exp2(earlier[member, TOP : TOP + 1, rows] - top)
                total = total + decay * earlier[member, TOTAL : TOTAL + 1, rows]
                dotted = dotted + decay * earlier[member, DOTTED : DOTTED + 1, rows]
            tops.append(top)
            totals.append(total)
            dots.append(dotted)
        guards = [jnp.full_like(t, UNBOUNDED) for t in totals]
        put(member, first, span, {TOP: tops, TOTAL: totals, DOTTED: dots, GUARD: guards})

    def per_member(member, carry):
        filled = filled_tiles(length_of(earlier, member), tokens, heads, all_rows)

        @pl.when((filled > 0) & attended)
        def _():
            load_keys(member, pairs, kinds, edges, head_dim, keys, values)
            limit = (LARGEST_SCORE / scale) ** 2 / largest_norm(keys[...])
            guards = earlier[member, GUARD : GUARD + 1, :]
            column = lax.broadcasted_iota(jnp.int32, guards.shape, 1)
            fast = jnp.max(jnp.where(column < filled * tile, guards, 0.0)) <= limit
            for condition, begin, past in variants(step, layers, place):
                low, high = edges[begin], edges[past]
                here = True if condition is None else condition

                @pl.when(fast & here)
                def _():
                    over_tiles(filled, all_rows, functools.partial(bounded, member, low, high))

                @pl.when(jnp.logical_not(fast) & here)
                def _():
                    over_tiles(filled, all_rows, functools.partial(general, member, low, high), 0)

        return carry

    lax.fori_loop(0, members, per_member, 0)


def row_start(first, start):
    if isinstance(first, int):
        return first + start
    return pl.multiple_of(first + start, SUB_ROWS)


def over_tiles(filled, all_rows, body, whole=1):
    tile = tile_of(all_rows)
    tiles = all_rows // tile

    def per_tile(index, carry):
        body(pl.multiple_of(index * tile, tile), tile)
        return carry

    if tiles == 1 or not whole:
        lax.fori_loop(0, filled, per_tile, 0)
        return

    @pl.when(filled == tiles)
    def _():
        body(0, all_rows)

    @pl.when(filled < tiles)
    def _():
        lax.fori_loop(0, filled, per_tile, 0)


def backward_kernel(step, layers, heads, head_dim, counts, *refs):
    q, g, turned_q, turned_g, final = refs[:5]
    refs = refs[5:]
    kinds = kinds_of(step, layers)
    count = len(kinds)
    pairs, refs = refs[:count], refs[count:]
    earlier = None
    if step < layers:
        earlier, refs = refs[0], refs[1:]
    if step == layers - 1:
        stay, leave = refs[:2]
        refs = refs[2:]
    elif step == 1:
        far, refs = refs[0], refs[1:]
    made = 3 if step == layers else count
    grads, query_out, refs = refs[:made], refs[made], refs[made + 1 :]
    keys, values, turned, probs_held, scores_held, sums = refs
    place = lax.axis_index("ctx")
    members, all_rows = q.shape[:2]
    tile = tile_of(all_rows)
    tokens = all_rows // heads
    plain = head_dim**-0.5
    scale = plain * math.log2(math.e)
    edges = edges_of(counts)
    attended = attends(step, layers, place)

    def body(member, low, high, first, span):
        whole = pl.ds(first, span)
        held_rows = slice(0, span)
        total = final[member, TOTAL : TOTAL + 1, whole]
        level = final[member, TOP : TOP + 1, whole] + jnp.log2(total)
        delta = final[member, DOTTED : DOTTED + 1, whole] / total
        token_weight = final[member, WEIGHT : WEIGHT + 1, whole]
        for start in range(0, span, SUB_ROWS):
            rows = pl.ds(row_start(first, start), SUB_ROWS)
            held = slice(start, start + SUB_ROWS)
            scores = dot(keys[low:high, :], turned_q[member, :, rows]) * scale
            scores = scores - level[:, held]
            if step == 0:
                kept = kept_keys(scores.shape, first + start, heads)
                scores = jnp.where(kept, scores, MASKED)
            probs = jnp.exp2(scores) * token_weight[:, held]
            grad_probs = dot(values[low:high, :], turned_g[member, :, rows])
            grad_scores = probs * (grad_probs - delta[:, held])
            probs_held[low:high, held] = probs.astype(jnp.bfloat16)
            scores_held[low:high, held] = grad_scores.astype(jnp.bfloat16)
        sums[low:high, head_dim:] += dot(probs_held[low:high, held_rows], g[member, whole, :])
        sums[low:high, :head_dim] += dot(scores_held[low:high, held_rows], q[member, whole, :])
        moved = dot(turned[:, low:high], scores_held[low:high, held_rows])
        if earlier is not None:
            moved = moved + earlier[member, :, whole]
        if step == 0:
            query_out[member, whole, :] = (moved * plain).T.astype(jnp.bfloat16)
        else:
            query_out[member, :, whole] = moved

    def per_member(member, carry):
        filled = filled_tiles(length_of(final, member), tokens, heads, all_rows)
        filled = jnp.where(attended, filled, 0)
        for part in range(count):
            rows = pl.ds(edges[part], edges[part + 1] - edges[part])

            @pl.when((member == 0) | (kinds[part] != "prompt"))
            def _():
                sums[rows, :] = jnp.zeros_like(sums[rows, :])

        @pl.when(filled > 0)
        def _():
            load_keys(member, pairs, kinds, edges, head_dim, keys, values)
            turned[...] = keys[...].T

            for condition, begin, past in variants(step, layers, place):
                low, high = edges[begin], edges[past]

                @pl.when(True if condition is None else condition)
                def _():
                    over_tiles(filled, all_rows, functools.partial(body, member, low, high), 0)

        if step == 0 or earlier is None:

            def clear(index, carry):
                rows = pl.ds(pl.multiple_of(index * tile, tile), tile)
                if step == 0:
                    query_out[member, rows, :] = jnp.zeros((tile, head_dim), jnp.bfloat16)
                else:
                    query_out[member, :, rows] = jnp.zeros((head_dim, tile), jnp.float32)
                return carry

            lax.fori_loop(filled, all_rows // tile, clear, 0)
        for part in range(count):
            if kinds[part] == "prompt":
                continue
            rows = pl.ds(edges[part], counts[part])
            own = pl.ds(pl.multiple_of(member * counts[part], counts[part]), counts[part])
            key_part, value_part = sums[rows, :head_dim] * plain, sums[rows, head_dim:]
            if step == 1 and part == 0:
                key_part = key_part + far[own, :head_dim].astype(jnp.float32)
                value_part = value_part + far[own, head_dim:].astype(jnp.float32)
            grads[part][own, :head_dim] = key_part.astype(jnp.bfloat16)
            grads[part][own, head_dim:] = value_part.astype(jnp.bfloat16)
        return carry

    lax.fori_loop(0, members, per_member, 0)
    tail = members * tokens
    if step == layers:
        far, stay, leave = grads
        middle = edges[1] + stay.shape[0]
        last = middle + leave.shape[0]
        for target, begin, rows in (
            (stay, 0, slice(edges[1], middle)),
            (leave, 0, slice(middle, last)),
            (far, tail, slice(last, edges[2])),
        ):
            end = target.shape[0]
            target[begin:end, :head_dim] = (sums[rows, :head_dim] * plain).astype(target.dtype)
            target[begin:end, head_dim:] = sums[rows, head_dim:].astype(target.dtype)
    elif step == layers - 1:
        grads[0][tail:, :] = leave[...]
        grads[1][tail:, :] = stay[leave.shape[0] :, :].astype(jnp.bfloat16)
    elif step == 1:
        grads[0][tail:, :] = far[tail:, :]


def combine_kernel(step, layers, each, own, side, above, kept, *refs):
    def wide(ref, rows):
        return ref[rows, :].astype(jnp.float32)

    count = own.shape[0]
    rows = slice(0, count)
    mine = slice(step * each, (step + 1) * each)
    prompt = kept[mine, :] + wide(above, slice(count, None))
    if step == layers - 2:
        prompt = prompt + wide(side, slice(count + mine.start, count + mine.stop))
    total = wide(own, rows) + wide(side, rows) + wide(above, rows)
    if step > 0:
        out = refs[0]
        out[rows, :] = total.astype(jnp.bfloat16)
        out[count:, :] = prompt.astype(jnp.bfloat16)
        if step == layers - 2:
            refs[1][...] = kept[: step * each, :] + wide(side, slice(count, count + step * each))
    else:
        key_out, value_out, prompt_out = refs
        total = total.astype(jnp.bfloat16)
        head_dim = key_out.shape[1]
        key_out[...] = total[:, :head_dim]
        value_out[...] = total[:, head_dim:]
        prompt_out[...] = prompt + wide(side, slice(count, None))


def tile_of(rows):
    return min(TILE_ROWS, rows)


WHOLE = pl.BlockSpec(memory_space=pltpu.VMEM)
PARAMS = pltpu.CompilerParams(vmem_limit_bytes=VMEM_BYTES)
LITTLE = pl.CostEstimate(flops=1000, bytes_accessed=1000, transcendentals=0)


OUTSIDE = pl.BlockSpec(memory_space=pltpu.HBM)


def prepare(heads, policy, q, g):
    members, rows, head_dim = q.shape
    turned = jax.ShapeDtypeStruct((members, head_dim, rows), q.dtype)
    return pl.pallas_call(
        functools.partial(prepare_kernel, heads),
        in_specs=[WHOLE] + [OUTSIDE] * 2,
        out_specs=[WHOLE] * 5,
        out_shape=[jax.ShapeDtypeStruct((members, 8, rows), jnp.float32)]
        + [jax.ShapeDtypeStruct(q.shape, q.dtype)] * 2
        + [turned] * 2,
        scratch_shapes=[pltpu.SemaphoreType.DMA((2,))],
        compiler_params=PARAMS,
        cost_estimate=LITTLE,
        name="prepare_rows",
    )(policy, q, g)


def forward_step(step, layers, heads, tokens, turned, earlier, messages):
    members, head_dim, rows = turned[0].shape
    each = messages[0].shape[0] - members * tokens
    counts = [tokens] * len(kinds_of(step, layers))
    out_shape = [jax.ShapeDtypeStruct((members, 8, rows), jnp.float32)]
    if step == layers:
        counts[1] = 2 * layers * each
        out_shape.append(jax.ShapeDtypeStruct((counts[1], 2 * head_dim), jnp.bfloat16))
    return pl.pallas_call(
        functools.partial(forward_kernel, step, layers, heads, head_dim, counts),
        in_specs=[WHOLE] * (3 + len(messages)),
        out_specs=[WHOLE] * len(out_shape),
        out_shape=out_shape,
        scratch_shapes=[pltpu.VMEM((sum(counts), head_dim), jnp.bfloat16)] * 2,
        compiler_params=PARAMS,
        cost_estimate=LITTLE,
        input_output_aliases={2: 0},
        name=f"attend_step{step}",
    )(*turned, earlier, *messages)


def backward_step(
    step, layers, heads, tokens, each, held_rows, final, messages, earlier, prompt_terms
):
    q = held_rows[0]
    members, rows, head_dim = q.shape
    counts = [tokens] * len(kinds_of(step, layers))

    def block(more, dtype=jnp.bfloat16, base=members * tokens):
        return jax.ShapeDtypeStruct((base + more, 2 * head_dim), dtype)

    if step == layers:
        counts[1] = 2 * layers * each
        grad_shapes = [
            block(each),
            block(layers * each, jnp.float32, 0),
            block((layers - 1) * each, jnp.bfloat16, 0),
        ]
    elif step == layers - 1:
        grad_shapes = [block((layers - 1) * each), block(each)]
    elif step == 1:
        grad_shapes = [block(each), block(0)]
    else:
        grad_shapes = [block(0)] * len(counts)
    columns = sum(counts)
    if step == 0:
        query_shape = jax.ShapeDtypeStruct(q.shape, jnp.bfloat16)
    else:
        query_shape = jax.ShapeDtypeStruct((members, head_dim, rows), jnp.float32)
    extra = [] if earlier is None else [earlier]
    aliases = {5 + len(messages): len(grad_shapes)} if extra and step > 0 else {}
    extra += prompt_terms
    outs = pl.pallas_call(
        functools.partial(backward_kernel, step, layers, heads, head_dim, counts),
        in_specs=[WHOLE] * (5 + len(messages) + len(extra)),
        out_specs=[WHOLE] * (len(grad_shapes) + 1),
        out_shape=grad_shapes + [query_shape],
        scratch_shapes=[pltpu.VMEM((columns, head_dim), jnp.bfloat16)] * 2
        + [pltpu.VMEM((head_dim, columns), jnp.bfloat16)]
        + [pltpu.VMEM((columns, tile_of(rows)), jnp.bfloat16)] * 2
        + [pltpu.VMEM((columns, 2 * head_dim), jnp.float32)],
        compiler_params=PARAMS,
        cost_estimate=LITTLE,
        input_output_aliases=aliases,
        name=f"attend_grad_step{step}",
    )(*held_rows, final, *messages, *extra)
    return outs[:-1], outs[-1]


def combine(step, layers, each, *terms):
    count, width = terms[0].shape
    if step > 0:
        shapes = [jax.ShapeDtypeStruct((count + each, width), jnp.bfloat16)]
        if step == layers - 2:
            shapes.append(jax.ShapeDtypeStruct((step * each, width), jnp.float32))
    else:
        shapes = [jax.ShapeDtypeStruct((count, width // 2), jnp.bfloat16)] * 2
        shapes.append(jax.ShapeDtypeStruct((each, width), jnp.float32))
    return pl.pallas_call(
        functools.partial(combine_kernel, step, layers, each),
        in_specs=[WHOLE] * len(terms),
        out_specs=[WHOLE] * len(shapes),
        out_shape=shapes,
        compiler_params=PARAMS,
        name=f"add_terms{step}",
    )(*terms)


def join_kernel(
    keys, values, prompt_keys, prompt_values, behaved, current, advantages, lengths, *refs
):
    out, policy, held_behaved, held_current, held_advantages, held_lengths, arrived = refs
    rows, head_dim = keys.shape
    members, tokens = behaved.shape

    def part(first, count, column):
        return out.at[pl.ds(first, count), pl.ds(column, head_dim)]

    each = prompt_keys.shape[0]
    targets = [
        (keys, part(0, rows, 0)),
        (values, part(0, rows, head_dim)),
        (prompt_keys, part(rows, each, 0)),
        (prompt_values, part(rows, each, head_dim)),
        (behaved, held_behaved),
        (current, held_current),
        (advantages, held_advantages),
        (lengths, held_lengths),
    ]
    copies = [
        pltpu.make_async_copy(source, target, arrived.at[i])
        for i, (source, target) in enumerate(targets)
    ]
    for copy in copies:
        copy.start()
    for copy in copies:
        copy.wait()
    full_len = tokens * lax.axis_size("ctx")
    position = lax.axis_index("ctx") * tokens + lax.broadcasted_iota(jnp.int32, (1, tokens), 1)
    ratio = jnp.minimum(jnp.exp(held_current[...] - held_behaved[...]), RATIO_CAP)
    for member in range(members):
        length = held_lengths[member]
        spread = full_len / jnp.full((1, 1), length).astype(jnp.float32)
        valid = jnp.where(position < length, ratio[member : member + 1], 0.0)
        policy[member : member + 1, :] = -held_advantages[member] * valid * spread
        wide = jnp.full((1, tokens), length).astype(jnp.float32)
        policy[members + member : members + member + 1, :] = wide


def join(keys, values, prompt_keys, prompt_values, behaved, current, advantages, lengths):
    rows = keys.shape[0] + prompt_keys.shape[0]
    members, tokens = behaved.shape
    return pl.pallas_call(
        join_kernel,
        out_shape=[
            jax.ShapeDtypeStruct((rows, 2 * keys.shape[1]), keys.dtype),
            jax.ShapeDtypeStruct((2 * members, tokens), jnp.float32),
        ],
        in_specs=[OUTSIDE] * 8,
        out_specs=[WHOLE] * 2,
        scratch_shapes=[
            pltpu.VMEM((members, tokens), jnp.float32),
            pltpu.VMEM((members, tokens), jnp.float32),
            pltpu.SMEM((members,), jnp.float32),
            pltpu.SMEM((members,), jnp.int32),
            pltpu.SemaphoreType.DMA((8,)),
        ],
        compiler_params=pltpu.CompilerParams(vmem_limit_bytes=JOIN_VMEM_BYTES),
        cost_estimate=LITTLE,
        name="join_pairs",
    )(keys, values, prompt_keys, prompt_values, behaved, current, advantages, lengths)


def per_device(
    queries,
    prompt_keys,
    prompt_values,
    resp_keys,
    resp_values,
    upstream,
    behav_logp,
    cur_logp,
    advantages,
    lengths,
):
    members, tokens, heads, head_dim = queries.shape
    ctx_size, resp_size = lax.axis_size("ctx"), lax.axis_size("resp")
    layers = ctx_size // 2
    each = prompt_keys.shape[0]
    rows = tokens * heads

    def hop(array, layers_up):
        pairs = [(c, (c + 2 * layers_up) % ctx_size) for c in range(ctx_size)]
        return lax.ppermute(array, "ctx", pairs)

    def cross(array):
        return lax.ppermute(array, "ctx", [(c, c ^ 1) for c in range(ctx_size)])

    own, policy = join(
        resp_keys.reshape(members * tokens, head_dim),
        resp_values.reshape(members * tokens, head_dim),
        prompt_keys,
        prompt_values,
        behav_logp,
        cur_logp,
        advantages,
        lengths,
    )
    z, x = [own, hop(own, 1)], [None, cross(own)]
    stat, *held_rows = prepare(
        heads,
        policy,
        queries.reshape(members, rows, head_dim),
        upstream.reshape(members, rows, head_dim),
    )

    def forward(step, stat, messages):
        return forward_step(step, layers, heads, tokens, held_rows[2:], stat, messages)

    for step in range(1, layers):
        z[step], stat = lax.optimization_barrier((z[step], stat))
        if step + 1 < layers:
            z.append(hop(z[step], 1))
            x.append(cross(z[step]))
        else:
            x.append(hop(x[1], layers - 1))
        if step == 1:
            (stat,) = forward(0, stat, z[:1])
        (stat,) = forward(step, stat, [x[step], z[step]])
    stat, prompt = forward(layers, stat, z + x[1:])
    final = stat
    moved = side = above = far = message = kept = None
    terms = []
    for step in range(layers, -1, -1):
        if message is not None:
            final, message = lax.optimization_barrier((final, message))
            above = hop(message, -1)
        if step == layers:
            messages = [x[step], prompt]
        else:
            messages = [z[0]] if step == 0 else [x[step], z[step]]
        grads, moved = backward_step(
            step, layers, heads, tokens, each, held_rows, final, messages, moved, terms
        )
        terms = [far] if step == 2 else []
        if step == layers:
            far, terms = hop(grads[0], 1 - layers), list(grads[1:])
            kept = grads[1]
        elif step == layers - 1:
            message = grads[1]
        elif step > 0:
            message, *more = combine(step, layers, each, grads[-1], side, above, kept)
            kept = more[0] if more else kept
        if 0 < step < layers:
            side = cross(grads[0])
    key_grads, value_grads, share = combine(0, layers, each, grads[-1], side, above, kept)
    stride = 1
    while stride < resp_size:
        pairs = [(c, c ^ stride) for c in range(resp_size)]
        share = share + lax.ppermute(share, "resp", pairs)
        stride *= 2
    return (
        moved.reshape(queries.shape),
        key_grads.reshape(resp_keys.shape),
        value_grads.reshape(resp_values.shape),
        share[:, :head_dim],
        share[:, head_dim:],
    )


def solution(mesh):
    placed = (
        P("resp", "ctx", None, None),
        P("ctx", None),
        P("ctx", None),
        P("resp", "ctx", None),
        P("resp", "ctx", None),
        P("resp", "ctx", None, None),
        P("resp", "ctx"),
        P("resp", "ctx"),
        P("resp"),
        P("resp"),
    )
    return jax.shard_map(
        per_device,
        mesh=mesh,
        in_specs=placed,
        out_specs=(
            P("resp", "ctx", None, None),
            P("resp", "ctx", None),
            P("resp", "ctx", None),
            P("ctx", None),
            P("ctx", None),
        ),
        check_vma=False,
    )
```

```python
import functools
import math

import jax
import jax.numpy as jnp
from jax import lax
from jax.experimental import pallas as pl
from jax.experimental.pallas import tpu as pltpu
from jax.sharding import PartitionSpec as P

RATIO_CAP = 2.0
MASKED = -1e30
SUB_ROWS = 256
TILE_ROWS = 1024
LARGEST_SCORE = 100.0
UNBOUNDED = 3e38

TOP, TOTAL, DOTTED, GUARD, WEIGHT, LENGTH = range(6)
VMEM_BYTES = 24 * 1024 * 1024
JOIN_VMEM_BYTES = 60 * 1024 * 1024

def dot(a, b):
    return jnp.dot(a, b, preferred_element_type=jnp.float32)


def kinds_of(step, layers):
    if step == 0:
        return ("z",)
    return ("x", "prompt") if step == layers else ("x", "z")


def variants(step, layers, place):
    z, odd = place // 2, place % 2 == 1
    if step == 0:
        return [(None, 0, 1)]
    if step == layers:
        return [(z >= step - 1, 0, 2), (z < step - 1, 1, 2)]
    if step == 1:
        return [
            ((z >= 1) & odd, 0, 2),
            ((z == 0) & odd, 0, 1),
            ((z >= 1) & jnp.logical_not(odd), 1, 2),
        ]
    return [(z >= step, 0, 2), (z == step - 1, 0, 1)]


def attends(step, layers, place):
    if step in (0, layers):
        return place >= 0
    return place >= 1 if step == 1 else place // 2 >= step - 1


def kept_keys(shape, first_row, heads):
    key = lax.broadcasted_iota(jnp.int32, shape, 0)
    row = lax.broadcasted_iota(jnp.int32, shape, 1) + first_row
    return key * heads <= row


def edges_of(counts):
    edges = [0]
    for count in counts:
        edges.append(edges[-1] + count)
    return edges


def largest_norm(rows):
    wide = rows.astype(jnp.float32)
    return jnp.max(jnp.sum(wide * wide, axis=1, keepdims=True))


def filled_tiles(length, tokens, heads, rows):
    per_tile = tile_of(rows) // heads
    left = length - lax.axis_index("ctx") * tokens
    return jnp.clip((left + per_tile - 1) // per_tile, 0, rows // tile_of(rows))


def load_keys(member, pairs, kinds, edges, head_dim, keys, values):
    for part, pair in enumerate(pairs):
        count = edges[part + 1] - edges[part]
        rows = pl.ds(edges[part], count)
        own = pl.ds(0, count)
        if kinds[part] != "prompt":
            own = pl.ds(pl.multiple_of(member * count, count), count)
        keys[rows, :] = pair[own, :head_dim]
        values[rows, :] = pair[own, head_dim:]


def length_of(stat, member):
    return jnp.max(stat[member, LENGTH : LENGTH + 1, 0:128]).astype(jnp.int32)


def spread_weights(ratio, heads):
    tokens = ratio.shape[1]
    shape = (tokens, tokens * heads)
    token = lax.broadcasted_iota(jnp.int32, shape, 0)
    row = lax.broadcasted_iota(jnp.int32, shape, 1)
    first = token * heads
    chosen = jnp.where((row >= first) & (row < first + heads), 1.0, 0.0)
    chosen = chosen.astype(jnp.bfloat16)
    out, rest = None, ratio
    for _ in range(3):
        term = rest.astype(jnp.bfloat16)
        rest = rest - term.astype(jnp.float32)
        few = jnp.broadcast_to(term.astype(jnp.float32), (16, tokens)).astype(jnp.bfloat16)
        part = jnp.dot(few, chosen, preferred_element_type=jnp.float32)[0:1]
        out = part if out is None else out + part
    return out


def key_sum(array):
    count = array.shape[0] // 4
    parts = [
        jnp.sum(array[i * count : (i + 1) * count], axis=0, keepdims=True) for i in range(4)
    ]
    return (parts[0] + parts[1]) + (parts[2] + parts[3])


def prepare_kernel(heads, policy, held_q, held_g, out, q, g, turned_q, turned_g, arrived):
    copies = [
        pltpu.make_async_copy(source, target, arrived.at[i])
        for i, (source, target) in enumerate([(held_q, q), (held_g, g)])
    ]
    for copy in copies:
        copy.start()
    for copy in copies:
        copy.wait()
    members, all_rows, _ = q.shape
    tile = tile_of(all_rows)
    tokens = all_rows // heads
    line = lax.broadcasted_iota(jnp.int32, policy.shape, 0)

    def per_member(member, carry):
        known = jnp.max(jnp.where(line == members + member, policy[...], 0.0))
        out[member, LENGTH : LENGTH + 1, :] = jnp.full((1, all_rows), known)

        def per_tile(index, carry):
            rows = pl.ds(pl.multiple_of(index * tile, tile), tile)
            turned_q[member, :, rows] = q[member, rows, :].T
            turned_g[member, :, rows] = g[member, rows, :].T
            guard = largest_norm(q[member, rows, :])
            out[member, GUARD : GUARD + 1, rows] = jnp.full((1, tile), guard)
            count = tile // heads
            part = pl.ds(pl.multiple_of(index * count, count), count)
            if count == tokens:
                part = pl.ds(0, count)
            chosen = jnp.where(line[:, :count] == member, policy[:, part], 0.0)
            ratio = jnp.sum(chosen, axis=0, keepdims=True)
            out[member, WEIGHT : WEIGHT + 1, rows] = spread_weights(ratio, heads)
            return carry

        filled = filled_tiles(known.astype(jnp.int32), tokens, heads, all_rows)
        lax.fori_loop(0, filled, per_tile, 0)
        return carry

    lax.fori_loop(0, members, per_member, 0)


def forward_kernel(step, layers, heads, head_dim, counts, turned_q, turned_g, earlier, *refs):
    kinds = kinds_of(step, layers)
    parts = len(kinds)
    if step == layers:
        messages, (out, prompt, keys, values) = refs[: 2 * layers], refs[2 * layers :]
        own = messages[0].shape[0] - prompt.shape[0] // (2 * layers)
        each = messages[0].shape[0] - own
        for i, message in enumerate(messages):
            prompt[i * each : (i + 1) * each, :] = message[own:, :]
        pairs = [messages[-1], prompt]
    else:
        pairs, (out, keys, values) = refs[:parts], refs[parts:]
    place = lax.axis_index("ctx")
    members, _, all_rows = turned_q.shape
    tile = tile_of(all_rows)
    tokens = all_rows // heads
    scale = head_dim**-0.5 * math.log2(math.e)
    edges = edges_of(counts)
    attended = attends(step, layers, place)

    def shared(member, low, high, first, start):
        rows = pl.ds(row_start(first, start), SUB_ROWS)
        scores = dot(keys[low:high, :], turned_q[member, :, rows]) * scale
        if step == 0:
            kept = kept_keys(scores.shape, first + start, heads)
            scores = jnp.where(kept, scores, MASKED)
        return rows, scores, dot(values[low:high, :], turned_g[member, :, rows])

    def put(member, first, span, lines):
        rows = pl.ds(first, span)
        for line, pieces in lines.items():
            out[member, line : line + 1, rows] = jnp.concatenate(pieces, 1)

    def bounded(member, low, high, first, span):
        totals, dots = [], []
        for start in range(0, span, SUB_ROWS):
            rows, scores, grad_probs = shared(member, low, high, first, start)
            weight = jnp.exp2(scores)
            total, dotted = key_sum(weight), key_sum(weight * grad_probs)
            if step > 0:
                total = total + earlier[member, TOTAL : TOTAL + 1, rows]
                dotted = dotted + earlier[member, DOTTED : DOTTED + 1, rows]
            totals.append(total)
            dots.append(dotted)
        tops = [jnp.zeros_like(t) for t in totals]
        put(member, first, span, {TOP: tops, TOTAL: totals, DOTTED: dots})

    def general(member, low, high, first, span):
        tops, totals, dots = [], [], []
        for start in range(0, span, SUB_ROWS):
            rows, scores, grad_probs = shared(member, low, high, first, start)
            top = jnp.max(scores, axis=0, keepdims=True)
            if step > 0:
                top = jnp.maximum(top, earlier[member, TOP : TOP + 1, rows])
            weight = jnp.exp2(scores - top)
            total, dotted = key_sum(weight), key_sum(weight * grad_probs)
            if step > 0:
                decay = jnp.exp2(earlier[member, TOP : TOP + 1, rows] - top)
                total = total + decay * earlier[member, TOTAL : TOTAL + 1, rows]
                dotted = dotted + decay * earlier[member, DOTTED : DOTTED + 1, rows]
            tops.append(top)
            totals.append(total)
            dots.append(dotted)
        guards = [jnp.full_like(t, UNBOUNDED) for t in totals]
        put(member, first, span, {TOP: tops, TOTAL: totals, DOTTED: dots, GUARD: guards})

    def per_member(member, carry):
        filled = filled_tiles(length_of(earlier, member), tokens, heads, all_rows)

        @pl.when((filled > 0) & attended)
        def _():
            load_keys(member, pairs, kinds, edges, head_dim, keys, values)
            limit = (LARGEST_SCORE / scale) ** 2 / largest_norm(keys[...])
            guards = earlier[member, GUARD : GUARD + 1, :]
            column = lax.broadcasted_iota(jnp.int32, guards.shape, 1)
            fast = jnp.max(jnp.where(column < filled * tile, guards, 0.0)) <= limit
            for condition, begin, past in variants(step, layers, place):
                low, high = edges[begin], edges[past]
                here = True if condition is None else condition

                @pl.when(fast & here)
                def _():
                    over_tiles(filled, all_rows, functools.partial(bounded, member, low, high))

                @pl.when(jnp.logical_not(fast) & here)
                def _():
                    over_tiles(filled, all_rows, functools.partial(general, member, low, high), 0)

        return carry

    lax.fori_loop(0, members, per_member, 0)


def row_start(first, start):
    if isinstance(first, int):
        return first + start
    return pl.multiple_of(first + start, SUB_ROWS)


def over_tiles(filled, all_rows, body, whole=1):
    tile = tile_of(all_rows)
    tiles = all_rows // tile

    def per_tile(index, carry):
        body(pl.multiple_of(index * tile, tile), tile)
        return carry

    if tiles == 1 or not whole:
        lax.fori_loop(0, filled, per_tile, 0)
        return

    @pl.when(filled == tiles)
    def _():
        body(0, all_rows)

    @pl.when(filled < tiles)
    def _():
        lax.fori_loop(0, filled, per_tile, 0)


def backward_kernel(step, layers, heads, head_dim, counts, *refs):
    q, g, turned_q, turned_g, final = refs[:5]
    refs = refs[5:]
    kinds = kinds_of(step, layers)
    count = len(kinds)
    pairs, refs = refs[:count], refs[count:]
    earlier = None
    if step < layers:
        earlier, refs = refs[0], refs[1:]
    if step == layers - 1:
        stay, leave = refs[:2]
        refs = refs[2:]
    made = 3 if step == layers else count
    grads, query_out, refs = refs[:made], refs[made], refs[made + 1 :]
    keys, values, turned, probs_held, scores_held, sums = refs
    place = lax.axis_index("ctx")
    members, all_rows = q.shape[:2]
    tile = tile_of(all_rows)
    tokens = all_rows // heads
    plain = head_dim**-0.5
    scale = plain * math.log2(math.e)
    edges = edges_of(counts)
    attended = attends(step, layers, place)

    def body(member, low, high, first, span):
        whole = pl.ds(first, span)
        held_rows = slice(0, span)
        total = final[member, TOTAL : TOTAL + 1, whole]
        level = final[member, TOP : TOP + 1, whole] + jnp.log2(total)
        delta = final[member, DOTTED : DOTTED + 1, whole] / total
        token_weight = final[member, WEIGHT : WEIGHT + 1, whole]
        for start in range(0, span, SUB_ROWS):
            rows = pl.ds(row_start(first, start), SUB_ROWS)
            held = slice(start, start + SUB_ROWS)
            scores = dot(keys[low:high, :], turned_q[member, :, rows]) * scale
            scores = scores - level[:, held]
            if step == 0:
                kept = kept_keys(scores.shape, first + start, heads)
                scores = jnp.where(kept, scores, MASKED)
            probs = jnp.exp2(scores) * token_weight[:, held]
            grad_probs = dot(values[low:high, :], turned_g[member, :, rows])
            grad_scores = probs * (grad_probs - delta[:, held])
            probs_held[low:high, held] = probs.astype(jnp.bfloat16)
            scores_held[low:high, held] = grad_scores.astype(jnp.bfloat16)
        sums[low:high, head_dim:] += dot(probs_held[low:high, held_rows], g[member, whole, :])
        sums[low:high, :head_dim] += dot(scores_held[low:high, held_rows], q[member, whole, :])
        moved = dot(turned[:, low:high], scores_held[low:high, held_rows])
        if earlier is not None:
            moved = moved + earlier[member, :, whole]
        if step == 0:
            query_out[member, whole, :] = (moved * plain).T.astype(jnp.bfloat16)
        else:
            query_out[member, :, whole] = moved

    def per_member(member, carry):
        filled = filled_tiles(length_of(final, member), tokens, heads, all_rows)
        filled = jnp.where(attended, filled, 0)
        for part in range(count):
            rows = pl.ds(edges[part], edges[part + 1] - edges[part])

            @pl.when((member == 0) | (kinds[part] != "prompt"))
            def _():
                sums[rows, :] = jnp.zeros_like(sums[rows, :])

        @pl.when(filled > 0)
        def _():
            load_keys(member, pairs, kinds, edges, head_dim, keys, values)
            turned[...] = keys[...].T

            for condition, begin, past in variants(step, layers, place):
                low, high = edges[begin], edges[past]

                @pl.when(True if condition is None else condition)
                def _():
                    over_tiles(filled, all_rows, functools.partial(body, member, low, high), 0)

        if step == 0 or earlier is None:

            def clear(index, carry):
                rows = pl.ds(pl.multiple_of(index * tile, tile), tile)
                if step == 0:
                    query_out[member, rows, :] = jnp.zeros((tile, head_dim), jnp.bfloat16)
                else:
                    query_out[member, :, rows] = jnp.zeros((head_dim, tile), jnp.float32)
                return carry

            lax.fori_loop(filled, all_rows // tile, clear, 0)
        for part in range(count):
            if kinds[part] == "prompt":
                continue
            rows = pl.ds(edges[part], counts[part])
            own = pl.ds(pl.multiple_of(member * counts[part], counts[part]), counts[part])
            key_part, value_part = sums[rows, :head_dim] * plain, sums[rows, head_dim:]
            grads[part][own, :head_dim] = key_part.astype(jnp.bfloat16)
            grads[part][own, head_dim:] = value_part.astype(jnp.bfloat16)
        return carry

    lax.fori_loop(0, members, per_member, 0)
    tail = members * tokens
    if step == layers:
        far, stay, leave = grads
        middle = edges[1] + stay.shape[0]
        last = middle + leave.shape[0]
        for target, begin, rows in (
            (stay, 0, slice(edges[1], middle)),
            (leave, 0, slice(middle, last)),
            (far, tail, slice(last, edges[2])),
        ):
            end = target.shape[0]
            target[begin:end, :head_dim] = (sums[rows, :head_dim] * plain).astype(target.dtype)
            target[begin:end, head_dim:] = sums[rows, head_dim:].astype(target.dtype)
    elif step == layers - 1:
        grads[0][tail:, :] = leave[...]
        grads[1][tail:, :] = stay[leave.shape[0] :, :].astype(jnp.bfloat16)


def combine_kernel(step, layers, each, own, side, above, *refs):
    def wide(ref, rows):
        return ref[rows, :].astype(jnp.float32)

    count = own.shape[0]
    rows = slice(0, count)
    total = wide(own, rows) + wide(side, rows) + wide(above, rows)
    if step == 0:
        key_out, value_out = refs
        total = total.astype(jnp.bfloat16)
        head_dim = key_out.shape[1]
        key_out[...] = total[:, :head_dim]
        value_out[...] = total[:, head_dim:]
        return
    kept, *refs = refs
    if step == 1:
        crossing, far, *refs = refs
    out, *refs = refs
    mine = slice(step * each, (step + 1) * each)
    prompt = kept[mine, :] + wide(above, slice(count, None))
    if step == layers - 2:
        prompt = prompt + wide(side, slice(count + mine.start, count + mine.stop))
        still_kept, *refs = refs
        still_kept[...] = kept[: step * each, :] + wide(side, slice(count, count + step * each))
    out[rows, :] = total.astype(jnp.bfloat16)
    out[count:, :] = prompt.astype(jnp.bfloat16)
    if step == 1:
        (leaving,) = refs
        leaving[rows, :] = (wide(crossing, rows) + wide(far, rows)).astype(jnp.bfloat16)
        leaving[count:, :] = far[count:, :]


def tile_of(rows):
    return min(TILE_ROWS, rows)


WHOLE = pl.BlockSpec(memory_space=pltpu.VMEM)
PARAMS = pltpu.CompilerParams(vmem_limit_bytes=VMEM_BYTES)
LITTLE = pl.CostEstimate(flops=1000, bytes_accessed=1000, transcendentals=0)


OUTSIDE = pl.BlockSpec(memory_space=pltpu.HBM)


def prepare(heads, policy, q, g):
    members, rows, head_dim = q.shape
    turned = jax.ShapeDtypeStruct((members, head_dim, rows), q.dtype)
    return pl.pallas_call(
        functools.partial(prepare_kernel, heads),
        in_specs=[WHOLE] + [OUTSIDE] * 2,
        out_specs=[WHOLE] * 5,
        out_shape=[jax.ShapeDtypeStruct((members, 8, rows), jnp.float32)]
        + [jax.ShapeDtypeStruct(q.shape, q.dtype)] * 2
        + [turned] * 2,
        scratch_shapes=[pltpu.SemaphoreType.DMA((2,))],
        compiler_params=PARAMS,
        cost_estimate=LITTLE,
        name="prepare_rows",
    )(policy, q, g)


def forward_step(step, layers, heads, tokens, turned, earlier, messages):
    members, head_dim, rows = turned[0].shape
    each = messages[0].shape[0] - members * tokens
    counts = [tokens] * len(kinds_of(step, layers))
    out_shape = [jax.ShapeDtypeStruct((members, 8, rows), jnp.float32)]
    if step == layers:
        counts[1] = 2 * layers * each
        out_shape.append(jax.ShapeDtypeStruct((counts[1], 2 * head_dim), jnp.bfloat16))
    return pl.pallas_call(
        functools.partial(forward_kernel, step, layers, heads, head_dim, counts),
        in_specs=[WHOLE] * (3 + len(messages)),
        out_specs=[WHOLE] * len(out_shape),
        out_shape=out_shape,
        scratch_shapes=[pltpu.VMEM((sum(counts), head_dim), jnp.bfloat16)] * 2,
        compiler_params=PARAMS,
        cost_estimate=LITTLE,
        input_output_aliases={2: 0},
        name=f"attend_step{step}",
    )(*turned, earlier, *messages)


def backward_step(
    step, layers, heads, tokens, each, held_rows, final, messages, earlier, prompt_terms
):
    q = held_rows[0]
    members, rows, head_dim = q.shape
    counts = [tokens] * len(kinds_of(step, layers))

    def block(more, dtype=jnp.bfloat16, base=members * tokens):
        return jax.ShapeDtypeStruct((base + more, 2 * head_dim), dtype)

    if step == layers:
        counts[1] = 2 * layers * each
        grad_shapes = [
            block(each),
            block(layers * each, jnp.float32, 0),
            block((layers - 1) * each, jnp.bfloat16, 0),
        ]
    elif step == layers - 1:
        grad_shapes = [block((layers - 1) * each), block(each)]
    else:
        grad_shapes = [block(0)] * len(counts)
    columns = sum(counts)
    if step == 0:
        query_shape = jax.ShapeDtypeStruct(q.shape, jnp.bfloat16)
    else:
        query_shape = jax.ShapeDtypeStruct((members, head_dim, rows), jnp.float32)
    extra = [] if earlier is None else [earlier]
    aliases = {5 + len(messages): len(grad_shapes)} if extra and step > 0 else {}
    extra += prompt_terms
    outs = pl.pallas_call(
        functools.partial(backward_kernel, step, layers, heads, head_dim, counts),
        in_specs=[WHOLE] * (5 + len(messages) + len(extra)),
        out_specs=[WHOLE] * (len(grad_shapes) + 1),
        out_shape=grad_shapes + [query_shape],
        scratch_shapes=[pltpu.VMEM((columns, head_dim), jnp.bfloat16)] * 2
        + [pltpu.VMEM((head_dim, columns), jnp.bfloat16)]
        + [pltpu.VMEM((columns, tile_of(rows)), jnp.bfloat16)] * 2
        + [pltpu.VMEM((columns, 2 * head_dim), jnp.float32)],
        compiler_params=PARAMS,
        cost_estimate=LITTLE,
        input_output_aliases=aliases,
        name=f"attend_grad_step{step}",
    )(*held_rows, final, *messages, *extra)
    return outs[:-1], outs[-1]


def combine(step, layers, each, *terms):
    count, width = terms[0].shape
    message = jax.ShapeDtypeStruct((count + each, width), jnp.bfloat16)
    if step == 0:
        shapes = [jax.ShapeDtypeStruct((count, width // 2), jnp.bfloat16)] * 2
    else:
        shapes = [message]
        if step == layers - 2:
            shapes.append(jax.ShapeDtypeStruct((step * each, width), jnp.float32))
        if step == 1:
            shapes.append(message)
    return pl.pallas_call(
        functools.partial(combine_kernel, step, layers, each),
        in_specs=[WHOLE] * len(terms),
        out_specs=[WHOLE] * len(shapes),
        out_shape=shapes,
        compiler_params=PARAMS,
        cost_estimate=LITTLE,
        name=f"add_terms{step}",
    )(*terms)


def join_kernel(
    keys, values, prompt_keys, prompt_values, behaved, current, advantages, lengths, *refs
):
    out, policy, held_behaved, held_current, held_advantages, held_lengths, arrived = refs
    rows, head_dim = keys.shape
    members, tokens = behaved.shape

    def part(first, count, column):
        return out.at[pl.ds(first, count), pl.ds(column, head_dim)]

    each = prompt_keys.shape[0]
    targets = [
        (keys, part(0, rows, 0)),
        (values, part(0, rows, head_dim)),
        (prompt_keys, part(rows, each, 0)),
        (prompt_values, part(rows, each, head_dim)),
        (behaved, held_behaved),
        (current, held_current),
        (advantages, held_advantages),
        (lengths, held_lengths),
    ]
    copies = [
        pltpu.make_async_copy(source, target, arrived.at[i])
        for i, (source, target) in enumerate(targets)
    ]
    for copy in copies:
        copy.start()
    for copy in copies:
        copy.wait()
    full_len = tokens * lax.axis_size("ctx")
    position = lax.axis_index("ctx") * tokens + lax.broadcasted_iota(jnp.int32, (1, tokens), 1)
    ratio = jnp.minimum(jnp.exp(held_current[...] - held_behaved[...]), RATIO_CAP)
    for member in range(members):
        length = held_lengths[member]
        spread = full_len / jnp.full((1, 1), length).astype(jnp.float32)
        valid = jnp.where(position < length, ratio[member : member + 1], 0.0)
        policy[member : member + 1, :] = -held_advantages[member] * valid * spread
        wide = jnp.full((1, tokens), length).astype(jnp.float32)
        policy[members + member : members + member + 1, :] = wide


def join(keys, values, prompt_keys, prompt_values, behaved, current, advantages, lengths):
    rows = keys.shape[0] + prompt_keys.shape[0]
    members, tokens = behaved.shape
    return pl.pallas_call(
        join_kernel,
        out_shape=[
            jax.ShapeDtypeStruct((rows, 2 * keys.shape[1]), keys.dtype),
            jax.ShapeDtypeStruct((2 * members, tokens), jnp.float32),
        ],
        in_specs=[OUTSIDE] * 8,
        out_specs=[WHOLE] * 2,
        scratch_shapes=[
            pltpu.VMEM((members, tokens), jnp.float32),
            pltpu.VMEM((members, tokens), jnp.float32),
            pltpu.SMEM((members,), jnp.float32),
            pltpu.SMEM((members,), jnp.int32),
            pltpu.SemaphoreType.DMA((8,)),
        ],
        compiler_params=pltpu.CompilerParams(vmem_limit_bytes=JOIN_VMEM_BYTES),
        cost_estimate=LITTLE,
        name="join_pairs",
    )(keys, values, prompt_keys, prompt_values, behaved, current, advantages, lengths)


def per_device(
    queries,
    prompt_keys,
    prompt_values,
    resp_keys,
    resp_values,
    upstream,
    behav_logp,
    cur_logp,
    advantages,
    lengths,
):
    members, tokens, heads, head_dim = queries.shape
    ctx_size, resp_size = lax.axis_size("ctx"), lax.axis_size("resp")
    layers = ctx_size // 2
    each = prompt_keys.shape[0]
    rows = tokens * heads

    def hop(array, layers_up):
        pairs = [(c, (c + 2 * layers_up) % ctx_size) for c in range(ctx_size)]
        return lax.ppermute(array, "ctx", pairs)

    def cross(array):
        return lax.ppermute(array, "ctx", [(c, c ^ 1) for c in range(ctx_size)])

    own, policy = join(
        resp_keys.reshape(members * tokens, head_dim),
        resp_values.reshape(members * tokens, head_dim),
        prompt_keys,
        prompt_values,
        behav_logp,
        cur_logp,
        advantages,
        lengths,
    )
    z, x = [own, hop(own, 1)], [None, cross(own)]
    stat, *held_rows = prepare(
        heads,
        policy,
        queries.reshape(members, rows, head_dim),
        upstream.reshape(members, rows, head_dim),
    )

    def forward(step, stat, messages):
        return forward_step(step, layers, heads, tokens, held_rows[2:], stat, messages)

    for step in range(1, layers):
        z[step], stat = lax.optimization_barrier((z[step], stat))
        if step + 1 < layers:
            z.append(hop(z[step], 1))
            x.append(cross(z[step]))
        else:
            x.append(hop(x[1], layers - 1))
        if step == 1:
            (stat,) = forward(0, stat, z[:1])
        (stat,) = forward(step, stat, [x[step], z[step]])
    stat, prompt = forward(layers, stat, z + x[1:])
    final = stat
    moved = side = above = far = message = kept = None
    terms = []
    for step in range(layers, -1, -1):
        if message is not None:
            final, message = lax.optimization_barrier((final, message))
            above = hop(message, -1)
        if step == layers:
            messages = [x[step], prompt]
        else:
            messages = [z[0]] if step == 0 else [x[step], z[step]]
        grads, moved = backward_step(
            step, layers, heads, tokens, each, held_rows, final, messages, moved, terms
        )
        terms = []
        if step == layers:
            far, terms = hop(grads[0], 1 - layers), list(grads[1:])
            kept = grads[1]
        elif step == layers - 1:
            message = grads[1]
        elif step > 0:
            crossing = [grads[0], far] if step == 1 else []
            message, *more = combine(
                step, layers, each, grads[-1], side, above, kept, *crossing
            )
            if step == layers - 2:
                kept, *more = more
            if step == 1:
                grads = more
        if 0 < step < layers:
            side = cross(grads[0])
    above, side, last = lax.optimization_barrier((above, side, grads[-1]))
    share = kept[:each]
    for term in (above, side):
        share = share + term[-each:].astype(jnp.float32)
    key_grads, value_grads = combine(0, layers, each, last, side, above)
    if resp_size <= 4:
        shares = [
            lax.ppermute(share, "resp", [(c, c ^ i) for c in range(resp_size)])
            for i in range(1, resp_size)
        ]
        share = functools.reduce(jnp.add, shares, share)
    else:
        stride = 1
        while stride < resp_size:
            pairs = [(c, c ^ stride) for c in range(resp_size)]
            share = share + lax.ppermute(share, "resp", pairs)
            stride *= 2
    return (
        moved.reshape(queries.shape),
        key_grads.reshape(resp_keys.shape),
        value_grads.reshape(resp_values.shape),
        share[:, :head_dim],
        share[:, head_dim:],
    )


def solution(mesh):
    placed = (
        P("resp", "ctx", None, None),
        P("ctx", None),
        P("ctx", None),
        P("resp", "ctx", None),
        P("resp", "ctx", None),
        P("resp", "ctx", None, None),
        P("resp", "ctx"),
        P("resp", "ctx"),
        P("resp"),
        P("resp"),
    )
    return jax.shard_map(
        per_device,
        mesh=mesh,
        in_specs=placed,
        out_specs=(
            P("resp", "ctx", None, None),
            P("resp", "ctx", None),
            P("resp", "ctx", None),
            P("ctx", None),
            P("ctx", None),
        ),
        check_vma=False,
    )
```

```python
import functools
import math

import jax
import jax.numpy as jnp
from jax import lax
from jax.experimental import pallas as pl
from jax.experimental.pallas import tpu as pltpu
from jax.sharding import PartitionSpec as P

RATIO_CAP = 2.0
MASKED = -1e30
SUB_ROWS = 512
TILE_ROWS = 1024
LARGEST_SCORE = 100.0
UNBOUNDED = 3e38

TOP, TOTAL, DOTTED, GUARD, LENGTH = range(5)
VMEM_BYTES = 24 * 1024 * 1024
JOIN_VMEM_BYTES = 60 * 1024 * 1024

def dot(a, b):
    return jnp.dot(a, b, preferred_element_type=jnp.float32)


def kinds_of(step, layers):
    if step == 0:
        return ("z",)
    return ("x", "prompt") if step == layers else ("x", "z")


def variants(step, layers, place):
    z, odd = place // 2, place % 2 == 1
    if step == 0:
        return [(None, 0, 1)]
    if step == layers:
        return [(z >= step - 1, 0, 2), (z < step - 1, 1, 2)]
    if step == 1:
        return [
            ((z >= 1) & odd, 0, 2),
            ((z == 0) & odd, 0, 1),
            ((z >= 1) & jnp.logical_not(odd), 1, 2),
        ]
    return [(z >= step, 0, 2), (z == step - 1, 0, 1)]


def attends(step, layers, place):
    if step in (0, layers):
        return place >= 0
    return place >= 1 if step == 1 else place // 2 >= step - 1


def kept_keys(shape, first_row, heads):
    key = lax.broadcasted_iota(jnp.int32, shape, 0)
    row = lax.broadcasted_iota(jnp.int32, shape, 1) + first_row
    return key * heads <= row


def edges_of(counts):
    edges = [0]
    for count in counts:
        edges.append(edges[-1] + count)
    return edges


def largest_norm(rows):
    wide = rows.astype(jnp.float32)
    return jnp.max(jnp.sum(wide * wide, axis=1, keepdims=True))


def filled_tiles(length, tokens, heads, rows):
    per_tile = tile_of(rows) // heads
    left = length - lax.axis_index("ctx") * tokens
    return jnp.clip((left + per_tile - 1) // per_tile, 0, rows // tile_of(rows))


def load_keys(member, pairs, kinds, edges, head_dim, keys, values):
    for part, pair in enumerate(pairs):
        count = edges[part + 1] - edges[part]
        rows = pl.ds(edges[part], count)
        own = pl.ds(0, count)
        if kinds[part] != "prompt":
            own = pl.ds(pl.multiple_of(member * count, count), count)
        keys[rows, :] = pair[own, :head_dim]
        values[rows, :] = pair[own, head_dim:]


def length_of(stat, member):
    return jnp.max(stat[member, LENGTH : LENGTH + 1, 0:128]).astype(jnp.int32)


def spread_weights(ratio, heads):
    tokens = ratio.shape[1]
    shape = (tokens, tokens * heads)
    token = lax.broadcasted_iota(jnp.int32, shape, 0)
    row = lax.broadcasted_iota(jnp.int32, shape, 1)
    first = token * heads
    chosen = jnp.where((row >= first) & (row < first + heads), 1.0, 0.0)
    chosen = chosen.astype(jnp.bfloat16)
    out, rest = None, ratio
    for _ in range(3):
        term = rest.astype(jnp.bfloat16)
        rest = rest - term.astype(jnp.float32)
        few = jnp.broadcast_to(term.astype(jnp.float32), (16, tokens)).astype(jnp.bfloat16)
        part = jnp.dot(few, chosen, preferred_element_type=jnp.float32)[0:1]
        out = part if out is None else out + part
    return out


def key_sum(array):
    count = array.shape[0] // 4
    parts = [
        jnp.sum(array[i * count : (i + 1) * count], axis=0, keepdims=True) for i in range(4)
    ]
    return (parts[0] + parts[1]) + (parts[2] + parts[3])


def prepare_kernel(heads, policy, held_q, held_g, out, q, g, turned_q, turned_g, arrived):
    copies = [
        pltpu.make_async_copy(source, target, arrived.at[i])
        for i, (source, target) in enumerate([(held_q, q), (held_g, g)])
    ]
    for copy in copies:
        copy.start()
    for copy in copies:
        copy.wait()
    members, all_rows, _ = q.shape
    tile = tile_of(all_rows)
    tokens = all_rows // heads
    line = lax.broadcasted_iota(jnp.int32, policy.shape, 0)

    def per_member(member, carry):
        known = jnp.max(jnp.where(line == members + member, policy[...], 0.0))
        out[member, LENGTH : LENGTH + 1, :] = jnp.full((1, all_rows), known)

        def per_tile(index, carry):
            rows = pl.ds(pl.multiple_of(index * tile, tile), tile)
            turned_q[member, :, rows] = q[member, rows, :].T
            guard = largest_norm(q[member, rows, :])
            out[member, GUARD : GUARD + 1, rows] = jnp.full((1, tile), guard)
            count = tile // heads
            part = pl.ds(pl.multiple_of(index * count, count), count)
            if count == tokens:
                part = pl.ds(0, count)
            chosen = jnp.where(line[:, :count] == member, policy[:, part], 0.0)
            ratio = jnp.sum(chosen, axis=0, keepdims=True)
            weighted = g[member, rows, :].T.astype(jnp.float32) * spread_weights(ratio, heads)
            weighted = weighted.astype(jnp.bfloat16)
            turned_g[member, :, rows] = weighted
            g[member, rows, :] = weighted.T
            return carry

        filled = filled_tiles(known.astype(jnp.int32), tokens, heads, all_rows)
        lax.fori_loop(0, filled, per_tile, 0)
        return carry

    lax.fori_loop(0, members, per_member, 0)


def forward_kernel(step, layers, heads, head_dim, counts, turned_q, turned_g, earlier, *refs):
    kinds = kinds_of(step, layers)
    parts = len(kinds)
    if step == layers:
        messages, (out, prompt, keys, values) = refs[: 2 * layers], refs[2 * layers :]
        own = messages[0].shape[0] - prompt.shape[0] // (2 * layers)
        each = messages[0].shape[0] - own
        for i, message in enumerate(messages):
            prompt[i * each : (i + 1) * each, :] = message[own:, :]
        pairs = [messages[-1], prompt]
    else:
        pairs, (out, keys, values) = refs[:parts], refs[parts:]
    place = lax.axis_index("ctx")
    members, _, all_rows = turned_q.shape
    tile = tile_of(all_rows)
    tokens = all_rows // heads
    scale = head_dim**-0.5 * math.log2(math.e)
    edges = edges_of(counts)
    attended = attends(step, layers, place)

    def shared(member, low, high, first, start):
        rows = pl.ds(row_start(first, start), SUB_ROWS)
        scores = dot(keys[low:high, :], turned_q[member, :, rows]) * scale
        if step == 0:
            kept = kept_keys(scores.shape, first + start, heads)
            scores = jnp.where(kept, scores, MASKED)
        return rows, scores, dot(values[low:high, :], turned_g[member, :, rows])

    def put(member, first, span, lines):
        rows = pl.ds(first, span)
        for line, pieces in lines.items():
            out[member, line : line + 1, rows] = jnp.concatenate(pieces, 1)

    def bounded(member, low, high, first, span):
        totals, dots = [], []
        for start in range(0, span, SUB_ROWS):
            rows, scores, grad_probs = shared(member, low, high, first, start)
            weight = jnp.exp2(scores)
            total, dotted = key_sum(weight), key_sum(weight * grad_probs)
            if step > 0:
                total = total + earlier[member, TOTAL : TOTAL + 1, rows]
                dotted = dotted + earlier[member, DOTTED : DOTTED + 1, rows]
            totals.append(total)
            dots.append(dotted)
        tops = [jnp.zeros_like(t) for t in totals]
        put(member, first, span, {TOP: tops, TOTAL: totals, DOTTED: dots})

    def general(member, low, high, first, span):
        tops, totals, dots = [], [], []
        for start in range(0, span, SUB_ROWS):
            rows, scores, grad_probs = shared(member, low, high, first, start)
            top = jnp.max(scores, axis=0, keepdims=True)
            if step > 0:
                top = jnp.maximum(top, earlier[member, TOP : TOP + 1, rows])
            weight = jnp.exp2(scores - top)
            total, dotted = key_sum(weight), key_sum(weight * grad_probs)
            if step > 0:
                decay = jnp.exp2(earlier[member, TOP : TOP + 1, rows] - top)
                total = total + decay * earlier[member, TOTAL : TOTAL + 1, rows]
                dotted = dotted + decay * earlier[member, DOTTED : DOTTED + 1, rows]
            tops.append(top)
            totals.append(total)
            dots.append(dotted)
        guards = [jnp.full_like(t, UNBOUNDED) for t in totals]
        put(member, first, span, {TOP: tops, TOTAL: totals, DOTTED: dots, GUARD: guards})

    def per_member(member, carry):
        filled = filled_tiles(length_of(earlier, member), tokens, heads, all_rows)

        @pl.when((filled > 0) & attended)
        def _():
            load_keys(member, pairs, kinds, edges, head_dim, keys, values)
            limit = (LARGEST_SCORE / scale) ** 2 / largest_norm(keys[...])
            guards = earlier[member, GUARD : GUARD + 1, :]
            column = lax.broadcasted_iota(jnp.int32, guards.shape, 1)
            fast = jnp.max(jnp.where(column < filled * tile, guards, 0.0)) <= limit
            for condition, begin, past in variants(step, layers, place):
                low, high = edges[begin], edges[past]
                here = True if condition is None else condition

                @pl.when(fast & here)
                def _():
                    over_tiles(filled, all_rows, functools.partial(bounded, member, low, high))

                @pl.when(jnp.logical_not(fast) & here)
                def _():
                    over_tiles(filled, all_rows, functools.partial(general, member, low, high), 0)

        return carry

    lax.fori_loop(0, members, per_member, 0)


def row_start(first, start):
    if isinstance(first, int):
        return first + start
    return pl.multiple_of(first + start, SUB_ROWS)


def over_tiles(filled, all_rows, body, whole=1):
    tile = tile_of(all_rows)
    tiles = all_rows // tile

    def per_tile(index, carry):
        body(pl.multiple_of(index * tile, tile), tile)
        return carry

    if tiles == 1 or not whole:
        lax.fori_loop(0, filled, per_tile, 0)
        return

    @pl.when(filled == tiles)
    def _():
        body(0, all_rows)

    @pl.when(filled < tiles)
    def _():
        lax.fori_loop(0, filled, per_tile, 0)


def backward_kernel(step, layers, heads, head_dim, counts, *refs):
    q, g, turned_q, turned_g, final = refs[:5]
    refs = refs[5:]
    kinds = kinds_of(step, layers)
    count = len(kinds)
    pairs, refs = refs[:count], refs[count:]
    earlier = None
    if step < layers:
        earlier, refs = refs[0], refs[1:]
    if step == layers - 1:
        stay, leave = refs[:2]
        refs = refs[2:]
    made = 3 if step == layers else count
    grads, query_out, refs = refs[:made], refs[made], refs[made + 1 :]
    keys, values, turned, probs_held, scores_held, sums = refs
    place = lax.axis_index("ctx")
    members, all_rows = q.shape[:2]
    tile = tile_of(all_rows)
    tokens = all_rows // heads
    plain = head_dim**-0.5
    scale = plain * math.log2(math.e)
    edges = edges_of(counts)
    attended = attends(step, layers, place)

    def body(member, low, high, first, span):
        whole = pl.ds(first, span)
        held_rows = slice(0, span)
        total = final[member, TOTAL : TOTAL + 1, whole]
        level = final[member, TOP : TOP + 1, whole] + jnp.log2(total)
        delta = final[member, DOTTED : DOTTED + 1, whole] / total
        for start in range(0, span, SUB_ROWS):
            rows = pl.ds(row_start(first, start), SUB_ROWS)
            held = slice(start, start + SUB_ROWS)
            scores = dot(keys[low:high, :], turned_q[member, :, rows]) * scale
            scores = scores - level[:, held]
            if step == 0:
                kept = kept_keys(scores.shape, first + start, heads)
                scores = jnp.where(kept, scores, MASKED)
            probs = jnp.exp2(scores)
            grad_probs = dot(values[low:high, :], turned_g[member, :, rows])
            grad_scores = probs * (grad_probs - delta[:, held])
            probs_held[low:high, held] = probs.astype(jnp.bfloat16)
            scores_held[low:high, held] = grad_scores.astype(jnp.bfloat16)
        sums[low:high, head_dim:] += dot(probs_held[low:high, held_rows], g[member, whole, :])
        sums[low:high, :head_dim] += dot(scores_held[low:high, held_rows], q[member, whole, :])
        moved = dot(turned[:, low:high], scores_held[low:high, held_rows])
        if earlier is not None:
            moved = moved + earlier[member, :, whole]
        if step == 0:
            query_out[member, whole, :] = (moved * plain).T.astype(jnp.bfloat16)
        else:
            query_out[member, :, whole] = moved

    def per_member(member, carry):
        filled = filled_tiles(length_of(final, member), tokens, heads, all_rows)
        filled = jnp.where(attended, filled, 0)
        for part in range(count):
            rows = pl.ds(edges[part], edges[part + 1] - edges[part])

            @pl.when((member == 0) | (kinds[part] != "prompt"))
            def _():
                sums[rows, :] = jnp.zeros_like(sums[rows, :])

        @pl.when(filled > 0)
        def _():
            load_keys(member, pairs, kinds, edges, head_dim, keys, values)
            turned[...] = keys[...].T

            for condition, begin, past in variants(step, layers, place):
                low, high = edges[begin], edges[past]

                @pl.when(True if condition is None else condition)
                def _():
                    over_tiles(filled, all_rows, functools.partial(body, member, low, high), 0)

        if step == 0 or earlier is None:

            def clear(index, carry):
                rows = pl.ds(pl.multiple_of(index * tile, tile), tile)
                if step == 0:
                    query_out[member, rows, :] = jnp.zeros((tile, head_dim), jnp.bfloat16)
                else:
                    query_out[member, :, rows] = jnp.zeros((head_dim, tile), jnp.float32)
                return carry

            lax.fori_loop(filled, all_rows // tile, clear, 0)
        for part in range(count):
            if kinds[part] == "prompt":
                continue
            rows = pl.ds(edges[part], counts[part])
            own = pl.ds(pl.multiple_of(member * counts[part], counts[part]), counts[part])
            key_part, value_part = sums[rows, :head_dim] * plain, sums[rows, head_dim:]
            grads[part][own, :head_dim] = key_part.astype(jnp.bfloat16)
            grads[part][own, head_dim:] = value_part.astype(jnp.bfloat16)
        return carry

    lax.fori_loop(0, members, per_member, 0)
    tail = members * tokens
    if step == layers:
        far, stay, leave = grads
        middle = edges[1] + stay.shape[0]
        last = middle + leave.shape[0]
        for target, begin, rows in (
            (stay, 0, slice(edges[1], middle)),
            (leave, 0, slice(middle, last)),
            (far, tail, slice(last, edges[2])),
        ):
            end = target.shape[0]
            target[begin:end, :head_dim] = (sums[rows, :head_dim] * plain).astype(target.dtype)
            target[begin:end, head_dim:] = sums[rows, head_dim:].astype(target.dtype)
    elif step == layers - 1:
        grads[0][tail:, :] = leave[...]
        grads[1][tail:, :] = stay[leave.shape[0] :, :].astype(jnp.bfloat16)


def combine_kernel(step, layers, each, own, side, above, *refs):
    def wide(ref, rows):
        return ref[rows, :].astype(jnp.float32)

    count = own.shape[0]
    rows = slice(0, count)
    total = wide(own, rows) + wide(side, rows) + wide(above, rows)
    if step == 0:
        key_out, value_out = refs
        total = total.astype(jnp.bfloat16)
        head_dim = key_out.shape[1]
        key_out[...] = total[:, :head_dim]
        value_out[...] = total[:, head_dim:]
        return
    kept, *refs = refs
    if step == 1:
        crossing, far, *refs = refs
    out, *refs = refs
    mine = slice(step * each, (step + 1) * each)
    prompt = kept[mine, :] + wide(above, slice(count, None))
    if step == layers - 2:
        prompt = prompt + wide(side, slice(count + mine.start, count + mine.stop))
        still_kept, *refs = refs
        still_kept[...] = kept[: step * each, :] + wide(side, slice(count, count + step * each))
    out[rows, :] = total.astype(jnp.bfloat16)
    out[count:, :] = prompt.astype(jnp.bfloat16)
    if step == 1:
        (leaving,) = refs
        leaving[rows, :] = (wide(crossing, rows) + wide(far, rows)).astype(jnp.bfloat16)
        leaving[count:, :] = far[count:, :]


def tile_of(rows):
    return min(TILE_ROWS, rows)


WHOLE = pl.BlockSpec(memory_space=pltpu.VMEM)
PARAMS = pltpu.CompilerParams(vmem_limit_bytes=VMEM_BYTES)
LITTLE = pl.CostEstimate(flops=1000, bytes_accessed=1000, transcendentals=0)


OUTSIDE = pl.BlockSpec(memory_space=pltpu.HBM)


def prepare(heads, policy, q, g):
    members, rows, head_dim = q.shape
    turned = jax.ShapeDtypeStruct((members, head_dim, rows), q.dtype)
    return pl.pallas_call(
        functools.partial(prepare_kernel, heads),
        in_specs=[WHOLE] + [OUTSIDE] * 2,
        out_specs=[WHOLE] * 5,
        out_shape=[jax.ShapeDtypeStruct((members, 8, rows), jnp.float32)]
        + [jax.ShapeDtypeStruct(q.shape, q.dtype)] * 2
        + [turned] * 2,
        scratch_shapes=[pltpu.SemaphoreType.DMA((2,))],
        compiler_params=PARAMS,
        cost_estimate=LITTLE,
        name="prepare_rows",
    )(policy, q, g)


def forward_step(step, layers, heads, tokens, turned, earlier, messages):
    members, head_dim, rows = turned[0].shape
    each = messages[0].shape[0] - members * tokens
    counts = [tokens] * len(kinds_of(step, layers))
    out_shape = [jax.ShapeDtypeStruct((members, 8, rows), jnp.float32)]
    if step == layers:
        counts[1] = 2 * layers * each
        out_shape.append(jax.ShapeDtypeStruct((counts[1], 2 * head_dim), jnp.bfloat16))
    return pl.pallas_call(
        functools.partial(forward_kernel, step, layers, heads, head_dim, counts),
        in_specs=[WHOLE] * (3 + len(messages)),
        out_specs=[WHOLE] * len(out_shape),
        out_shape=out_shape,
        scratch_shapes=[pltpu.VMEM((sum(counts), head_dim), jnp.bfloat16)] * 2,
        compiler_params=PARAMS,
        cost_estimate=LITTLE,
        input_output_aliases={2: 0},
        name=f"attend_step{step}",
    )(*turned, earlier, *messages)


def backward_step(
    step, layers, heads, tokens, each, held_rows, final, messages, earlier, prompt_terms
):
    q = held_rows[0]
    members, rows, head_dim = q.shape
    counts = [tokens] * len(kinds_of(step, layers))

    def block(more, dtype=jnp.bfloat16, base=members * tokens):
        return jax.ShapeDtypeStruct((base + more, 2 * head_dim), dtype)

    if step == layers:
        counts[1] = 2 * layers * each
        grad_shapes = [
            block(each),
            block(layers * each, jnp.float32, 0),
            block((layers - 1) * each, jnp.bfloat16, 0),
        ]
    elif step == layers - 1:
        grad_shapes = [block((layers - 1) * each), block(each)]
    else:
        grad_shapes = [block(0)] * len(counts)
    columns = sum(counts)
    if step == 0:
        query_shape = jax.ShapeDtypeStruct(q.shape, jnp.bfloat16)
    else:
        query_shape = jax.ShapeDtypeStruct((members, head_dim, rows), jnp.float32)
    extra = [] if earlier is None else [earlier]
    aliases = {5 + len(messages): len(grad_shapes)} if extra and step > 0 else {}
    extra += prompt_terms
    outs = pl.pallas_call(
        functools.partial(backward_kernel, step, layers, heads, head_dim, counts),
        in_specs=[WHOLE] * (5 + len(messages) + len(extra)),
        out_specs=[WHOLE] * (len(grad_shapes) + 1),
        out_shape=grad_shapes + [query_shape],
        scratch_shapes=[pltpu.VMEM((columns, head_dim), jnp.bfloat16)] * 2
        + [pltpu.VMEM((head_dim, columns), jnp.bfloat16)]
        + [pltpu.VMEM((columns, tile_of(rows)), jnp.bfloat16)] * 2
        + [pltpu.VMEM((columns, 2 * head_dim), jnp.float32)],
        compiler_params=PARAMS,
        cost_estimate=LITTLE,
        input_output_aliases=aliases,
        name=f"attend_grad_step{step}",
    )(*held_rows, final, *messages, *extra)
    return outs[:-1], outs[-1]


def combine(step, layers, each, *terms):
    count, width = terms[0].shape
    message = jax.ShapeDtypeStruct((count + each, width), jnp.bfloat16)
    if step == 0:
        shapes = [jax.ShapeDtypeStruct((count, width // 2), jnp.bfloat16)] * 2
    else:
        shapes = [message]
        if step == layers - 2:
            shapes.append(jax.ShapeDtypeStruct((step * each, width), jnp.float32))
        if step == 1:
            shapes.append(message)
    return pl.pallas_call(
        functools.partial(combine_kernel, step, layers, each),
        in_specs=[WHOLE] * len(terms),
        out_specs=[WHOLE] * len(shapes),
        out_shape=shapes,
        compiler_params=PARAMS,
        cost_estimate=LITTLE,
        name=f"add_terms{step}",
    )(*terms)


def join_kernel(
    keys, values, prompt_keys, prompt_values, behaved, current, advantages, lengths, *refs
):
    out, policy, held_behaved, held_current, held_advantages, held_lengths, arrived = refs
    rows, head_dim = keys.shape
    members, tokens = behaved.shape

    def part(first, count, column):
        return out.at[pl.ds(first, count), pl.ds(column, head_dim)]

    each = prompt_keys.shape[0]
    targets = [
        (keys, part(0, rows, 0)),
        (values, part(0, rows, head_dim)),
        (prompt_keys, part(rows, each, 0)),
        (prompt_values, part(rows, each, head_dim)),
        (behaved, held_behaved),
        (current, held_current),
        (advantages, held_advantages),
        (lengths, held_lengths),
    ]
    copies = [
        pltpu.make_async_copy(source, target, arrived.at[i])
        for i, (source, target) in enumerate(targets)
    ]
    for copy in copies:
        copy.start()
    for copy in copies:
        copy.wait()
    full_len = tokens * lax.axis_size("ctx")
    position = lax.axis_index("ctx") * tokens + lax.broadcasted_iota(jnp.int32, (1, tokens), 1)
    ratio = jnp.minimum(jnp.exp(held_current[...] - held_behaved[...]), RATIO_CAP)
    for member in range(members):
        length = held_lengths[member]
        spread = full_len / jnp.full((1, 1), length).astype(jnp.float32)
        valid = jnp.where(position < length, ratio[member : member + 1], 0.0)
        policy[member : member + 1, :] = -held_advantages[member] * valid * spread
        wide = jnp.full((1, tokens), length).astype(jnp.float32)
        policy[members + member : members + member + 1, :] = wide


def join(keys, values, prompt_keys, prompt_values, behaved, current, advantages, lengths):
    rows = keys.shape[0] + prompt_keys.shape[0]
    members, tokens = behaved.shape
    return pl.pallas_call(
        join_kernel,
        out_shape=[
            jax.ShapeDtypeStruct((rows, 2 * keys.shape[1]), keys.dtype),
            jax.ShapeDtypeStruct((2 * members, tokens), jnp.float32),
        ],
        in_specs=[OUTSIDE] * 8,
        out_specs=[WHOLE] * 2,
        scratch_shapes=[
            pltpu.VMEM((members, tokens), jnp.float32),
            pltpu.VMEM((members, tokens), jnp.float32),
            pltpu.SMEM((members,), jnp.float32),
            pltpu.SMEM((members,), jnp.int32),
            pltpu.SemaphoreType.DMA((8,)),
        ],
        compiler_params=pltpu.CompilerParams(vmem_limit_bytes=JOIN_VMEM_BYTES),
        cost_estimate=LITTLE,
        name="join_pairs",
    )(keys, values, prompt_keys, prompt_values, behaved, current, advantages, lengths)


def per_device(
    queries,
    prompt_keys,
    prompt_values,
    resp_keys,
    resp_values,
    upstream,
    behav_logp,
    cur_logp,
    advantages,
    lengths,
):
    members, tokens, heads, head_dim = queries.shape
    ctx_size, resp_size = lax.axis_size("ctx"), lax.axis_size("resp")
    layers = ctx_size // 2
    each = prompt_keys.shape[0]
    rows = tokens * heads

    def hop(array, layers_up):
        pairs = [(c, (c + 2 * layers_up) % ctx_size) for c in range(ctx_size)]
        return lax.ppermute(array, "ctx", pairs)

    def cross(array):
        return lax.ppermute(array, "ctx", [(c, c ^ 1) for c in range(ctx_size)])

    own, policy = join(
        resp_keys.reshape(members * tokens, head_dim),
        resp_values.reshape(members * tokens, head_dim),
        prompt_keys,
        prompt_values,
        behav_logp,
        cur_logp,
        advantages,
        lengths,
    )
    z, x = [own, hop(own, 1)], [None, cross(own)]
    stat, *held_rows = prepare(
        heads,
        policy,
        queries.reshape(members, rows, head_dim),
        upstream.reshape(members, rows, head_dim),
    )

    def forward(step, stat, messages):
        return forward_step(step, layers, heads, tokens, held_rows[2:], stat, messages)

    for step in range(1, layers):
        z[step], stat = lax.optimization_barrier((z[step], stat))
        if step + 1 < layers:
            z.append(hop(z[step], 1))
            x.append(cross(z[step]))
        else:
            x.append(hop(x[1], layers - 1))
        if step == 1:
            (stat,) = forward(0, stat, z[:1])
        (stat,) = forward(step, stat, [x[step], z[step]])
    stat, prompt = forward(layers, stat, z + x[1:])
    final = stat
    moved = side = above = far = message = kept = None
    terms = []
    for step in range(layers, -1, -1):
        if message is not None:
            final, message = lax.optimization_barrier((final, message))
            above = hop(message, -1)
        if step == layers:
            messages = [x[step], prompt]
        else:
            messages = [z[0]] if step == 0 else [x[step], z[step]]
        grads, moved = backward_step(
            step, layers, heads, tokens, each, held_rows, final, messages, moved, terms
        )
        terms = []
        if step == layers:
            far, terms = hop(grads[0], 1 - layers), list(grads[1:])
            kept = grads[1]
        elif step == layers - 1:
            message = grads[1]
        elif step > 0:
            crossing = [grads[0], far] if step == 1 else []
            message, *more = combine(
                step, layers, each, grads[-1], side, above, kept, *crossing
            )
            if step == layers - 2:
                kept, *more = more
            if step == 1:
                grads = more
        if 0 < step < layers:
            side = cross(grads[0])
    above, side, last = lax.optimization_barrier((above, side, grads[-1]))
    share = kept[:each]
    for term in (above, side):
        share = share + term[-each:].astype(jnp.float32)
    key_grads, value_grads = combine(0, layers, each, last, side, above)
    if resp_size <= 4:
        shares = [
            lax.ppermute(share, "resp", [(c, c ^ i) for c in range(resp_size)])
            for i in range(1, resp_size)
        ]
        share = functools.reduce(jnp.add, shares, share)
    else:
        stride = 1
        while stride < resp_size:
            pairs = [(c, c ^ stride) for c in range(resp_size)]
            share = share + lax.ppermute(share, "resp", pairs)
            stride *= 2
    return (
        moved.reshape(queries.shape),
        key_grads.reshape(resp_keys.shape),
        value_grads.reshape(resp_values.shape),
        share[:, :head_dim],
        share[:, head_dim:],
    )


def solution(mesh):
    placed = (
        P("resp", "ctx", None, None),
        P("ctx", None),
        P("ctx", None),
        P("resp", "ctx", None),
        P("resp", "ctx", None),
        P("resp", "ctx", None, None),
        P("resp", "ctx"),
        P("resp", "ctx"),
        P("resp"),
        P("resp"),
    )
    return jax.shard_map(
        per_device,
        mesh=mesh,
        in_specs=placed,
        out_specs=(
            P("resp", "ctx", None, None),
            P("resp", "ctx", None),
            P("resp", "ctx", None),
            P("ctx", None),
            P("ctx", None),
        ),
        check_vma=False,
    )
```

```python
import functools
import math

import jax
import jax.numpy as jnp
from jax import lax
from jax.experimental import pallas as pl
from jax.experimental.pallas import tpu as pltpu
from jax.sharding import PartitionSpec as P

RATIO_CAP = 2.0
MASKED = -1e30
SUB_ROWS = 256
TILE_ROWS = 1024
LARGEST_SCORE = 100.0
UNBOUNDED = 3e38

TOP, TOTAL, DOTTED, GUARD, WEIGHT, LENGTH = range(6)
VMEM_BYTES = 24 * 1024 * 1024
JOIN_VMEM_BYTES = 60 * 1024 * 1024

def dot(a, b):
    return jnp.dot(a, b, preferred_element_type=jnp.float32)


def kinds_of(step, layers):
    if step == 0:
        return ("z",)
    return ("x", "prompt") if step == layers else ("x", "z")


def variants(step, layers, place):
    z, odd = place // 2, place % 2 == 1
    if step == 0:
        return [(None, 0, 1)]
    if step == layers:
        return [(z >= step - 1, 0, 2), (z < step - 1, 1, 2)]
    if step == 1:
        return [
            ((z >= 1) & odd, 0, 2),
            ((z == 0) & odd, 0, 1),
            ((z >= 1) & jnp.logical_not(odd), 1, 2),
        ]
    return [(z >= step, 0, 2), (z == step - 1, 0, 1)]


def attends(step, layers, place):
    if step in (0, layers):
        return place >= 0
    return place >= 1 if step == 1 else place // 2 >= step - 1


def kept_keys(shape, first_row, heads):
    key = lax.broadcasted_iota(jnp.int32, shape, 0)
    row = lax.broadcasted_iota(jnp.int32, shape, 1) + first_row
    return key * heads <= row


def edges_of(counts):
    edges = [0]
    for count in counts:
        edges.append(edges[-1] + count)
    return edges


def largest_norm(rows):
    wide = rows.astype(jnp.float32)
    return jnp.max(jnp.sum(wide * wide, axis=1, keepdims=True))


def filled_tiles(length, tokens, heads, rows):
    per_tile = tile_of(rows) // heads
    left = length - lax.axis_index("ctx") * tokens
    return jnp.clip((left + per_tile - 1) // per_tile, 0, rows // tile_of(rows))


def load_keys(member, pairs, kinds, edges, head_dim, keys, values):
    for part, pair in enumerate(pairs):
        count = edges[part + 1] - edges[part]
        rows = pl.ds(edges[part], count)
        own = pl.ds(0, count)
        if kinds[part] != "prompt":
            own = pl.ds(pl.multiple_of(member * count, count), count)
        keys[rows, :] = pair[own, :head_dim]
        values[rows, :] = pair[own, head_dim:]


def length_of(stat, member):
    return jnp.max(stat[member, LENGTH : LENGTH + 1, 0:128]).astype(jnp.int32)


def spread_weights(ratio, heads):
    tokens = ratio.shape[1]
    shape = (tokens, tokens * heads)
    token = lax.broadcasted_iota(jnp.int32, shape, 0)
    row = lax.broadcasted_iota(jnp.int32, shape, 1)
    first = token * heads
    chosen = jnp.where((row >= first) & (row < first + heads), 1.0, 0.0)
    chosen = chosen.astype(jnp.bfloat16)
    out, rest = None, ratio
    for _ in range(3):
        term = rest.astype(jnp.bfloat16)
        rest = rest - term.astype(jnp.float32)
        few = jnp.broadcast_to(term.astype(jnp.float32), (16, tokens)).astype(jnp.bfloat16)
        part = jnp.dot(few, chosen, preferred_element_type=jnp.float32)[0:1]
        out = part if out is None else out + part
    return out


def key_sum(array):
    count = array.shape[0] // 4
    parts = [
        jnp.sum(array[i * count : (i + 1) * count], axis=0, keepdims=True) for i in range(4)
    ]
    return (parts[0] + parts[1]) + (parts[2] + parts[3])


def prepare_kernel(heads, policy, held_q, held_g, out, q, g, turned_q, turned_g, arrived):
    copies = [
        pltpu.make_async_copy(source, target, arrived.at[i])
        for i, (source, target) in enumerate([(held_q, q), (held_g, g)])
    ]
    for copy in copies:
        copy.start()
    for copy in copies:
        copy.wait()
    members, all_rows, _ = q.shape
    tile = tile_of(all_rows)
    tokens = all_rows // heads
    line = lax.broadcasted_iota(jnp.int32, policy.shape, 0)

    def per_member(member, carry):
        known = jnp.max(jnp.where(line == members + member, policy[...], 0.0))
        out[member, LENGTH : LENGTH + 1, :] = jnp.full((1, all_rows), known)

        def per_tile(index, carry):
            rows = pl.ds(pl.multiple_of(index * tile, tile), tile)
            turned_q[member, :, rows] = q[member, rows, :].T
            turned_g[member, :, rows] = g[member, rows, :].T
            guard = largest_norm(q[member, rows, :])
            out[member, GUARD : GUARD + 1, rows] = jnp.full((1, tile), guard)
            count = tile // heads
            part = pl.ds(pl.multiple_of(index * count, count), count)
            if count == tokens:
                part = pl.ds(0, count)
            chosen = jnp.where(line[:, :count] == member, policy[:, part], 0.0)
            ratio = jnp.sum(chosen, axis=0, keepdims=True)
            out[member, WEIGHT : WEIGHT + 1, rows] = spread_weights(ratio, heads)
            return carry

        filled = filled_tiles(known.astype(jnp.int32), tokens, heads, all_rows)
        lax.fori_loop(0, filled, per_tile, 0)
        return carry

    lax.fori_loop(0, members, per_member, 0)


def forward_kernel(step, layers, heads, head_dim, counts, turned_q, turned_g, earlier, *refs):
    kinds = kinds_of(step, layers)
    parts = len(kinds)
    if step == layers:
        messages, (out, prompt, keys, values) = refs[: 2 * layers], refs[2 * layers :]
        own = messages[0].shape[0] - prompt.shape[0] // (2 * layers)
        each = messages[0].shape[0] - own
        for i, message in enumerate(messages):
            prompt[i * each : (i + 1) * each, :] = message[own:, :]
        pairs = [messages[-1], prompt]
    else:
        pairs, (out, keys, values) = refs[:parts], refs[parts:]
    place = lax.axis_index("ctx")
    members, _, all_rows = turned_q.shape
    tile = tile_of(all_rows)
    tokens = all_rows // heads
    scale = head_dim**-0.5 * math.log2(math.e)
    edges = edges_of(counts)
    attended = attends(step, layers, place)

    def shared(member, low, high, first, start):
        rows = pl.ds(row_start(first, start), SUB_ROWS)
        scores = dot(keys[low:high, :], turned_q[member, :, rows]) * scale
        if step == 0:
            kept = kept_keys(scores.shape, first + start, heads)
            scores = jnp.where(kept, scores, MASKED)
        return rows, scores, dot(values[low:high, :], turned_g[member, :, rows])

    def put(member, first, span, lines):
        rows = pl.ds(first, span)
        for line, pieces in lines.items():
            out[member, line : line + 1, rows] = jnp.concatenate(pieces, 1)

    def bounded(member, low, high, first, span):
        totals, dots = [], []
        for start in range(0, span, SUB_ROWS):
            rows, scores, grad_probs = shared(member, low, high, first, start)
            weight = jnp.exp2(scores)
            total, dotted = key_sum(weight), key_sum(weight * grad_probs)
            if step > 0:
                total = total + earlier[member, TOTAL : TOTAL + 1, rows]
                dotted = dotted + earlier[member, DOTTED : DOTTED + 1, rows]
            totals.append(total)
            dots.append(dotted)
        tops = [jnp.zeros_like(t) for t in totals]
        put(member, first, span, {TOP: tops, TOTAL: totals, DOTTED: dots})

    def general(member, low, high, first, span):
        tops, totals, dots = [], [], []
        for start in range(0, span, SUB_ROWS):
            rows, scores, grad_probs = shared(member, low, high, first, start)
            top = jnp.max(scores, axis=0, keepdims=True)
            if step > 0:
                top = jnp.maximum(top, earlier[member, TOP : TOP + 1, rows])
            weight = jnp.exp2(scores - top)
            total, dotted = key_sum(weight), key_sum(weight * grad_probs)
            if step > 0:
                decay = jnp.exp2(earlier[member, TOP : TOP + 1, rows] - top)
                total = total + decay * earlier[member, TOTAL : TOTAL + 1, rows]
                dotted = dotted + decay * earlier[member, DOTTED : DOTTED + 1, rows]
            tops.append(top)
            totals.append(total)
            dots.append(dotted)
        guards = [jnp.full_like(t, UNBOUNDED) for t in totals]
        put(member, first, span, {TOP: tops, TOTAL: totals, DOTTED: dots, GUARD: guards})

    def per_member(member, carry):
        filled = filled_tiles(length_of(earlier, member), tokens, heads, all_rows)

        @pl.when((filled > 0) & attended)
        def _():
            load_keys(member, pairs, kinds, edges, head_dim, keys, values)
            limit = (LARGEST_SCORE / scale) ** 2 / largest_norm(keys[...])
            guards = earlier[member, GUARD : GUARD + 1, :]
            column = lax.broadcasted_iota(jnp.int32, guards.shape, 1)
            fast = jnp.max(jnp.where(column < filled * tile, guards, 0.0)) <= limit
            for condition, begin, past in variants(step, layers, place):
                low, high = edges[begin], edges[past]
                here = True if condition is None else condition

                @pl.when(fast & here)
                def _():
                    over_tiles(filled, all_rows, functools.partial(bounded, member, low, high))

                @pl.when(jnp.logical_not(fast) & here)
                def _():
                    over_tiles(filled, all_rows, functools.partial(general, member, low, high), 0)

        return carry

    lax.fori_loop(0, members, per_member, 0)


def row_start(first, start):
    if isinstance(first, int):
        return first + start
    return pl.multiple_of(first + start, SUB_ROWS)


def over_tiles(filled, all_rows, body, whole=1):
    tile = tile_of(all_rows)
    tiles = all_rows // tile

    def per_tile(index, carry):
        body(pl.multiple_of(index * tile, tile), tile)
        return carry

    if tiles == 1 or not whole:
        lax.fori_loop(0, filled, per_tile, 0)
        return

    @pl.when(filled == tiles)
    def _():
        body(0, all_rows)

    @pl.when(filled < tiles)
    def _():
        lax.fori_loop(0, filled, per_tile, 0)


def backward_kernel(step, layers, heads, head_dim, counts, *refs):
    q, g, turned_q, turned_g, final = refs[:5]
    refs = refs[5:]
    kinds = kinds_of(step, layers)
    count = len(kinds)
    pairs, refs = refs[:count], refs[count:]
    earlier = None
    if step < layers:
        earlier, refs = refs[0], refs[1:]
    if step == layers - 1:
        stay, leave = refs[:2]
        refs = refs[2:]
    made = 3 if step == layers else count
    grads, query_out, refs = refs[:made], refs[made], refs[made + 1 :]
    keys, values, turned, probs_held, scores_held, sums = refs
    place = lax.axis_index("ctx")
    members, all_rows = q.shape[:2]
    tile = tile_of(all_rows)
    tokens = all_rows // heads
    plain = head_dim**-0.5
    scale = plain * math.log2(math.e)
    edges = edges_of(counts)
    attended = attends(step, layers, place)

    def body(member, low, high, first, span):
        whole = pl.ds(first, span)
        held_rows = slice(0, span)
        total = final[member, TOTAL : TOTAL + 1, whole]
        level = final[member, TOP : TOP + 1, whole] + jnp.log2(total)
        delta = final[member, DOTTED : DOTTED + 1, whole] / total
        token_weight = final[member, WEIGHT : WEIGHT + 1, whole]
        for start in range(0, span, SUB_ROWS):
            rows = pl.ds(row_start(first, start), SUB_ROWS)
            held = slice(start, start + SUB_ROWS)
            scores = dot(keys[low:high, :], turned_q[member, :, rows]) * scale
            scores = scores - level[:, held]
            if step == 0:
                kept = kept_keys(scores.shape, first + start, heads)
                scores = jnp.where(kept, scores, MASKED)
            probs = jnp.exp2(scores) * token_weight[:, held]
            grad_probs = dot(values[low:high, :], turned_g[member, :, rows])
            grad_scores = probs * (grad_probs - delta[:, held])
            probs_held[low:high, held] = probs.astype(jnp.bfloat16)
            scores_held[low:high, held] = grad_scores.astype(jnp.bfloat16)
        sums[low:high, head_dim:] += dot(probs_held[low:high, held_rows], g[member, whole, :])
        sums[low:high, :head_dim] += dot(scores_held[low:high, held_rows], q[member, whole, :])
        moved = dot(turned[:, low:high], scores_held[low:high, held_rows])
        if earlier is not None:
            moved = moved + earlier[member, :, whole]
        if step == 0:
            query_out[member, whole, :] = (moved * plain).T.astype(jnp.bfloat16)
        else:
            query_out[member, :, whole] = moved

    def per_member(member, carry):
        filled = filled_tiles(length_of(final, member), tokens, heads, all_rows)
        filled = jnp.where(attended, filled, 0)
        for part in range(count):
            rows = pl.ds(edges[part], edges[part + 1] - edges[part])

            @pl.when((member == 0) | (kinds[part] != "prompt"))
            def _():
                sums[rows, :] = jnp.zeros_like(sums[rows, :])

        @pl.when(filled > 0)
        def _():
            load_keys(member, pairs, kinds, edges, head_dim, keys, values)
            turned[...] = keys[...].T

            for condition, begin, past in variants(step, layers, place):
                low, high = edges[begin], edges[past]

                @pl.when(True if condition is None else condition)
                def _():
                    over_tiles(filled, all_rows, functools.partial(body, member, low, high), 0)

        if step == 0 or earlier is None:

            def clear(index, carry):
                rows = pl.ds(pl.multiple_of(index * tile, tile), tile)
                if step == 0:
                    query_out[member, rows, :] = jnp.zeros((tile, head_dim), jnp.bfloat16)
                else:
                    query_out[member, :, rows] = jnp.zeros((head_dim, tile), jnp.float32)
                return carry

            lax.fori_loop(filled, all_rows // tile, clear, 0)
        for part in range(count):
            if kinds[part] == "prompt":
                continue
            rows = pl.ds(edges[part], counts[part])
            own = pl.ds(pl.multiple_of(member * counts[part], counts[part]), counts[part])
            key_part, value_part = sums[rows, :head_dim] * plain, sums[rows, head_dim:]
            grads[part][own, :head_dim] = key_part.astype(jnp.bfloat16)
            grads[part][own, head_dim:] = value_part.astype(jnp.bfloat16)
        return carry

    lax.fori_loop(0, members, per_member, 0)
    tail = members * tokens
    if step == layers:
        far, stay, leave = grads
        middle = edges[1] + stay.shape[0]
        last = middle + leave.shape[0]
        for target, begin, rows in (
            (stay, 0, slice(edges[1], middle)),
            (leave, 0, slice(middle, last)),
            (far, tail, slice(last, edges[2])),
        ):
            end = target.shape[0]
            target[begin:end, :head_dim] = (sums[rows, :head_dim] * plain).astype(target.dtype)
            target[begin:end, head_dim:] = sums[rows, head_dim:].astype(target.dtype)
    elif step == layers - 1:
        grads[0][tail:, :] = leave[...]
        grads[1][tail:, :] = stay[leave.shape[0] :, :].astype(jnp.bfloat16)


def combine_kernel(step, layers, each, own, side, above, *refs):
    def wide(ref, rows):
        return ref[rows, :].astype(jnp.float32)

    count = own.shape[0]
    rows = slice(0, count)
    total = wide(own, rows) + wide(side, rows) + wide(above, rows)
    if step == 0:
        key_out, value_out = refs
        total = total.astype(jnp.bfloat16)
        head_dim = key_out.shape[1]
        key_out[...] = total[:, :head_dim]
        value_out[...] = total[:, head_dim:]
        return
    kept, *refs = refs
    if step == 1:
        crossing, far, *refs = refs
    out, *refs = refs
    mine = slice(step * each, (step + 1) * each)
    prompt = kept[mine, :] + wide(above, slice(count, None))
    if step == layers - 2:
        prompt = prompt + wide(side, slice(count + mine.start, count + mine.stop))
        still_kept, *refs = refs
        still_kept[...] = kept[: step * each, :] + wide(side, slice(count, count + step * each))
    out[rows, :] = total.astype(jnp.bfloat16)
    out[count:, :] = prompt.astype(jnp.bfloat16)
    if step == 1:
        (leaving,) = refs
        leaving[rows, :] = (wide(crossing, rows) + wide(far, rows)).astype(jnp.bfloat16)
        leaving[count:, :] = far[count:, :]


def tile_of(rows):
    return min(TILE_ROWS, rows)


WHOLE = pl.BlockSpec(memory_space=pltpu.VMEM)
PARAMS = pltpu.CompilerParams(vmem_limit_bytes=VMEM_BYTES)
LITTLE = pl.CostEstimate(flops=1000, bytes_accessed=1000, transcendentals=0)


OUTSIDE = pl.BlockSpec(memory_space=pltpu.HBM)


def prepare(heads, policy, q, g):
    members, rows, head_dim = q.shape
    turned = jax.ShapeDtypeStruct((members, head_dim, rows), q.dtype)
    return pl.pallas_call(
        functools.partial(prepare_kernel, heads),
        in_specs=[WHOLE] + [OUTSIDE] * 2,
        out_specs=[WHOLE] * 5,
        out_shape=[jax.ShapeDtypeStruct((members, 8, rows), jnp.float32)]
        + [jax.ShapeDtypeStruct(q.shape, q.dtype)] * 2
        + [turned] * 2,
        scratch_shapes=[pltpu.SemaphoreType.DMA((2,))],
        compiler_params=PARAMS,
        cost_estimate=LITTLE,
        name="prepare_rows",
    )(policy, q, g)


def forward_step(step, layers, heads, tokens, turned, earlier, messages):
    members, head_dim, rows = turned[0].shape
    each = messages[0].shape[0] - members * tokens
    counts = [tokens] * len(kinds_of(step, layers))
    out_shape = [jax.ShapeDtypeStruct((members, 8, rows), jnp.float32)]
    if step == layers:
        counts[1] = 2 * layers * each
        out_shape.append(jax.ShapeDtypeStruct((counts[1], 2 * head_dim), jnp.bfloat16))
    return pl.pallas_call(
        functools.partial(forward_kernel, step, layers, heads, head_dim, counts),
        in_specs=[WHOLE] * (3 + len(messages)),
        out_specs=[WHOLE] * len(out_shape),
        out_shape=out_shape,
        scratch_shapes=[pltpu.VMEM((sum(counts), head_dim), jnp.bfloat16)] * 2,
        compiler_params=PARAMS,
        cost_estimate=LITTLE,
        input_output_aliases={2: 0},
        name=f"attend_step{step}",
    )(*turned, earlier, *messages)


def backward_step(
    step, layers, heads, tokens, each, held_rows, final, messages, earlier, prompt_terms
):
    q = held_rows[0]
    members, rows, head_dim = q.shape
    counts = [tokens] * len(kinds_of(step, layers))

    def block(more, dtype=jnp.bfloat16, base=members * tokens):
        return jax.ShapeDtypeStruct((base + more, 2 * head_dim), dtype)

    if step == layers:
        counts[1] = 2 * layers * each
        grad_shapes = [
            block(each),
            block(layers * each, jnp.float32, 0),
            block((layers - 1) * each, jnp.bfloat16, 0),
        ]
    elif step == layers - 1:
        grad_shapes = [block((layers - 1) * each), block(each)]
    else:
        grad_shapes = [block(0)] * len(counts)
    columns = sum(counts)
    if step == 0:
        query_shape = jax.ShapeDtypeStruct(q.shape, jnp.bfloat16)
    else:
        query_shape = jax.ShapeDtypeStruct((members, head_dim, rows), jnp.float32)
    extra = [] if earlier is None else [earlier]
    aliases = {5 + len(messages): len(grad_shapes)} if extra and step > 0 else {}
    extra += prompt_terms
    outs = pl.pallas_call(
        functools.partial(backward_kernel, step, layers, heads, head_dim, counts),
        in_specs=[WHOLE] * (5 + len(messages) + len(extra)),
        out_specs=[WHOLE] * (len(grad_shapes) + 1),
        out_shape=grad_shapes + [query_shape],
        scratch_shapes=[pltpu.VMEM((columns, head_dim), jnp.bfloat16)] * 2
        + [pltpu.VMEM((head_dim, columns), jnp.bfloat16)]
        + [pltpu.VMEM((columns, tile_of(rows)), jnp.bfloat16)] * 2
        + [pltpu.VMEM((columns, 2 * head_dim), jnp.float32)],
        compiler_params=PARAMS,
        cost_estimate=LITTLE,
        input_output_aliases=aliases,
        name=f"attend_grad_step{step}",
    )(*held_rows, final, *messages, *extra)
    return outs[:-1], outs[-1]


def combine(step, layers, each, *terms):
    count, width = terms[0].shape
    message = jax.ShapeDtypeStruct((count + each, width), jnp.bfloat16)
    if step == 0:
        shapes = [jax.ShapeDtypeStruct((count, width // 2), jnp.bfloat16)] * 2
    else:
        shapes = [message]
        if step == layers - 2:
            shapes.append(jax.ShapeDtypeStruct((step * each, width), jnp.float32))
        if step == 1:
            shapes.append(message)
    return pl.pallas_call(
        functools.partial(combine_kernel, step, layers, each),
        in_specs=[WHOLE] * len(terms),
        out_specs=[WHOLE] * len(shapes),
        out_shape=shapes,
        compiler_params=PARAMS,
        cost_estimate=LITTLE,
        name=f"add_terms{step}",
    )(*terms)


def join_kernel(
    keys, values, prompt_keys, prompt_values, behaved, current, advantages, lengths, *refs
):
    out, policy, held_behaved, held_current, held_advantages, held_lengths, arrived = refs
    rows, head_dim = keys.shape
    members, tokens = behaved.shape

    def part(first, count, column):
        return out.at[pl.ds(first, count), pl.ds(column, head_dim)]

    each = prompt_keys.shape[0]
    targets = [
        (keys, part(0, rows, 0)),
        (values, part(0, rows, head_dim)),
        (prompt_keys, part(rows, each, 0)),
        (prompt_values, part(rows, each, head_dim)),
        (behaved, held_behaved),
        (current, held_current),
        (advantages, held_advantages),
        (lengths, held_lengths),
    ]
    copies = [
        pltpu.make_async_copy(source, target, arrived.at[i])
        for i, (source, target) in enumerate(targets)
    ]
    for copy in copies:
        copy.start()
    for copy in copies:
        copy.wait()
    full_len = tokens * lax.axis_size("ctx")
    position = lax.axis_index("ctx") * tokens + lax.broadcasted_iota(jnp.int32, (1, tokens), 1)
    ratio = jnp.minimum(jnp.exp(held_current[...] - held_behaved[...]), RATIO_CAP)
    for member in range(members):
        length = held_lengths[member]
        spread = full_len / jnp.full((1, 1), length).astype(jnp.float32)
        valid = jnp.where(position < length, ratio[member : member + 1], 0.0)
        policy[member : member + 1, :] = -held_advantages[member] * valid * spread
        wide = jnp.full((1, tokens), length).astype(jnp.float32)
        policy[members + member : members + member + 1, :] = wide


def join(keys, values, prompt_keys, prompt_values, behaved, current, advantages, lengths):
    rows = keys.shape[0] + prompt_keys.shape[0]
    members, tokens = behaved.shape
    return pl.pallas_call(
        join_kernel,
        out_shape=[
            jax.ShapeDtypeStruct((rows, 2 * keys.shape[1]), keys.dtype),
            jax.ShapeDtypeStruct((2 * members, tokens), jnp.float32),
        ],
        in_specs=[OUTSIDE] * 8,
        out_specs=[WHOLE] * 2,
        scratch_shapes=[
            pltpu.VMEM((members, tokens), jnp.float32),
            pltpu.VMEM((members, tokens), jnp.float32),
            pltpu.SMEM((members,), jnp.float32),
            pltpu.SMEM((members,), jnp.int32),
            pltpu.SemaphoreType.DMA((8,)),
        ],
        compiler_params=pltpu.CompilerParams(vmem_limit_bytes=JOIN_VMEM_BYTES),
        cost_estimate=LITTLE,
        name="join_pairs",
    )(keys, values, prompt_keys, prompt_values, behaved, current, advantages, lengths)


def per_device(
    queries,
    prompt_keys,
    prompt_values,
    resp_keys,
    resp_values,
    upstream,
    behav_logp,
    cur_logp,
    advantages,
    lengths,
):
    members, tokens, heads, head_dim = queries.shape
    ctx_size, resp_size = lax.axis_size("ctx"), lax.axis_size("resp")
    layers = ctx_size // 2
    each = prompt_keys.shape[0]
    rows = tokens * heads

    def hop(array, layers_up):
        pairs = [(c, (c + 2 * layers_up) % ctx_size) for c in range(ctx_size)]
        return lax.ppermute(array, "ctx", pairs)

    def cross(array):
        return lax.ppermute(array, "ctx", [(c, c ^ 1) for c in range(ctx_size)])

    own, policy = join(
        resp_keys.reshape(members * tokens, head_dim),
        resp_values.reshape(members * tokens, head_dim),
        prompt_keys,
        prompt_values,
        behav_logp,
        cur_logp,
        advantages,
        lengths,
    )
    z, x = [own, hop(own, 1)], [None, cross(own)]
    stat, *held_rows = prepare(
        heads,
        policy,
        queries.reshape(members, rows, head_dim),
        upstream.reshape(members, rows, head_dim),
    )

    def forward(step, stat, messages):
        return forward_step(step, layers, heads, tokens, held_rows[2:], stat, messages)

    for step in range(1, layers):
        z[step], stat = lax.optimization_barrier((z[step], stat))
        if step + 1 < layers:
            z.append(hop(z[step], 1))
        x.append(cross(z[step]))
        if step == 1:
            (stat,) = forward(0, stat, z[:1])
        (stat,) = forward(step, stat, [x[step], z[step]])
    stat, prompt = forward(layers, stat, z + x[1:])
    final = stat
    moved = side = above = far = message = kept = None
    terms = []
    for step in range(layers, -1, -1):
        if message is not None:
            final, message = lax.optimization_barrier((final, message))
            above = hop(message, -1)
        if step == layers:
            messages = [x[step], prompt]
        else:
            messages = [z[0]] if step == 0 else [x[step], z[step]]
        grads, moved = backward_step(
            step, layers, heads, tokens, each, held_rows, final, messages, moved, terms
        )
        terms = []
        if step == layers:
            far, terms = hop(grads[0], 1 - layers), list(grads[1:])
            kept = grads[1]
        elif step == layers - 1:
            message = grads[1]
        elif step > 0:
            crossing = [grads[0], far] if step == 1 else []
            message, *more = combine(
                step, layers, each, grads[-1], side, above, kept, *crossing
            )
            if step == layers - 2:
                kept, *more = more
            if step == 1:
                grads = more
        if 0 < step < layers:
            side = cross(grads[0])
    above, side, last = lax.optimization_barrier((above, side, grads[-1]))
    share = kept[:each]
    for term in (above, side):
        share = share + term[-each:].astype(jnp.float32)
    key_grads, value_grads = combine(0, layers, each, last, side, above)
    if resp_size <= 4:
        shares = [
            lax.ppermute(share, "resp", [(c, c ^ i) for c in range(resp_size)])
            for i in range(1, resp_size)
        ]
        share = functools.reduce(jnp.add, shares, share)
    else:
        stride = 1
        while stride < resp_size:
            pairs = [(c, c ^ stride) for c in range(resp_size)]
            share = share + lax.ppermute(share, "resp", pairs)
            stride *= 2
    return (
        moved.reshape(queries.shape),
        key_grads.reshape(resp_keys.shape),
        value_grads.reshape(resp_values.shape),
        share[:, :head_dim],
        share[:, head_dim:],
    )


def solution(mesh):
    placed = (
        P("resp", "ctx", None, None),
        P("ctx", None),
        P("ctx", None),
        P("resp", "ctx", None),
        P("resp", "ctx", None),
        P("resp", "ctx", None, None),
        P("resp", "ctx"),
        P("resp", "ctx"),
        P("resp"),
        P("resp"),
    )
    return jax.shard_map(
        per_device,
        mesh=mesh,
        in_specs=placed,
        out_specs=(
            P("resp", "ctx", None, None),
            P("resp", "ctx", None),
            P("resp", "ctx", None),
            P("ctx", None),
            P("ctx", None),
        ),
        check_vma=False,
    )
```

```python
import functools
import math

import jax
import jax.numpy as jnp
from jax import lax
from jax.experimental import pallas as pl
from jax.experimental.pallas import tpu as pltpu
from jax.sharding import PartitionSpec as P

RATIO_CAP = 2.0
MASKED = -1e30
SUB_ROWS = 256
TILE_ROWS = 1024
LARGEST_SCORE = 100.0
UNBOUNDED = 3e38

TOP, TOTAL, DOTTED, GUARD, WEIGHT, LENGTH = range(6)
VMEM_BYTES = 24 * 1024 * 1024
JOIN_VMEM_BYTES = 60 * 1024 * 1024

def dot(a, b):
    return jnp.dot(a, b, preferred_element_type=jnp.float32)


def kinds_of(step, layers):
    if step == 0:
        return ("z",)
    return ("x", "prompt") if step == layers else ("x", "z")


def variants(step, layers, place):
    z, odd = place // 2, place % 2 == 1
    if step == 0:
        return [(None, 0, 1)]
    if step == layers:
        return [(z >= step - 1, 0, 2), (z < step - 1, 1, 2)]
    if step == 1:
        return [
            ((z >= 1) & odd, 0, 2),
            ((z == 0) & odd, 0, 1),
            ((z >= 1) & jnp.logical_not(odd), 1, 2),
        ]
    return [(z >= step, 0, 2), (z == step - 1, 0, 1)]


def attends(step, layers, place):
    if step in (0, layers):
        return place >= 0
    return place >= 1 if step == 1 else place // 2 >= step - 1


def kept_keys(shape, first_row, heads):
    key = lax.broadcasted_iota(jnp.int32, shape, 0)
    row = lax.broadcasted_iota(jnp.int32, shape, 1) + first_row
    return key * heads <= row


def edges_of(counts):
    edges = [0]
    for count in counts:
        edges.append(edges[-1] + count)
    return edges


def largest_norm(rows):
    wide = rows.astype(jnp.float32)
    return jnp.max(jnp.sum(wide * wide, axis=1, keepdims=True))


def filled_tiles(length, tokens, heads, rows):
    per_tile = tile_of(rows) // heads
    left = length - lax.axis_index("ctx") * tokens
    return jnp.clip((left + per_tile - 1) // per_tile, 0, rows // tile_of(rows))


def load_keys(member, pairs, kinds, edges, head_dim, keys, values):
    for part, pair in enumerate(pairs):
        count = edges[part + 1] - edges[part]
        rows = pl.ds(edges[part], count)
        own = pl.ds(0, count)
        if kinds[part] != "prompt":
            own = pl.ds(pl.multiple_of(member * count, count), count)
        keys[rows, :] = pair[own, :head_dim]
        values[rows, :] = pair[own, head_dim:]


def length_of(stat, member):
    return jnp.max(stat[member, LENGTH : LENGTH + 1, 0:128]).astype(jnp.int32)


def spread_weights(ratio, heads):
    tokens = ratio.shape[1]
    shape = (tokens, tokens * heads)
    token = lax.broadcasted_iota(jnp.int32, shape, 0)
    row = lax.broadcasted_iota(jnp.int32, shape, 1)
    first = token * heads
    chosen = jnp.where((row >= first) & (row < first + heads), 1.0, 0.0)
    chosen = chosen.astype(jnp.bfloat16)
    out, rest = None, ratio
    for _ in range(3):
        term = rest.astype(jnp.bfloat16)
        rest = rest - term.astype(jnp.float32)
        few = jnp.broadcast_to(term.astype(jnp.float32), (16, tokens)).astype(jnp.bfloat16)
        part = jnp.dot(few, chosen, preferred_element_type=jnp.float32)[0:1]
        out = part if out is None else out + part
    return out


def key_sum(array):
    count = array.shape[0] // 4
    parts = [
        jnp.sum(array[i * count : (i + 1) * count], axis=0, keepdims=True) for i in range(4)
    ]
    return (parts[0] + parts[1]) + (parts[2] + parts[3])


def prepare_kernel(heads, policy, held_q, held_g, out, q, g, turned_q, turned_g, arrived):
    copies = [
        pltpu.make_async_copy(source, target, arrived.at[i])
        for i, (source, target) in enumerate([(held_q, q), (held_g, g)])
    ]
    for copy in copies:
        copy.start()
    for copy in copies:
        copy.wait()
    members, all_rows, _ = q.shape
    tile = tile_of(all_rows)
    tokens = all_rows // heads
    line = lax.broadcasted_iota(jnp.int32, policy.shape, 0)

    def per_member(member, carry):
        known = jnp.max(jnp.where(line == members + member, policy[...], 0.0))
        out[member, LENGTH : LENGTH + 1, :] = jnp.full((1, all_rows), known)

        def per_tile(index, carry):
            rows = pl.ds(pl.multiple_of(index * tile, tile), tile)
            turned_q[member, :, rows] = q[member, rows, :].T
            turned_g[member, :, rows] = g[member, rows, :].T
            guard = largest_norm(q[member, rows, :])
            out[member, GUARD : GUARD + 1, rows] = jnp.full((1, tile), guard)
            count = tile // heads
            part = pl.ds(pl.multiple_of(index * count, count), count)
            if count == tokens:
                part = pl.ds(0, count)
            chosen = jnp.where(line[:, :count] == member, policy[:, part], 0.0)
            ratio = jnp.sum(chosen, axis=0, keepdims=True)
            out[member, WEIGHT : WEIGHT + 1, rows] = spread_weights(ratio, heads)
            return carry

        filled = filled_tiles(known.astype(jnp.int32), tokens, heads, all_rows)
        lax.fori_loop(0, filled, per_tile, 0)
        return carry

    lax.fori_loop(0, members, per_member, 0)


def forward_kernel(step, layers, heads, head_dim, counts, turned_q, turned_g, earlier, *refs):
    kinds = kinds_of(step, layers)
    parts = len(kinds)
    if step == layers:
        messages, (out, prompt, keys, values) = refs[: 2 * layers], refs[2 * layers :]
        own = messages[0].shape[0] - prompt.shape[0] // (2 * layers)
        each = messages[0].shape[0] - own
        for i, message in enumerate(messages):
            prompt[i * each : (i + 1) * each, :] = message[own:, :]
        pairs = [messages[-1], prompt]
    else:
        pairs, (out, keys, values) = refs[:parts], refs[parts:]
    place = lax.axis_index("ctx")
    members, _, all_rows = turned_q.shape
    tile = tile_of(all_rows)
    tokens = all_rows // heads
    scale = head_dim**-0.5 * math.log2(math.e)
    edges = edges_of(counts)
    attended = attends(step, layers, place)

    def shared(member, low, high, first, start):
        rows = pl.ds(row_start(first, start), SUB_ROWS)
        scores = dot(keys[low:high, :], turned_q[member, :, rows]) * scale
        if step == 0:
            kept = kept_keys(scores.shape, first + start, heads)
            scores = jnp.where(kept, scores, MASKED)
        return rows, scores, dot(values[low:high, :], turned_g[member, :, rows])

    def put(member, first, span, lines):
        rows = pl.ds(first, span)
        for line, pieces in lines.items():
            out[member, line : line + 1, rows] = jnp.concatenate(pieces, 1)

    def bounded(member, low, high, first, span):
        totals, dots = [], []
        for start in range(0, span, SUB_ROWS):
            rows, scores, grad_probs = shared(member, low, high, first, start)
            weight = jnp.exp2(scores)
            total, dotted = key_sum(weight), key_sum(weight * grad_probs)
            if step > 0:
                total = total + earlier[member, TOTAL : TOTAL + 1, rows]
                dotted = dotted + earlier[member, DOTTED : DOTTED + 1, rows]
            totals.append(total)
            dots.append(dotted)
        tops = [jnp.zeros_like(t) for t in totals]
        put(member, first, span, {TOP: tops, TOTAL: totals, DOTTED: dots})

    def general(member, low, high, first, span):
        tops, totals, dots = [], [], []
        for start in range(0, span, SUB_ROWS):
            rows, scores, grad_probs = shared(member, low, high, first, start)
            top = jnp.max(scores, axis=0, keepdims=True)
            if step > 0:
                top = jnp.maximum(top, earlier[member, TOP : TOP + 1, rows])
            weight = jnp.exp2(scores - top)
            total, dotted = key_sum(weight), key_sum(weight * grad_probs)
            if step > 0:
                decay = jnp.exp2(earlier[member, TOP : TOP + 1, rows] - top)
                total = total + decay * earlier[member, TOTAL : TOTAL + 1, rows]
                dotted = dotted + decay * earlier[member, DOTTED : DOTTED + 1, rows]
            tops.append(top)
            totals.append(total)
            dots.append(dotted)
        guards = [jnp.full_like(t, UNBOUNDED) for t in totals]
        put(member, first, span, {TOP: tops, TOTAL: totals, DOTTED: dots, GUARD: guards})

    def per_member(member, carry):
        filled = filled_tiles(length_of(earlier, member), tokens, heads, all_rows)

        @pl.when((filled > 0) & attended)
        def _():
            load_keys(member, pairs, kinds, edges, head_dim, keys, values)
            limit = (LARGEST_SCORE / scale) ** 2 / largest_norm(keys[...])
            guards = earlier[member, GUARD : GUARD + 1, :]
            column = lax.broadcasted_iota(jnp.int32, guards.shape, 1)
            fast = jnp.max(jnp.where(column < filled * tile, guards, 0.0)) <= limit
            for condition, begin, past in variants(step, layers, place):
                low, high = edges[begin], edges[past]
                here = True if condition is None else condition

                @pl.when(fast & here)
                def _():
                    over_tiles(filled, all_rows, functools.partial(bounded, member, low, high))

                @pl.when(jnp.logical_not(fast) & here)
                def _():
                    over_tiles(filled, all_rows, functools.partial(general, member, low, high), 0)

        return carry

    lax.fori_loop(0, members, per_member, 0)


def row_start(first, start):
    if isinstance(first, int):
        return first + start
    return pl.multiple_of(first + start, SUB_ROWS)


def over_tiles(filled, all_rows, body, whole=1):
    tile = tile_of(all_rows)
    tiles = all_rows // tile

    def per_tile(index, carry):
        body(pl.multiple_of(index * tile, tile), tile)
        return carry

    if tiles == 1 or not whole:
        lax.fori_loop(0, filled, per_tile, 0)
        return

    @pl.when(filled == tiles)
    def _():
        body(0, all_rows)

    @pl.when(filled < tiles)
    def _():
        lax.fori_loop(0, filled, per_tile, 0)


def backward_kernel(step, layers, heads, head_dim, counts, *refs):
    q, g, turned_q, turned_g, final = refs[:5]
    refs = refs[5:]
    kinds = kinds_of(step, layers)
    count = len(kinds)
    pairs, refs = refs[:count], refs[count:]
    earlier = None
    if step < layers:
        earlier, refs = refs[0], refs[1:]
    if step == layers - 1:
        stay, leave = refs[:2]
        refs = refs[2:]
    made = 3 if step == layers else count
    grads, query_out, refs = refs[:made], refs[made], refs[made + 1 :]
    keys, values, turned, probs_held, scores_held, sums = refs
    place = lax.axis_index("ctx")
    members, all_rows = q.shape[:2]
    tile = tile_of(all_rows)
    tokens = all_rows // heads
    plain = head_dim**-0.5
    scale = plain * math.log2(math.e)
    edges = edges_of(counts)
    attended = attends(step, layers, place)

    def body(member, low, high, first, span):
        whole = pl.ds(first, span)
        held_rows = slice(0, span)
        total = final[member, TOTAL : TOTAL + 1, whole]
        level = final[member, TOP : TOP + 1, whole] + jnp.log2(total)
        delta = final[member, DOTTED : DOTTED + 1, whole] / total
        token_weight = final[member, WEIGHT : WEIGHT + 1, whole]
        for start in range(0, span, SUB_ROWS):
            rows = pl.ds(row_start(first, start), SUB_ROWS)
            held = slice(start, start + SUB_ROWS)
            scores = dot(keys[low:high, :], turned_q[member, :, rows]) * scale
            scores = scores - level[:, held]
            if step == 0:
                kept = kept_keys(scores.shape, first + start, heads)
                scores = jnp.where(kept, scores, MASKED)
            probs = jnp.exp2(scores) * token_weight[:, held]
            grad_probs = dot(values[low:high, :], turned_g[member, :, rows])
            grad_scores = probs * (grad_probs - delta[:, held])
            probs_held[low:high, held] = probs.astype(jnp.bfloat16)
            scores_held[low:high, held] = grad_scores.astype(jnp.bfloat16)
        sums[low:high, head_dim:] += dot(probs_held[low:high, held_rows], g[member, whole, :])
        sums[low:high, :head_dim] += dot(scores_held[low:high, held_rows], q[member, whole, :])
        moved = dot(turned[:, low:high], scores_held[low:high, held_rows])
        if earlier is not None:
            moved = moved + earlier[member, :, whole]
        if step == 0:
            query_out[member, whole, :] = (moved * plain).T.astype(jnp.bfloat16)
        else:
            query_out[member, :, whole] = moved

    def per_member(member, carry):
        filled = filled_tiles(length_of(final, member), tokens, heads, all_rows)
        filled = jnp.where(attended, filled, 0)
        for part in range(count):
            rows = pl.ds(edges[part], edges[part + 1] - edges[part])

            @pl.when((member == 0) | (kinds[part] != "prompt"))
            def _():
                sums[rows, :] = jnp.zeros_like(sums[rows, :])

        @pl.when(filled > 0)
        def _():
            load_keys(member, pairs, kinds, edges, head_dim, keys, values)
            turned[...] = keys[...].T

            for condition, begin, past in variants(step, layers, place):
                low, high = edges[begin], edges[past]

                @pl.when(True if condition is None else condition)
                def _():
                    over_tiles(filled, all_rows, functools.partial(body, member, low, high), 0)

        if step == 0 or earlier is None:

            def clear(index, carry):
                rows = pl.ds(pl.multiple_of(index * tile, tile), tile)
                if step == 0:
                    query_out[member, rows, :] = jnp.zeros((tile, head_dim), jnp.bfloat16)
                else:
                    query_out[member, :, rows] = jnp.zeros((head_dim, tile), jnp.float32)
                return carry

            lax.fori_loop(filled, all_rows // tile, clear, 0)
        for part in range(count):
            if kinds[part] == "prompt":
                continue
            rows = pl.ds(edges[part], counts[part])
            own = pl.ds(pl.multiple_of(member * counts[part], counts[part]), counts[part])
            key_part, value_part = sums[rows, :head_dim] * plain, sums[rows, head_dim:]
            grads[part][own, :head_dim] = key_part.astype(jnp.bfloat16)
            grads[part][own, head_dim:] = value_part.astype(jnp.bfloat16)
        return carry

    lax.fori_loop(0, members, per_member, 0)
    tail = members * tokens
    if step == layers:
        far, stay, leave = grads
        middle = edges[1] + stay.shape[0]
        last = middle + leave.shape[0]
        for target, begin, rows in (
            (stay, 0, slice(edges[1], middle)),
            (leave, 0, slice(middle, last)),
            (far, tail, slice(last, edges[2])),
        ):
            end = target.shape[0]
            target[begin:end, :head_dim] = (sums[rows, :head_dim] * plain).astype(target.dtype)
            target[begin:end, head_dim:] = sums[rows, head_dim:].astype(target.dtype)
    elif step == layers - 1:
        grads[0][tail:, :] = leave[...]
        grads[1][tail:, :] = stay[leave.shape[0] :, :].astype(jnp.bfloat16)


def combine_kernel(step, layers, each, own, side, above, *refs):
    def wide(ref, rows):
        return ref[rows, :].astype(jnp.float32)

    count = own.shape[0]
    rows = slice(0, count)
    total = wide(own, rows) + wide(side, rows) + wide(above, rows)
    if step == 0:
        key_out, value_out = refs
        total = total.astype(jnp.bfloat16)
        head_dim = key_out.shape[1]
        key_out[...] = total[:, :head_dim]
        value_out[...] = total[:, head_dim:]
        return
    kept, *refs = refs
    if step == 1:
        crossing, far, *refs = refs
    out, *refs = refs
    mine = slice(step * each, (step + 1) * each)
    prompt = kept[mine, :] + wide(above, slice(count, None))
    if step == layers - 2:
        prompt = prompt + wide(side, slice(count + mine.start, count + mine.stop))
        still_kept, *refs = refs
        still_kept[...] = kept[: step * each, :] + wide(side, slice(count, count + step * each))
    out[rows, :] = total.astype(jnp.bfloat16)
    out[count:, :] = prompt.astype(jnp.bfloat16)
    if step == 1:
        (leaving,) = refs
        leaving[rows, :] = (wide(crossing, rows) + wide(far, rows)).astype(jnp.bfloat16)
        leaving[count:, :] = far[count:, :]


def tile_of(rows):
    return min(TILE_ROWS, rows)


WHOLE = pl.BlockSpec(memory_space=pltpu.VMEM)
PARAMS = pltpu.CompilerParams(vmem_limit_bytes=VMEM_BYTES)
LITTLE = pl.CostEstimate(flops=1000, bytes_accessed=1000, transcendentals=0)


OUTSIDE = pl.BlockSpec(memory_space=pltpu.HBM)


def prepare(heads, policy, q, g):
    members, rows, head_dim = q.shape
    turned = jax.ShapeDtypeStruct((members, head_dim, rows), q.dtype)
    return pl.pallas_call(
        functools.partial(prepare_kernel, heads),
        in_specs=[WHOLE] + [OUTSIDE] * 2,
        out_specs=[WHOLE] * 5,
        out_shape=[jax.ShapeDtypeStruct((members, 8, rows), jnp.float32)]
        + [jax.ShapeDtypeStruct(q.shape, q.dtype)] * 2
        + [turned] * 2,
        scratch_shapes=[pltpu.SemaphoreType.DMA((2,))],
        compiler_params=PARAMS,
        cost_estimate=LITTLE,
        name="prepare_rows",
    )(policy, q, g)


def forward_step(step, layers, heads, tokens, turned, earlier, messages):
    members, head_dim, rows = turned[0].shape
    each = messages[0].shape[0] - members * tokens
    counts = [tokens] * len(kinds_of(step, layers))
    out_shape = [jax.ShapeDtypeStruct((members, 8, rows), jnp.float32)]
    if step == layers:
        counts[1] = 2 * layers * each
        out_shape.append(jax.ShapeDtypeStruct((counts[1], 2 * head_dim), jnp.bfloat16))
    return pl.pallas_call(
        functools.partial(forward_kernel, step, layers, heads, head_dim, counts),
        in_specs=[WHOLE] * (3 + len(messages)),
        out_specs=[WHOLE] * len(out_shape),
        out_shape=out_shape,
        scratch_shapes=[pltpu.VMEM((sum(counts), head_dim), jnp.bfloat16)] * 2,
        compiler_params=PARAMS,
        cost_estimate=LITTLE,
        input_output_aliases={2: 0},
        name=f"attend_step{step}",
    )(*turned, earlier, *messages)


def backward_step(
    step, layers, heads, tokens, each, held_rows, final, messages, earlier, prompt_terms
):
    q = held_rows[0]
    members, rows, head_dim = q.shape
    counts = [tokens] * len(kinds_of(step, layers))

    def block(more, dtype=jnp.bfloat16, base=members * tokens):
        return jax.ShapeDtypeStruct((base + more, 2 * head_dim), dtype)

    if step == layers:
        counts[1] = 2 * layers * each
        grad_shapes = [
            block(each),
            block(layers * each, jnp.float32, 0),
            block((layers - 1) * each, jnp.bfloat16, 0),
        ]
    elif step == layers - 1:
        grad_shapes = [block((layers - 1) * each), block(each)]
    else:
        grad_shapes = [block(0)] * len(counts)
    columns = sum(counts)
    if step == 0:
        query_shape = jax.ShapeDtypeStruct(q.shape, jnp.bfloat16)
    else:
        query_shape = jax.ShapeDtypeStruct((members, head_dim, rows), jnp.float32)
    extra = [] if earlier is None else [earlier]
    aliases = {5 + len(messages): len(grad_shapes)} if extra and step > 0 else {}
    extra += prompt_terms
    outs = pl.pallas_call(
        functools.partial(backward_kernel, step, layers, heads, head_dim, counts),
        in_specs=[WHOLE] * (5 + len(messages) + len(extra)),
        out_specs=[WHOLE] * (len(grad_shapes) + 1),
        out_shape=grad_shapes + [query_shape],
        scratch_shapes=[pltpu.VMEM((columns, head_dim), jnp.bfloat16)] * 2
        + [pltpu.VMEM((head_dim, columns), jnp.bfloat16)]
        + [pltpu.VMEM((columns, tile_of(rows)), jnp.bfloat16)] * 2
        + [pltpu.VMEM((columns, 2 * head_dim), jnp.float32)],
        compiler_params=PARAMS,
        cost_estimate=LITTLE,
        input_output_aliases=aliases,
        name=f"attend_grad_step{step}",
    )(*held_rows, final, *messages, *extra)
    return outs[:-1], outs[-1]


def combine(step, layers, each, *terms):
    count, width = terms[0].shape
    message = jax.ShapeDtypeStruct((count + each, width), jnp.bfloat16)
    if step == 0:
        shapes = [jax.ShapeDtypeStruct((count, width // 2), jnp.bfloat16)] * 2
    else:
        shapes = [message]
        if step == layers - 2:
            shapes.append(jax.ShapeDtypeStruct((step * each, width), jnp.float32))
        if step == 1:
            shapes.append(message)
    return pl.pallas_call(
        functools.partial(combine_kernel, step, layers, each),
        in_specs=[WHOLE] * len(terms),
        out_specs=[WHOLE] * len(shapes),
        out_shape=shapes,
        compiler_params=PARAMS,
        cost_estimate=LITTLE,
        name=f"add_terms{step}",
    )(*terms)


def join_kernel(
    keys, values, prompt_keys, prompt_values, behaved, current, advantages, lengths, *refs
):
    out, policy, held_behaved, held_current, held_advantages, held_lengths, arrived = refs
    rows, head_dim = keys.shape
    members, tokens = behaved.shape

    def part(first, count, column):
        return out.at[pl.ds(first, count), pl.ds(column, head_dim)]

    each = prompt_keys.shape[0]
    targets = [
        (keys, part(0, rows, 0)),
        (values, part(0, rows, head_dim)),
        (prompt_keys, part(rows, each, 0)),
        (prompt_values, part(rows, each, head_dim)),
        (behaved, held_behaved),
        (current, held_current),
        (advantages, held_advantages),
        (lengths, held_lengths),
    ]
    copies = [
        pltpu.make_async_copy(source, target, arrived.at[i])
        for i, (source, target) in enumerate(targets)
    ]
    for copy in copies:
        copy.start()
    for copy in copies:
        copy.wait()
    full_len = tokens * lax.axis_size("ctx")
    position = lax.axis_index("ctx") * tokens + lax.broadcasted_iota(jnp.int32, (1, tokens), 1)
    ratio = jnp.minimum(jnp.exp(held_current[...] - held_behaved[...]), RATIO_CAP)
    for member in range(members):
        length = held_lengths[member]
        spread = full_len / jnp.full((1, 1), length).astype(jnp.float32)
        valid = jnp.where(position < length, ratio[member : member + 1], 0.0)
        policy[member : member + 1, :] = -held_advantages[member] * valid * spread
        wide = jnp.full((1, tokens), length).astype(jnp.float32)
        policy[members + member : members + member + 1, :] = wide


def join(keys, values, prompt_keys, prompt_values, behaved, current, advantages, lengths):
    rows = keys.shape[0] + prompt_keys.shape[0]
    members, tokens = behaved.shape
    return pl.pallas_call(
        join_kernel,
        out_shape=[
            jax.ShapeDtypeStruct((rows, 2 * keys.shape[1]), keys.dtype),
            jax.ShapeDtypeStruct((2 * members, tokens), jnp.float32),
        ],
        in_specs=[OUTSIDE] * 8,
        out_specs=[WHOLE] * 2,
        scratch_shapes=[
            pltpu.VMEM((members, tokens), jnp.float32),
            pltpu.VMEM((members, tokens), jnp.float32),
            pltpu.SMEM((members,), jnp.float32),
            pltpu.SMEM((members,), jnp.int32),
            pltpu.SemaphoreType.DMA((8,)),
        ],
        compiler_params=pltpu.CompilerParams(vmem_limit_bytes=JOIN_VMEM_BYTES),
        cost_estimate=LITTLE,
        name="join_pairs",
    )(keys, values, prompt_keys, prompt_values, behaved, current, advantages, lengths)


def per_device(
    queries,
    prompt_keys,
    prompt_values,
    resp_keys,
    resp_values,
    upstream,
    behav_logp,
    cur_logp,
    advantages,
    lengths,
):
    members, tokens, heads, head_dim = queries.shape
    ctx_size, resp_size = lax.axis_size("ctx"), lax.axis_size("resp")
    layers = ctx_size // 2
    each = prompt_keys.shape[0]
    rows = tokens * heads

    def hop(array, layers_up):
        pairs = [(c, (c + 2 * layers_up) % ctx_size) for c in range(ctx_size)]
        return lax.ppermute(array, "ctx", pairs)

    def cross(array):
        return lax.ppermute(array, "ctx", [(c, c ^ 1) for c in range(ctx_size)])

    own, policy = join(
        resp_keys.reshape(members * tokens, head_dim),
        resp_values.reshape(members * tokens, head_dim),
        prompt_keys,
        prompt_values,
        behav_logp,
        cur_logp,
        advantages,
        lengths,
    )
    z, x = [own, hop(own, 1)], [None, cross(own)]
    stat, *held_rows = prepare(
        heads,
        policy,
        queries.reshape(members, rows, head_dim),
        upstream.reshape(members, rows, head_dim),
    )

    def forward(step, stat, messages):
        return forward_step(step, layers, heads, tokens, held_rows[2:], stat, messages)

    for step in range(1, layers):
        z[step], stat = lax.optimization_barrier((z[step], stat))
        if step + 1 < layers:
            z.append(hop(z[step], 1))
            x.append(cross(z[step]))
        else:
            x.append(hop(x[1], layers - 1))
        if step == 1:
            (stat,) = forward(0, stat, z[:1])
        (stat,) = forward(step, stat, [x[step], z[step]])
    stat, prompt = forward(layers, stat, z + x[1:])
    final = stat
    moved = side = above = far = message = kept = None
    terms = []
    for step in range(layers, -1, -1):
        if message is not None:
            final, message = lax.optimization_barrier((final, message))
            above = hop(message, -1)
        if step == layers:
            messages = [x[step], prompt]
        else:
            messages = [z[0]] if step == 0 else [x[step], z[step]]
        grads, moved = backward_step(
            step, layers, heads, tokens, each, held_rows, final, messages, moved, terms
        )
        terms = []
        if step == layers:
            far, terms = hop(grads[0], 1 - layers), list(grads[1:])
            kept = grads[1]
        elif step == layers - 1:
            message = grads[1]
        elif step > 0:
            crossing = [grads[0], far] if step == 1 else []
            message, *more = combine(
                step, layers, each, grads[-1], side, above, kept, *crossing
            )
            if step == layers - 2:
                kept, *more = more
            if step == 1:
                grads = more
        if 0 < step < layers:
            side = cross(grads[0])
    above, side, last = lax.optimization_barrier((above, side, grads[-1]))
    share = kept[:each]
    for term in (above, side):
        share = share + term[-each:].astype(jnp.float32)
    key_grads, value_grads = combine(0, layers, each, last, side, above)
    if resp_size <= 4:
        shares = [share] + [
            lax.ppermute(share, "resp", [(c, c ^ i) for c in range(resp_size)])
            for i in range(1, resp_size)
        ]
    else:
        shares, stride = [share], 1
        while stride < resp_size:
            pairs = [(c, c ^ stride) for c in range(resp_size)]
            shares = [sum(shares), lax.ppermute(sum(shares), "resp", pairs)]
            stride *= 2
    return (
        moved.reshape(queries.shape),
        key_grads.reshape(resp_keys.shape),
        value_grads.reshape(resp_values.shape),
        sum(part[:, :head_dim] for part in shares),
        sum(part[:, head_dim:] for part in shares),
    )


def solution(mesh):
    placed = (
        P("resp", "ctx", None, None),
        P("ctx", None),
        P("ctx", None),
        P("resp", "ctx", None),
        P("resp", "ctx", None),
        P("resp", "ctx", None, None),
        P("resp", "ctx"),
        P("resp", "ctx"),
        P("resp"),
        P("resp"),
    )
    return jax.shard_map(
        per_device,
        mesh=mesh,
        in_specs=placed,
        out_specs=(
            P("resp", "ctx", None, None),
            P("resp", "ctx", None),
            P("resp", "ctx", None),
            P("ctx", None),
            P("ctx", None),
        ),
        check_vma=False,
    )
```

```python
import functools
import math

import jax
import jax.numpy as jnp
from jax import lax
from jax.experimental import pallas as pl
from jax.experimental.pallas import tpu as pltpu
from jax.sharding import PartitionSpec as P

RATIO_CAP = 2.0
MASKED = -1e30
SUB_ROWS = 256
TILE_ROWS = 1024
LARGEST_SCORE = 100.0
UNBOUNDED = 3e38

TOP, TOTAL, DOTTED, GUARD, WEIGHT, LENGTH = range(6)
VMEM_BYTES = 24 * 1024 * 1024
JOIN_VMEM_BYTES = 60 * 1024 * 1024

def dot(a, b):
    return jnp.dot(a, b, preferred_element_type=jnp.float32)


def kinds_of(step, layers):
    if step == 0:
        return ("z",)
    return ("x", "prompt") if step == layers else ("x", "z")


def variants(step, layers, place):
    z, odd = place // 2, place % 2 == 1
    if step == 0:
        return [(None, 0, 1)]
    if step == layers:
        return [(z >= step - 1, 0, 2), (z < step - 1, 1, 2)]
    if step == 1:
        return [
            ((z >= 1) & odd, 0, 2),
            ((z == 0) & odd, 0, 1),
            ((z >= 1) & jnp.logical_not(odd), 1, 2),
        ]
    return [(z >= step, 0, 2), (z == step - 1, 0, 1)]


def attends(step, layers, place):
    if step in (0, layers):
        return place >= 0
    return place >= 1 if step == 1 else place // 2 >= step - 1


def kept_keys(shape, first_row, heads):
    key = lax.broadcasted_iota(jnp.int32, shape, 0)
    row = lax.broadcasted_iota(jnp.int32, shape, 1) + first_row
    return key * heads <= row


def edges_of(counts):
    edges = [0]
    for count in counts:
        edges.append(edges[-1] + count)
    return edges


def largest_norm(rows):
    wide = rows.astype(jnp.float32)
    return jnp.max(jnp.sum(wide * wide, axis=1, keepdims=True))


def filled_tiles(length, tokens, heads, rows):
    per_tile = tile_of(rows) // heads
    left = length - lax.axis_index("ctx") * tokens
    return jnp.clip((left + per_tile - 1) // per_tile, 0, rows // tile_of(rows))


def load_keys(member, pairs, kinds, edges, head_dim, keys, values):
    for part, pair in enumerate(pairs):
        count = edges[part + 1] - edges[part]
        rows = pl.ds(edges[part], count)
        own = pl.ds(0, count)
        if kinds[part] != "prompt":
            own = pl.ds(pl.multiple_of(member * count, count), count)
        keys[rows, :] = pair[own, :head_dim]
        values[rows, :] = pair[own, head_dim:]


def length_of(stat, member):
    return jnp.max(stat[member, LENGTH : LENGTH + 1, 0:128]).astype(jnp.int32)


def spread_weights(ratio, heads):
    tokens = ratio.shape[1]
    shape = (tokens, tokens * heads)
    token = lax.broadcasted_iota(jnp.int32, shape, 0)
    row = lax.broadcasted_iota(jnp.int32, shape, 1)
    first = token * heads
    chosen = jnp.where((row >= first) & (row < first + heads), 1.0, 0.0)
    chosen = chosen.astype(jnp.bfloat16)
    out, rest = None, ratio
    for _ in range(3):
        term = rest.astype(jnp.bfloat16)
        rest = rest - term.astype(jnp.float32)
        few = jnp.broadcast_to(term.astype(jnp.float32), (16, tokens)).astype(jnp.bfloat16)
        part = jnp.dot(few, chosen, preferred_element_type=jnp.float32)[0:1]
        out = part if out is None else out + part
    return out


def key_sum(array):
    count = array.shape[0] // 4
    parts = [
        jnp.sum(array[i * count : (i + 1) * count], axis=0, keepdims=True) for i in range(4)
    ]
    return (parts[0] + parts[1]) + (parts[2] + parts[3])


def prepare_kernel(heads, policy, held_q, held_g, out, q, g, turned_q, turned_g, arrived):
    copies = [
        pltpu.make_async_copy(source, target, arrived.at[i])
        for i, (source, target) in enumerate([(held_q, q), (held_g, g)])
    ]
    for copy in copies:
        copy.start()
    for copy in copies:
        copy.wait()
    members, all_rows, _ = q.shape
    tile = tile_of(all_rows)
    tokens = all_rows // heads
    line = lax.broadcasted_iota(jnp.int32, policy.shape, 0)

    def per_member(member, carry):
        known = jnp.max(jnp.where(line == members + member, policy[...], 0.0))
        out[member, LENGTH : LENGTH + 1, :] = jnp.full((1, all_rows), known)

        def per_tile(index, carry):
            rows = pl.ds(pl.multiple_of(index * tile, tile), tile)
            turned_q[member, :, rows] = q[member, rows, :].T
            turned_g[member, :, rows] = g[member, rows, :].T
            guard = largest_norm(q[member, rows, :])
            out[member, GUARD : GUARD + 1, rows] = jnp.full((1, tile), guard)
            count = tile // heads
            part = pl.ds(pl.multiple_of(index * count, count), count)
            if count == tokens:
                part = pl.ds(0, count)
            chosen = jnp.where(line[:, :count] == member, policy[:, part], 0.0)
            ratio = jnp.sum(chosen, axis=0, keepdims=True)
            out[member, WEIGHT : WEIGHT + 1, rows] = spread_weights(ratio, heads)
            return carry

        filled = filled_tiles(known.astype(jnp.int32), tokens, heads, all_rows)
        lax.fori_loop(0, filled, per_tile, 0)
        return carry

    lax.fori_loop(0, members, per_member, 0)


def forward_kernel(step, layers, heads, head_dim, counts, turned_q, turned_g, earlier, *refs):
    kinds = kinds_of(step, layers)
    parts = len(kinds)
    if step == layers:
        messages, (out, prompt, keys, values) = refs[: 2 * layers], refs[2 * layers :]
        own = messages[0].shape[0] - prompt.shape[0] // (2 * layers)
        each = messages[0].shape[0] - own
        for i, message in enumerate(messages):
            prompt[i * each : (i + 1) * each, :] = message[own:, :]
        pairs = [messages[-1], prompt]
    else:
        pairs, (out, keys, values) = refs[:parts], refs[parts:]
    place = lax.axis_index("ctx")
    members, _, all_rows = turned_q.shape
    tile = tile_of(all_rows)
    tokens = all_rows // heads
    scale = head_dim**-0.5 * math.log2(math.e)
    edges = edges_of(counts)
    attended = attends(step, layers, place)

    def shared(member, low, high, first, start):
        rows = pl.ds(row_start(first, start), SUB_ROWS)
        scores = dot(keys[low:high, :], turned_q[member, :, rows]) * scale
        if step == 0:
            kept = kept_keys(scores.shape, first + start, heads)
            scores = jnp.where(kept, scores, MASKED)
        return rows, scores, dot(values[low:high, :], turned_g[member, :, rows])

    def put(member, first, span, lines):
        rows = pl.ds(first, span)
        for line, pieces in lines.items():
            out[member, line : line + 1, rows] = jnp.concatenate(pieces, 1)

    def bounded(member, low, high, first, span):
        totals, dots = [], []
        for start in range(0, span, SUB_ROWS):
            rows, scores, grad_probs = shared(member, low, high, first, start)
            weight = jnp.exp2(scores)
            total, dotted = key_sum(weight), key_sum(weight * grad_probs)
            if step > 0:
                total = total + earlier[member, TOTAL : TOTAL + 1, rows]
                dotted = dotted + earlier[member, DOTTED : DOTTED + 1, rows]
            totals.append(total)
            dots.append(dotted)
        tops = [jnp.zeros_like(t) for t in totals]
        put(member, first, span, {TOP: tops, TOTAL: totals, DOTTED: dots})

    def general(member, low, high, first, span):
        tops, totals, dots = [], [], []
        for start in range(0, span, SUB_ROWS):
            rows, scores, grad_probs = shared(member, low, high, first, start)
            top = jnp.max(scores, axis=0, keepdims=True)
            if step > 0:
                top = jnp.maximum(top, earlier[member, TOP : TOP + 1, rows])
            weight = jnp.exp2(scores - top)
            total, dotted = key_sum(weight), key_sum(weight * grad_probs)
            if step > 0:
                decay = jnp.exp2(earlier[member, TOP : TOP + 1, rows] - top)
                total = total + decay * earlier[member, TOTAL : TOTAL + 1, rows]
                dotted = dotted + decay * earlier[member, DOTTED : DOTTED + 1, rows]
            tops.append(top)
            totals.append(total)
            dots.append(dotted)
        guards = [jnp.full_like(t, UNBOUNDED) for t in totals]
        put(member, first, span, {TOP: tops, TOTAL: totals, DOTTED: dots, GUARD: guards})

    def per_member(member, carry):
        filled = filled_tiles(length_of(earlier, member), tokens, heads, all_rows)

        @pl.when((filled > 0) & attended)
        def _():
            load_keys(member, pairs, kinds, edges, head_dim, keys, values)
            limit = (LARGEST_SCORE / scale) ** 2 / largest_norm(keys[...])
            guards = earlier[member, GUARD : GUARD + 1, :]
            column = lax.broadcasted_iota(jnp.int32, guards.shape, 1)
            fast = jnp.max(jnp.where(column < filled * tile, guards, 0.0)) <= limit
            for condition, begin, past in variants(step, layers, place):
                low, high = edges[begin], edges[past]
                here = True if condition is None else condition

                @pl.when(fast & here)
                def _():
                    over_tiles(filled, all_rows, functools.partial(bounded, member, low, high))

                @pl.when(jnp.logical_not(fast) & here)
                def _():
                    over_tiles(filled, all_rows, functools.partial(general, member, low, high), 0)

        return carry

    lax.fori_loop(0, members, per_member, 0)


def row_start(first, start):
    if isinstance(first, int):
        return first + start
    return pl.multiple_of(first + start, SUB_ROWS)


def over_tiles(filled, all_rows, body, whole=1):
    tile = tile_of(all_rows)
    tiles = all_rows // tile

    def per_tile(index, carry):
        body(pl.multiple_of(index * tile, tile), tile)
        return carry

    if tiles == 1 or not whole:
        lax.fori_loop(0, filled, per_tile, 0)
        return

    @pl.when(filled == tiles)
    def _():
        body(0, all_rows)

    @pl.when(filled < tiles)
    def _():
        lax.fori_loop(0, filled, per_tile, 0)


def backward_kernel(step, layers, heads, head_dim, counts, *refs):
    q, g, turned_q, turned_g, final = refs[:5]
    refs = refs[5:]
    kinds = kinds_of(step, layers)
    count = len(kinds)
    pairs, refs = refs[:count], refs[count:]
    earlier = None
    if step < layers:
        earlier, refs = refs[0], refs[1:]
    if step == layers - 1:
        stay, leave = refs[:2]
        refs = refs[2:]
    made = 3 if step == layers else count
    grads, query_out, refs = refs[:made], refs[made], refs[made + 1 :]
    keys, values, turned, probs_held, scores_held, sums = refs
    place = lax.axis_index("ctx")
    members, all_rows = q.shape[:2]
    tile = tile_of(all_rows)
    tokens = all_rows // heads
    plain = head_dim**-0.5
    scale = plain * math.log2(math.e)
    edges = edges_of(counts)
    attended = attends(step, layers, place)

    def body(member, low, high, first, span):
        whole = pl.ds(first, span)
        held_rows = slice(0, span)
        total = final[member, TOTAL : TOTAL + 1, whole]
        level = final[member, TOP : TOP + 1, whole] + jnp.log2(total)
        delta = final[member, DOTTED : DOTTED + 1, whole] / total
        token_weight = final[member, WEIGHT : WEIGHT + 1, whole]
        for start in range(0, span, SUB_ROWS):
            rows = pl.ds(row_start(first, start), SUB_ROWS)
            held = slice(start, start + SUB_ROWS)
            scores = dot(keys[low:high, :], turned_q[member, :, rows]) * scale
            scores = scores - level[:, held]
            if step == 0:
                kept = kept_keys(scores.shape, first + start, heads)
                scores = jnp.where(kept, scores, MASKED)
            probs = jnp.exp2(scores) * token_weight[:, held]
            grad_probs = dot(values[low:high, :], turned_g[member, :, rows])
            grad_scores = probs * (grad_probs - delta[:, held])
            probs_held[low:high, held] = probs.astype(jnp.bfloat16)
            scores_held[low:high, held] = grad_scores.astype(jnp.bfloat16)
        sums[low:high, head_dim:] += dot(probs_held[low:high, held_rows], g[member, whole, :])
        sums[low:high, :head_dim] += dot(scores_held[low:high, held_rows], q[member, whole, :])
        moved = dot(turned[:, low:high], scores_held[low:high, held_rows])
        if earlier is not None:
            moved = moved + earlier[member, :, whole]
        if step == 0:
            query_out[member, whole, :] = (moved * plain).T.astype(jnp.bfloat16)
        else:
            query_out[member, :, whole] = moved

    def per_member(member, carry):
        filled = filled_tiles(length_of(final, member), tokens, heads, all_rows)
        filled = jnp.where(attended, filled, 0)
        for part in range(count):
            rows = pl.ds(edges[part], edges[part + 1] - edges[part])

            @pl.when((member == 0) | (kinds[part] != "prompt"))
            def _():
                sums[rows, :] = jnp.zeros_like(sums[rows, :])

        @pl.when(filled > 0)
        def _():
            load_keys(member, pairs, kinds, edges, head_dim, keys, values)
            turned[...] = keys[...].T

            for condition, begin, past in variants(step, layers, place):
                low, high = edges[begin], edges[past]

                @pl.when(True if condition is None else condition)
                def _():
                    over_tiles(filled, all_rows, functools.partial(body, member, low, high), 0)

        if step == 0 or earlier is None:

            def clear(index, carry):
                rows = pl.ds(pl.multiple_of(index * tile, tile), tile)
                if step == 0:
                    query_out[member, rows, :] = jnp.zeros((tile, head_dim), jnp.bfloat16)
                else:
                    query_out[member, :, rows] = jnp.zeros((head_dim, tile), jnp.float32)
                return carry

            lax.fori_loop(filled, all_rows // tile, clear, 0)
        for part in range(count):
            if kinds[part] == "prompt":
                continue
            rows = pl.ds(edges[part], counts[part])
            own = pl.ds(pl.multiple_of(member * counts[part], counts[part]), counts[part])
            key_part, value_part = sums[rows, :head_dim] * plain, sums[rows, head_dim:]
            grads[part][own, :head_dim] = key_part.astype(jnp.bfloat16)
            grads[part][own, head_dim:] = value_part.astype(jnp.bfloat16)
        return carry

    lax.fori_loop(0, members, per_member, 0)
    tail = members * tokens
    if step == layers:
        far, stay, leave = grads
        middle = edges[1] + stay.shape[0]
        last = middle + leave.shape[0]
        for target, begin, rows in (
            (stay, 0, slice(edges[1], middle)),
            (leave, 0, slice(middle, last)),
            (far, tail, slice(last, edges[2])),
        ):
            end = target.shape[0]
            target[begin:end, :head_dim] = (sums[rows, :head_dim] * plain).astype(target.dtype)
            target[begin:end, head_dim:] = sums[rows, head_dim:].astype(target.dtype)
    elif step == layers - 1:
        grads[0][tail:, :] = leave[...]
        grads[1][tail:, :] = stay[leave.shape[0] :, :].astype(jnp.bfloat16)


def combine_kernel(step, layers, each, own, side, above, *refs):
    def wide(ref, rows):
        return ref[rows, :].astype(jnp.float32)

    count = own.shape[0]
    rows = slice(0, count)
    total = wide(own, rows) + wide(side, rows) + wide(above, rows)
    if step == 0:
        key_out, value_out = refs
        total = total.astype(jnp.bfloat16)
        head_dim = key_out.shape[1]
        key_out[...] = total[:, :head_dim]
        value_out[...] = total[:, head_dim:]
        return
    kept, *refs = refs
    if step == 1:
        crossing, far, *refs = refs
    out, *refs = refs
    mine = slice(step * each, (step + 1) * each)
    prompt = kept[mine, :] + wide(above, slice(count, None))
    if step == layers - 2:
        prompt = prompt + wide(side, slice(count + mine.start, count + mine.stop))
        still_kept, *refs = refs
        still_kept[...] = kept[: step * each, :] + wide(side, slice(count, count + step * each))
    out[rows, :] = total.astype(jnp.bfloat16)
    out[count:, :] = prompt.astype(jnp.bfloat16)
    if step == 1:
        (leaving,) = refs
        leaving[rows, :] = (wide(crossing, rows) + wide(far, rows)).astype(jnp.bfloat16)
        leaving[count:, :] = far[count:, :]


def tile_of(rows):
    return min(TILE_ROWS, rows)


WHOLE = pl.BlockSpec(memory_space=pltpu.VMEM)
PARAMS = pltpu.CompilerParams(vmem_limit_bytes=VMEM_BYTES)
LITTLE = pl.CostEstimate(flops=1000, bytes_accessed=1000, transcendentals=0)


OUTSIDE = pl.BlockSpec(memory_space=pltpu.HBM)


def prepare(heads, policy, q, g):
    members, rows, head_dim = q.shape
    turned = jax.ShapeDtypeStruct((members, head_dim, rows), q.dtype)
    return pl.pallas_call(
        functools.partial(prepare_kernel, heads),
        in_specs=[WHOLE] + [OUTSIDE] * 2,
        out_specs=[WHOLE] * 5,
        out_shape=[jax.ShapeDtypeStruct((members, 8, rows), jnp.float32)]
        + [jax.ShapeDtypeStruct(q.shape, q.dtype)] * 2
        + [turned] * 2,
        scratch_shapes=[pltpu.SemaphoreType.DMA((2,))],
        compiler_params=PARAMS,
        cost_estimate=LITTLE,
        name="prepare_rows",
    )(policy, q, g)


def forward_step(step, layers, heads, tokens, turned, earlier, messages):
    members, head_dim, rows = turned[0].shape
    each = messages[0].shape[0] - members * tokens
    counts = [tokens] * len(kinds_of(step, layers))
    out_shape = [jax.ShapeDtypeStruct((members, 8, rows), jnp.float32)]
    if step == layers:
        counts[1] = 2 * layers * each
        out_shape.append(jax.ShapeDtypeStruct((counts[1], 2 * head_dim), jnp.bfloat16))
    return pl.pallas_call(
        functools.partial(forward_kernel, step, layers, heads, head_dim, counts),
        in_specs=[WHOLE] * (3 + len(messages)),
        out_specs=[WHOLE] * len(out_shape),
        out_shape=out_shape,
        scratch_shapes=[pltpu.VMEM((sum(counts), head_dim), jnp.bfloat16)] * 2,
        compiler_params=PARAMS,
        cost_estimate=LITTLE,
        input_output_aliases={2: 0},
        name=f"attend_step{step}",
    )(*turned, earlier, *messages)


def backward_step(
    step, layers, heads, tokens, each, held_rows, final, messages, earlier, prompt_terms
):
    q = held_rows[0]
    members, rows, head_dim = q.shape
    counts = [tokens] * len(kinds_of(step, layers))

    def block(more, dtype=jnp.bfloat16, base=members * tokens):
        return jax.ShapeDtypeStruct((base + more, 2 * head_dim), dtype)

    if step == layers:
        counts[1] = 2 * layers * each
        grad_shapes = [
            block(each),
            block(layers * each, jnp.float32, 0),
            block((layers - 1) * each, jnp.bfloat16, 0),
        ]
    elif step == layers - 1:
        grad_shapes = [block((layers - 1) * each), block(each)]
    else:
        grad_shapes = [block(0)] * len(counts)
    columns = sum(counts)
    if step == 0:
        query_shape = jax.ShapeDtypeStruct(q.shape, jnp.bfloat16)
    else:
        query_shape = jax.ShapeDtypeStruct((members, head_dim, rows), jnp.float32)
    extra = [] if earlier is None else [earlier]
    aliases = {5 + len(messages): len(grad_shapes)} if extra and step > 0 else {}
    extra += prompt_terms
    outs = pl.pallas_call(
        functools.partial(backward_kernel, step, layers, heads, head_dim, counts),
        in_specs=[WHOLE] * (5 + len(messages) + len(extra)),
        out_specs=[WHOLE] * (len(grad_shapes) + 1),
        out_shape=grad_shapes + [query_shape],
        scratch_shapes=[pltpu.VMEM((columns, head_dim), jnp.bfloat16)] * 2
        + [pltpu.VMEM((head_dim, columns), jnp.bfloat16)]
        + [pltpu.VMEM((columns, tile_of(rows)), jnp.bfloat16)] * 2
        + [pltpu.VMEM((columns, 2 * head_dim), jnp.float32)],
        compiler_params=PARAMS,
        cost_estimate=LITTLE,
        input_output_aliases=aliases,
        name=f"attend_grad_step{step}",
    )(*held_rows, final, *messages, *extra)
    return outs[:-1], outs[-1]


def combine(step, layers, each, *terms):
    count, width = terms[0].shape
    message = jax.ShapeDtypeStruct((count + each, width), jnp.bfloat16)
    if step == 0:
        shapes = [jax.ShapeDtypeStruct((count, width // 2), jnp.bfloat16)] * 2
    else:
        shapes = [message]
        if step == layers - 2:
            shapes.append(jax.ShapeDtypeStruct((step * each, width), jnp.float32))
        if step == 1:
            shapes.append(message)
    return pl.pallas_call(
        functools.partial(combine_kernel, step, layers, each),
        in_specs=[WHOLE] * len(terms),
        out_specs=[WHOLE] * len(shapes),
        out_shape=shapes,
        compiler_params=PARAMS,
        cost_estimate=LITTLE,
        name=f"add_terms{step}",
    )(*terms)


def join_kernel(
    keys, values, prompt_keys, prompt_values, behaved, current, advantages, lengths, *refs
):
    out, policy, held_behaved, held_current, held_advantages, held_lengths, arrived = refs
    rows, head_dim = keys.shape
    members, tokens = behaved.shape

    def part(first, count, column):
        return out.at[pl.ds(first, count), pl.ds(column, head_dim)]

    each = prompt_keys.shape[0]
    targets = [
        (keys, part(0, rows, 0)),
        (values, part(0, rows, head_dim)),
        (prompt_keys, part(rows, each, 0)),
        (prompt_values, part(rows, each, head_dim)),
        (behaved, held_behaved),
        (current, held_current),
        (advantages, held_advantages),
        (lengths, held_lengths),
    ]
    copies = [
        pltpu.make_async_copy(source, target, arrived.at[i])
        for i, (source, target) in enumerate(targets)
    ]
    for copy in copies:
        copy.start()
    for copy in copies:
        copy.wait()
    full_len = tokens * lax.axis_size("ctx")
    position = lax.axis_index("ctx") * tokens + lax.broadcasted_iota(jnp.int32, (1, tokens), 1)
    ratio = jnp.minimum(jnp.exp(held_current[...] - held_behaved[...]), RATIO_CAP)
    for member in range(members):
        length = held_lengths[member]
        spread = full_len / jnp.full((1, 1), length).astype(jnp.float32)
        valid = jnp.where(position < length, ratio[member : member + 1], 0.0)
        policy[member : member + 1, :] = -held_advantages[member] * valid * spread
        wide = jnp.full((1, tokens), length).astype(jnp.float32)
        policy[members + member : members + member + 1, :] = wide


def join(keys, values, prompt_keys, prompt_values, behaved, current, advantages, lengths):
    rows = keys.shape[0] + prompt_keys.shape[0]
    members, tokens = behaved.shape
    return pl.pallas_call(
        join_kernel,
        out_shape=[
            jax.ShapeDtypeStruct((rows, 2 * keys.shape[1]), keys.dtype),
            jax.ShapeDtypeStruct((2 * members, tokens), jnp.float32),
        ],
        in_specs=[OUTSIDE] * 8,
        out_specs=[WHOLE] * 2,
        scratch_shapes=[
            pltpu.VMEM((members, tokens), jnp.float32),
            pltpu.VMEM((members, tokens), jnp.float32),
            pltpu.SMEM((members,), jnp.float32),
            pltpu.SMEM((members,), jnp.int32),
            pltpu.SemaphoreType.DMA((8,)),
        ],
        compiler_params=pltpu.CompilerParams(vmem_limit_bytes=JOIN_VMEM_BYTES),
        cost_estimate=LITTLE,
        name="join_pairs",
    )(keys, values, prompt_keys, prompt_values, behaved, current, advantages, lengths)


def per_device(
    queries,
    prompt_keys,
    prompt_values,
    resp_keys,
    resp_values,
    upstream,
    behav_logp,
    cur_logp,
    advantages,
    lengths,
):
    members, tokens, heads, head_dim = queries.shape
    ctx_size, resp_size = lax.axis_size("ctx"), lax.axis_size("resp")
    layers = ctx_size // 2
    each = prompt_keys.shape[0]
    rows = tokens * heads

    def hop(array, layers_up):
        pairs = [(c, (c + 2 * layers_up) % ctx_size) for c in range(ctx_size)]
        return lax.ppermute(array, "ctx", pairs)

    def cross(array):
        return lax.ppermute(array, "ctx", [(c, c ^ 1) for c in range(ctx_size)])

    own, policy = join(
        resp_keys.reshape(members * tokens, head_dim),
        resp_values.reshape(members * tokens, head_dim),
        prompt_keys,
        prompt_values,
        behav_logp,
        cur_logp,
        advantages,
        lengths,
    )
    z, x = [own, hop(own, 1)], [None, cross(own)]
    stat, *held_rows = prepare(
        heads,
        policy,
        queries.reshape(members, rows, head_dim),
        upstream.reshape(members, rows, head_dim),
    )

    def forward(step, stat, messages):
        return forward_step(step, layers, heads, tokens, held_rows[2:], stat, messages)

    for step in range(1, layers):
        z[step], stat = lax.optimization_barrier((z[step], stat))
        if step + 1 < layers:
            z.append(hop(z[step], 1))
            x.append(cross(z[step]))
        else:
            x.append(hop(x[1], layers - 1))
        if step == 1:
            (stat,) = forward(0, stat, z[:1])
        (stat,) = forward(step, stat, [x[step], z[step]])
    stat, prompt = forward(layers, stat, z + x[1:])
    final = stat
    moved = side = above = far = message = kept = None
    terms = []
    for step in range(layers, -1, -1):
        if message is not None:
            final, message = lax.optimization_barrier((final, message))
            above = hop(message, -1)
            if 0 < step < layers - 2:
                final, side = lax.optimization_barrier((final, side))
        if step == layers:
            messages = [x[step], prompt]
        else:
            messages = [z[0]] if step == 0 else [x[step], z[step]]
        grads, moved = backward_step(
            step, layers, heads, tokens, each, held_rows, final, messages, moved, terms
        )
        terms = []
        if step == layers:
            far, terms = hop(grads[0], 1 - layers), list(grads[1:])
            kept = grads[1]
        elif step == layers - 1:
            message = grads[1]
        elif step > 0:
            crossing = [grads[0], far] if step == 1 else []
            message, *more = combine(
                step, layers, each, grads[-1], side, above, kept, *crossing
            )
            if step == layers - 2:
                kept, *more = more
            if step == 1:
                grads = more
        if 0 < step < layers:
            side = cross(grads[0])
    above, side, last = lax.optimization_barrier((above, side, grads[-1]))
    share = kept[:each]
    for term in (above, side):
        share = share + term[-each:].astype(jnp.float32)
    key_grads, value_grads = combine(0, layers, each, last, side, above)
    if resp_size <= 4:
        shares = [share] + [
            lax.ppermute(share, "resp", [(c, c ^ i) for c in range(resp_size)])
            for i in range(1, resp_size)
        ]
    else:
        shares, stride = [share], 1
        while stride < resp_size:
            pairs = [(c, c ^ stride) for c in range(resp_size)]
            shares = [sum(shares), lax.ppermute(sum(shares), "resp", pairs)]
            stride *= 2
    return (
        moved.reshape(queries.shape),
        key_grads.reshape(resp_keys.shape),
        value_grads.reshape(resp_values.shape),
        sum(part[:, :head_dim] for part in shares),
        sum(part[:, head_dim:] for part in shares),
    )


def solution(mesh):
    placed = (
        P("resp", "ctx", None, None),
        P("ctx", None),
        P("ctx", None),
        P("resp", "ctx", None),
        P("resp", "ctx", None),
        P("resp", "ctx", None, None),
        P("resp", "ctx"),
        P("resp", "ctx"),
        P("resp"),
        P("resp"),
    )
    return jax.shard_map(
        per_device,
        mesh=mesh,
        in_specs=placed,
        out_specs=(
            P("resp", "ctx", None, None),
            P("resp", "ctx", None),
            P("resp", "ctx", None),
            P("ctx", None),
            P("ctx", None),
        ),
        check_vma=False,
    )
```
